256 devices in a mesh: lon: 128 (over y_hi, x, z, core), lat: 2 (over y_lo).
Axes of the slice: x: 4, y: 4 (y_hi: 2, y_lo: 2; y = y_hi * 2 + y_lo), z: 8, core: 2. Of those that a mesh axis runs over, the one named last changes fastest.
Arguments:
- inputs: bfloat16 [1, 2, 12, 1536, 512], P(None, None, 'lat', 'lon'), may hold values from -24 to 24
- grad_out: bfloat16 [1, 2, 12, 1536, 512], P(None, None, 'lat', 'lon'), may hold values from -6 to 6
- gains: float32 [2, 512], replicated, may hold values from 0.5 to 1.5
- qkv_weight: bfloat16 [2, 512, 1536], replicated, may hold values from -0.5 to 0.5
- proj_weight: bfloat16 [2, 512, 512], replicated, may hold values from -0.25 to 0.25
- bias_table: float32 [2, 2, 16, 759], replicated, may hold values from -3 to 303
- rel_ids: int32 [144, 144], replicated, may hold values from 0 to 758
- groups: int32 [2, 12, 1536], P(None, 'lat', 'lon'), may hold values from 0 to 3
Outputs:
- outputs: bfloat16 [1, 2, 12, 1536, 512], P(None, None, 'lat', 'lon')
- grad_inputs: bfloat16 [1, 2, 12, 1536, 512], P(None, None, 'lat', 'lon')
- grad_gains: float32 [2, 512], replicated
- grad_qkv: float32 [2, 512, 1536], P(None, 'lon')
- grad_proj: float32 [2, 512, 512], P(None, 'lon')
- grad_bias: float32 [2, 2, 16, 759], replicated
The draws below stay inside these ranges and needn't reach their ends.
All inputs are finite; a program needn't handle non-finite values.
Results may differ from the reference program's by a relative error of at most 0.035.
The reference program's roundings to bfloat16 on the way count: a program that leaves them out, or rounds other values in their place, can miss the bound.
Values may be sent and summed in bfloat16 or wider, within the bound.
No kernel may reach another device: no remote copies, remote signals or barrier semaphores. Data moves between devices by JAX's collectives and lax.ppermute only.
A program may use at most 128 MiB of HBM per device.

```python
import jax
import jax.numpy as jnp
from jax import lax

D = 512
HEADS = 16
LEVELS = 2
WT = 6
WN = 12
WTOK = 144
NREL = 759
LAT = 12
LATWIN = 2
LON_DEV = 12
LON = 1536
BATCH = 1
TOKENS = 36864


def draw_bias_table(key, part):
    key = jax.random.fold_in(key, 11)
    second = jax.random.fold_in(key, 1)
    full_shape = (2, LATWIN, HEADS, NREL)
    return jax.random.truncated_normal(second, -3.0, 3.0, full_shape, jnp.float32)


def place_ends(entries, key, least, top_value):
    extent = entries.shape
    index_at = [jax.random.randint(jax.random.fold_in(key, axis), (), 0, extent[axis]) for axis in range(len(extent))]
    entries = entries.at[tuple(index_at)].set(least)
    longest = extent.index(max(extent))
    index_at[longest] = (index_at[longest] + 1) % extent[longest]
    return entries.at[tuple(index_at)].set(top_value)


def strengthened(drawn, key, source, target, parts, factor):
    owner, partner = [(jnp.arange(drawn.shape[position]) // (drawn.shape[position] // parts)).reshape([-1 if axis == position else 1 for axis in range(drawn.ndim)]) for position in (source, target)]
    chosen = jax.random.permutation(key, parts)[partner]
    strong = (owner == chosen) | (owner == (partner + parts // 2) % parts)
    return jnp.where(strong, factor * drawn, drawn)


def block_levels(stream_key, shape, pieces, least, largest):
    loudness, own = 1.0, jax.random.fold_in(stream_key, 6)
    for axis_at, shards_of in pieces:
        steps = jnp.exp(jax.random.uniform(jax.random.fold_in(own, axis_at), (shards_of,), jnp.float32, least / len(pieces), largest / len(pieces)))
        loudness = loudness * jnp.repeat(steps, shape[axis_at] // shards_of).reshape([-1 if axis == axis_at else 1 for axis in range(len(shape))])
    return loudness


def gaussian(rng, extent, spread, bound, cuts=(), held_as=jnp.bfloat16):
    values = spread * jax.random.normal(rng, extent, jnp.float32)
    if cuts:
        values = values * block_levels(rng, extent, cuts, -0.22, 0.18)
    return jnp.clip(values, -bound, bound).astype(held_as)


def noise_with(stream_key, shape, scale, limit, cuts, heavy, dtype=jnp.bfloat16):
    values = scale * jax.random.normal(stream_key, shape, jnp.float32)
    if cuts:
        values = values * block_levels(stream_key, shape, cuts, -0.22, 0.18)
    return jnp.clip(strengthened(values, jax.random.fold_in(stream_key, 3), *heavy), -limit, limit).astype(dtype)


def setup_inputs(seed: int = 0) -> dict:
    key_of = jax.random.split(jax.random.key(seed), 9)
    return {
        "inputs": noise_with(key_of[0], (BATCH, LEVELS, LAT, LON, D), 1.0, 24.0, ((2, 2), (3, 128)), (3, 4, 128, 5.5)),
        "grad_out": gaussian(key_of[1], (BATCH, LEVELS, LAT, LON, D), 1.0, 6.0, ((2, 2), (3, 128))),
        "gains": jnp.clip(1.0 + 0.1 * jax.random.normal(key_of[2], (2, D), jnp.float32), 0.5, 1.5),
        "qkv_weight": gaussian(key_of[3], (2, D, 3 * D), (D // 4) ** -0.5, 0.5),
        "proj_weight": gaussian(key_of[4], (2, D, D), D ** -0.5, 0.25),
        "bias_table": draw_bias_table(jax.random.fold_in(key_of[8], 71), 0),
        "rel_ids": place_ends(jax.random.randint(key_of[6], (WTOK, WTOK), 0, NREL), jax.random.fold_in(key_of[6], 1), 0, NREL - 1).astype(jnp.int32),
        "groups": place_ends(jax.random.randint(key_of[7], (LEVELS, LAT, LON), 0, 4), jax.random.fold_in(key_of[7], 1), 0, 3).astype(jnp.int32),
    }


EPSILON = 1e-05
NEGATIVE = -1e+30

def normalize(fields):
    center = fields - lax.optimization_barrier(jnp.mean(fields, axis=-1, keepdims=True))
    inv_std = lax.rsqrt(lax.optimization_barrier(jnp.mean(center * center, axis=-1, keepdims=True)) + EPSILON)
    return (center * inv_std, inv_std)

def attend_forward(frame, gain_row, qkv_mat, proj_mat, bias_heads, allowed, heads):
    count_win, tokens_win, features = frame.shape
    head_dim = features // heads
    factor = head_dim ** (-0.5)
    frame_wide = frame.astype(jnp.float32)
    normed, inv_std = normalize(frame_wide)
    hidden = (normed * gain_row).astype(jnp.bfloat16)
    packed = jnp.dot(hidden.reshape(count_win * tokens_win, features), qkv_mat, preferred_element_type=jnp.float32)
    packed = packed.astype(jnp.bfloat16).reshape(count_win, tokens_win, 3, heads, head_dim)
    queries = packed[:, :, 0]
    keys_part = packed[:, :, 1]
    values_part = packed[:, :, 2]
    scores = jnp.einsum('wqhc,wkhc->whqk', queries.astype(jnp.float32), keys_part.astype(jnp.float32)) * factor + bias_heads[None]
    scores = jnp.where(allowed[:, None], scores, NEGATIVE)
    row_top = lax.optimization_barrier(jnp.max(scores, axis=-1, keepdims=True))
    exponent = jnp.exp(scores - row_top)
    probs_full = exponent / lax.optimization_barrier(jnp.sum(exponent, axis=-1, keepdims=True))
    probs_low = probs_full.astype(jnp.bfloat16)
    mixed_heads = jnp.einsum('whqk,wkhc->wqhc', probs_low.astype(jnp.float32), values_part.astype(jnp.float32))
    mixed_heads = mixed_heads.astype(jnp.bfloat16).reshape(count_win * tokens_win, features)
    branch = jnp.dot(mixed_heads, proj_mat, preferred_element_type=jnp.float32)
    result = (frame_wide + branch.reshape(count_win, tokens_win, features)).astype(jnp.bfloat16)
    return (result, (normed, inv_std, hidden, queries, keys_part, values_part, probs_full, probs_low, mixed_heads))

def attend_backward(cotangent, saved, gain_row, qkv_mat, proj_mat, heads):
    count_win, tokens_win, features = cotangent.shape
    head_dim = features // heads
    factor = head_dim ** (-0.5)
    normed, inv_std, hidden, queries, keys_part, values_part, probs_full, probs_low, mixed_heads = saved
    flat_grad = cotangent.reshape(count_win * tokens_win, features)
    grad_proj = jnp.dot(mixed_heads.T, flat_grad, preferred_element_type=jnp.float32)
    grad_mixed = jnp.dot(flat_grad, proj_mat.T, preferred_element_type=jnp.float32)
    grad_mixed = grad_mixed.astype(jnp.bfloat16).reshape(count_win, tokens_win, heads, head_dim).astype(jnp.float32)
    grad_probs = jnp.einsum('wqhc,wkhc->whqk', grad_mixed, values_part.astype(jnp.float32))
    grad_values = jnp.einsum('whqk,wqhc->wkhc', probs_low.astype(jnp.float32), grad_mixed)
    grad_scores = probs_full * (grad_probs - lax.optimization_barrier(jnp.sum(grad_probs * probs_full, axis=-1, keepdims=True)))
    grad_bias = lax.optimization_barrier(jnp.sum(grad_scores, axis=0))
    scores_low = grad_scores.astype(jnp.bfloat16).astype(jnp.float32)
    grad_queries = jnp.einsum('whqk,wkhc->wqhc', scores_low, keys_part.astype(jnp.float32)) * factor
    grad_keys = jnp.einsum('whqk,wqhc->wkhc', scores_low, queries.astype(jnp.float32)) * factor
    grad_packed = jnp.stack([grad_queries, grad_keys, grad_values], axis=2).astype(jnp.bfloat16)
    grad_packed = grad_packed.reshape(count_win * tokens_win, 3 * features)
    flat_hidden = hidden.reshape(count_win * tokens_win, features)
    grad_qkv = jnp.dot(flat_hidden.T, grad_packed, preferred_element_type=jnp.float32)
    grad_hidden = jnp.dot(grad_packed, qkv_mat.T, preferred_element_type=jnp.float32).reshape(count_win, tokens_win, features)
    grad_gain = lax.optimization_barrier(jnp.sum(grad_hidden * normed, axis=(0, 1)))
    grad_normed = grad_hidden * gain_row
    grad_frame = inv_std * (grad_normed - lax.optimization_barrier(jnp.mean(grad_normed, axis=-1, keepdims=True)) - normed * lax.optimization_barrier(jnp.mean(grad_normed * normed, axis=-1, keepdims=True)))
    grad_frame = grad_frame + cotangent.astype(jnp.float32)
    return (grad_frame.astype(jnp.bfloat16), grad_qkv, grad_proj, grad_gain, grad_bias)

def to_windows(grid):
    batch_size, level_count, lat_rows, lon_cols, features = grid.shape
    view = grid.reshape(batch_size, level_count, lat_rows // WT, WT, lon_cols // WN, WN, features)
    view = view.transpose(2, 0, 4, 1, 3, 5, 6)
    return view.reshape(lat_rows // WT, batch_size * (lon_cols // WN), level_count * WT * WN, features)

def from_windows(stacked, full_shape):
    batch_size, level_count, lat_rows, lon_cols, features = full_shape
    view = stacked.reshape(lat_rows // WT, batch_size, lon_cols // WN, level_count, WT, WN, features)
    return view.transpose(1, 3, 0, 4, 2, 5, 6).reshape(full_shape)

def block_forward(frame, index, gains, qkv_weight, proj_weight, bias_table, rel_ids, keys_grid):
    windows = to_windows(frame)
    key_win = to_windows(keys_grid[..., None])[..., 0]
    heads = bias_table.shape[2]
    group = 2 * (LON_DEV // WN)
    tokens_win = windows.shape[2]
    features = windows.shape[3]
    results = []
    for latwin_id in range(windows.shape[0]):
        bias_heads = bias_table[index, latwin_id][:, rel_ids]
        items = windows[latwin_id].reshape(-1, group, tokens_win, features)
        key_items = key_win[latwin_id].reshape(-1, group, tokens_win)

        def apply_one(couple, bias_heads=bias_heads):
            allowed = couple[1][:, :, None] == couple[1][:, None, :]
            return attend_forward(couple[0], gains[index], qkv_weight[index], proj_weight[index], bias_heads, allowed, heads)[0]
        outcome = lax.map(apply_one, (items, key_items))
        results.append(outcome.reshape(windows.shape[1], tokens_win, features))
    return from_windows(jnp.stack(results), frame.shape)

def block_backward(frame, cotangent, index, gains, qkv_weight, proj_weight, bias_table, rel_ids, keys_grid):
    windows = to_windows(frame)
    grad_win = to_windows(cotangent)
    key_win = to_windows(keys_grid[..., None])[..., 0]
    heads = bias_table.shape[2]
    group = 2 * (LON_DEV // WN)
    tokens_win = windows.shape[2]
    features = windows.shape[3]
    total_qkv = jnp.zeros((features, 3 * features), jnp.float32)
    total_proj = jnp.zeros((features, features), jnp.float32)
    total_gain = jnp.zeros((features,), jnp.float32)
    grads = []
    tables = []
    for latwin_id in range(windows.shape[0]):
        bias_heads = bias_table[index, latwin_id][:, rel_ids]
        items = windows[latwin_id].reshape(-1, group, tokens_win, features)
        grad_items = grad_win[latwin_id].reshape(-1, group, tokens_win, features)
        key_items = key_win[latwin_id].reshape(-1, group, tokens_win)

        def step(carry, triple, bias_heads=bias_heads):
            frame_part, grad_part, key_part = triple
            allowed = key_part[:, :, None] == key_part[:, None, :]
            saved = attend_forward(frame_part, gains[index], qkv_weight[index], proj_weight[index], bias_heads, allowed, heads)[1]
            grad_frame, grad_qkv, grad_proj, grad_gain, grad_bias = attend_backward(grad_part, saved, gains[index], qkv_weight[index], proj_weight[index], heads)
            return ((carry[0] + grad_qkv, carry[1] + grad_proj, carry[2] + grad_gain, carry[3] + grad_bias), grad_frame)
        start = (total_qkv, total_proj, total_gain, jnp.zeros((heads, tokens_win, tokens_win), jnp.float32))
        carry, grad_frames = lax.scan(step, start, (items, grad_items, key_items))
        total_qkv, total_proj, total_gain = (carry[0], carry[1], carry[2])
        summed = jax.ops.segment_sum(carry[3].reshape(heads, -1).T, rel_ids.reshape(-1), num_segments=NREL)
        tables.append(summed.T)
        grads.append(grad_frames.reshape(windows.shape[1], tokens_win, features))
    return (from_windows(jnp.stack(grads), frame.shape), total_qkv, total_proj, total_gain, jnp.stack(tables))

def shift_keys(groups, batch_size):
    level_count, lat_rows, lon_cols = groups.shape
    rolled = jnp.roll(groups, (-(level_count // 2), -(WT // 2), -(WN // 2)), axis=(0, 1, 2))
    row_seg = (jnp.arange(lat_rows) >= lat_rows - WT // 2).astype(jnp.int32)
    level_seg = (jnp.arange(level_count) >= level_count - level_count // 2).astype(jnp.int32)
    keys_grid = rolled * 4 + row_seg[None, :, None] * 2 + level_seg[:, None, None]
    return jnp.broadcast_to(keys_grid[None], (batch_size, level_count, lat_rows, lon_cols))

def reference(inputs, grad_out, gains, qkv_weight, proj_weight, bias_table, rel_ids, groups):
    level_count = inputs.shape[1]
    forward_roll = (-(level_count // 2), -(WT // 2), -(WN // 2))
    backward_roll = (level_count // 2, WT // 2, WN // 2)
    plain_keys = jnp.zeros(inputs.shape[:4], jnp.int32)
    shifted_keys = shift_keys(groups, inputs.shape[0])
    mid = block_forward(inputs, 0, gains, qkv_weight, proj_weight, bias_table, rel_ids, plain_keys)
    frame_one = jnp.roll(mid, forward_roll, axis=(1, 2, 3))
    out_one = block_forward(frame_one, 1, gains, qkv_weight, proj_weight, bias_table, rel_ids, shifted_keys)
    outputs = jnp.roll(out_one, backward_roll, axis=(1, 2, 3))
    grad_frame_one = jnp.roll(grad_out, forward_roll, axis=(1, 2, 3))
    dframe_one, qkv_one, proj_one, gain_one, bias_one = block_backward(frame_one, grad_frame_one, 1, gains, qkv_weight, proj_weight, bias_table, rel_ids, shifted_keys)
    grad_mid = jnp.roll(dframe_one, backward_roll, axis=(1, 2, 3))
    grad_inputs, qkv_zero, proj_zero, gain_zero, bias_zero = block_backward(inputs, grad_mid, 0, gains, qkv_weight, proj_weight, bias_table, rel_ids, plain_keys)
    factor = TOKENS ** (-0.5)
    grad_gains = jnp.stack([gain_zero, gain_one]) * factor
    grad_qkv = jnp.stack([qkv_zero, qkv_one]) * factor
    grad_proj = jnp.stack([proj_zero, proj_one]) * factor
    grad_bias = jnp.stack([bias_zero, bias_one]) * factor
    return (outputs, grad_inputs, grad_gains, grad_qkv, grad_proj, grad_bias)
```

```python
import functools

import jax
import jax.numpy as jnp
import numpy as np
from jax import lax
from jax.experimental import pallas as pl
from jax.experimental.pallas import tpu as pltpu
from jax.sharding import Mesh, PartitionSpec as P

F32 = jnp.float32
BF16 = jnp.bfloat16
EPSILON = 1e-05
NEGATIVE = -1e30
D = 512
HEADS = 16
NREL = 759
SCALE = 32 ** (-0.5)
AXES = ("yh", "x", "z", "c", "yl")
SIZES = (2, 4, 8, 2, 2)
VMEM = 56 << 20

QUADS = ((1, 1), (1, 0), (0, 1), (0, 0))


def _token(rh, ch, l, r, c):
    return (rh * 2 + ch) * 36 + l * 18 + r * 6 + c


def _tables():
    px = np.zeros((144, 192), np.float32)
    ps = np.zeros((192, 144), np.float32)
    pf = np.zeros((144, 192), np.float32)
    pm = np.zeros((144, 144), np.float32)
    rows = np.zeros((144, 12), np.float32)
    cols = np.zeros((144, 12), np.float32)
    flags = np.zeros((144, 2), np.float32)
    for l in range(2):
        for row in range(6):
            for col in range(12):
                rh, r, ch, c = row // 3, row % 3, col // 6, col % 6
                t = _token(rh, ch, l, r, c)
                px[t, 16 * (l * 6 + row) + col] = 1
                pm[t, l * 72 + row * 12 + col] = 1
                rows[t, l * 6 + row] = 1
                cols[t, col] = 1
                flags[t] = (l, rh)
                k = QUADS.index((rh, ch))
                ps[48 * k + (1 - l) * 18 + r * 6 + c, t] = 1
    for k in range(4):
        for i in range(36):
            pf[36 * k + i, 48 * k + i] = 1
    bf = jnp.bfloat16
    return {
        "px": px.astype(bf),
        "ps": ps.astype(bf),
        "pf": pf.astype(bf),
        "pft": pf.T.copy().astype(bf),
        "pst": ps.T.copy().astype(bf),
        "slab": (px.T @ ps.T).astype(bf),
        "slabt": px.T.copy().astype(bf),
        "pm": pm.astype(bf),
        "rows": rows.astype(bf),
        "cols": cols,
        "flags": flags,
    }


TABLES = _tables()


def dot(a, b):
    return lax.dot_general(a, b, (((1,), (0,)), ((), ())), preferred_element_type=F32)


def dot_nt(a, b):
    return lax.dot_general(a, b, (((1,), (1,)), ((), ())), preferred_element_type=F32)


def dot_tn(a, b):
    return lax.dot_general(a, b, (((0,), (0,)), ((), ())), preferred_element_type=F32)


def lane_masks():
    lane = lax.broadcasted_iota(jnp.int32, (1, 128), 1) >> 5
    return [jnp.where(lane == k, 1.0, 0.0).astype(F32) for k in range(4)]


def stack_heads(group, masks):
    return jnp.concatenate([group * m.astype(BF16) for m in masks], axis=0)


def fold_heads(stacked, masks):
    total = stacked[0:144] * masks[0]
    for k in range(1, 4):
        total = total + stacked[144 * k : 144 * (k + 1)] * masks[k]
    return total


def pad_keys(group):
    return jnp.concatenate([group, jnp.zeros((112, 128), BF16)], axis=0)


def normalize(x):
    center = x - jnp.mean(x, axis=-1, keepdims=True)
    rstd = lax.rsqrt(jnp.mean(center * center, axis=-1, keepdims=True) + EPSILON)
    return center * rstd, rstd


def place_table(tab, scr):
    scr[...] = jnp.full((HEADS, 768), NEGATIVE, F32)
    scr[:, 0:NREL] = tab


def gather_bias(scr, rel_lo, rel_hi, head):
    acc = None
    for k in range(6):
        row = jnp.broadcast_to(scr[head : head + 1, k * 128 : (k + 1) * 128], (144, 128))
        got = [jnp.take_along_axis(row, lo, axis=1) for lo in rel_lo]
        acc = got if k == 0 else [jnp.where(hi == k, g, a) for hi, g, a in zip(rel_hi, got, acc)]
    return jnp.concatenate(acc, axis=1)


def split_rel(rel_ref):
    tiles = [rel_ref[:, 0:128], rel_ref[:, 128:256]]
    return [t & 127 for t in tiles], [t >> 7 for t in tiles]


def group_probs(qkv_ref, g, masks, scr, rel_lo, rel_hi, allowed):
    qg = qkv_ref[:, 128 * g : 128 * (g + 1)]
    kg = pad_keys(qkv_ref[:, 512 + 128 * g : 512 + 128 * (g + 1)])
    q4 = stack_heads(qg, masks)
    s4 = dot_nt(q4, kg) * SCALE
    out = []
    for k in range(4):
        s = s4[144 * k : 144 * (k + 1)] + gather_bias(scr, rel_lo, rel_hi, 4 * g + k)
        if allowed is not None:
            s = jnp.where(allowed, s, NEGATIVE)
        e = jnp.exp(s - jnp.max(s, axis=-1, keepdims=True))
        out.append(e * (1.0 / jnp.sum(e, axis=-1, keepdims=True)))
    return q4, kg, jnp.concatenate(out, axis=0)


def group_back(g, q4, kg, vg, p4, p4b, do, masks, dqkv_ref, ds0_ref, ds1_ref):
    do4 = stack_heads(do[:, 128 * g : 128 * (g + 1)], masks)
    dp4 = dot_nt(do4, vg)
    dqkv_ref[:, 1024 + 128 * g : 1024 + 128 * (g + 1)] = dot_tn(p4b, do4)[0:144].astype(BF16)
    ds4 = p4 * (dp4 - jnp.sum(dp4 * p4, axis=-1, keepdims=True))
    ds0_ref[576 * g : 576 * (g + 1), :] = ds4[:, 0:128]
    ds1_ref[576 * g : 576 * (g + 1), :] = ds4[:, 128:256]
    ds4b = ds4.astype(BF16)
    dq = fold_heads(dot(ds4b, kg), masks) * SCALE
    dqkv_ref[:, 128 * g : 128 * (g + 1)] = dq.astype(BF16)
    dk = dot_tn(ds4b, q4)[0:144] * SCALE
    dqkv_ref[:, 512 + 128 * g : 512 + 128 * (g + 1)] = dk.astype(BF16)


def finish_back(dqkv_ref, wqkv_ref, n, rstd, gain, g32, dgain_ref):
    dh = dot_nt(dqkv_ref[...], wqkv_ref[0])
    dgain_ref[...] = jnp.sum(dh * n, axis=0, keepdims=True)
    dn = dh * gain
    return (
        rstd
        * (
            dn
            - jnp.mean(dn, axis=-1, keepdims=True)
            - n * jnp.mean(dn * n, axis=-1, keepdims=True)
        )
        + g32
    )


def weight_terms(idx_ref, h, o, dqkv, g, keep_ref, send_ref):
    core = idx_ref[0]
    p = lax.broadcasted_iota(jnp.int32, (256, 512), 0)
    row = lax.broadcasted_iota(jnp.int32, (256, 512), 1)
    base = ((p >> 5) << 6) + (((p >> 2) & 1) << 5) + (((p >> 3) & 1) << 4) + (((p >> 4) & 1) << 3)
    base = base + (p & 3)
    for which, ref in ((core, keep_ref), (1 - core, send_ref)):
        pick = jnp.where(row == base + which * 4, 1.0, 0.0).astype(BF16)
        ht = dot_nt(pick, h).astype(BF16)
        ot = dot_nt(pick, o).astype(BF16)
        ref[:, 0:1536] = dot(ht, dqkv).astype(BF16)
        ref[:, 1536:2048] = dot(ot, g).astype(BF16)


def first_kernel(
    idx_ref, x_ref, go_ref, grp_ref, gain_ref, wqkv_ref, wproj_ref, tab_ref, rel_ref,
    px_ref, ps_ref, pm_ref, rows_ref, cols_ref,
    own_ref, lon_ref, lat_ref, dia_ref, n_ref, rstd_ref, qkv_ref, p_ref, o_ref, relp_ref,
    slab, pay, tabs,
):
    masks = lane_masks()
    px = px_ref[...]
    slab[...] = jnp.zeros((192, 1024), BF16)
    for l in range(2):
        for r in range(6):
            at = 16 * (l * 6 + r)
            slab[at : at + 12, 0:512] = x_ref[0, l, r]
            slab[at : at + 12, 512:1024] = go_ref[0, l, r]
    both = dot(px, slab[...])
    x = both[:, 0:512]
    pay[:, 512:1024] = both[:, 512:1024].astype(BF16)
    grid = jnp.concatenate([grp_ref[0], grp_ref[1]], axis=0).astype(F32).astype(BF16)
    picked = dot(rows_ref[...], grid) * cols_ref[...]
    group = jnp.sum(picked, axis=-1, keepdims=True)
    pay[:, 1024:1152] = jnp.broadcast_to(group, (144, 128)).astype(BF16)

    rel = rel_ref[...]
    pm = pm_ref[...]
    parts = []
    for part in (rel >> 5, rel & 31):
        half = dot(pm, part.astype(F32).astype(BF16)).astype(BF16)
        parts.append(dot_nt(half, pm).astype(jnp.int32))
    relp_ref[...] = jnp.full((144, 256), 767, jnp.int32)
    relp_ref[:, 0:144] = parts[0] * 32 + parts[1]
    rel_lo, rel_hi = split_rel(relp_ref)

    n, rstd = normalize(x)
    n_ref[...] = n
    rstd_ref[...] = rstd
    h = (n * gain_ref[0:1, :]).astype(BF16)
    qkv_ref[...] = dot(h, wqkv_ref[0]).astype(BF16)
    place_table(tab_ref[0, idx_ref[1]], tabs)
    for g in range(4):
        _, _, p4 = group_probs(qkv_ref, g, masks, tabs, rel_lo, rel_hi, None)
        p4b = p4.astype(BF16)
        p_ref[576 * g : 576 * (g + 1), :] = p4b
        vg = pad_keys(qkv_ref[:, 1024 + 128 * g : 1024 + 128 * (g + 1)])
        o_ref[:, 128 * g : 128 * (g + 1)] = fold_heads(dot(p4b, vg), masks).astype(BF16)
    pay[:, 0:512] = (x + dot(o_ref[...], wproj_ref[0])).astype(BF16)
    out = dot(ps_ref[...], pay[...]).astype(BF16)
    own_ref[...] = out[0:48]
    lon_ref[...] = out[48:96]
    lat_ref[...] = out[96:144]
    dia_ref[...] = out[144:192]


def second_kernel(
    idx_ref, own_ref, lon_ref, lat_ref, dia_ref, gain_ref, wqkv_ref, wproj_ref, tab_ref, rel_ref,
    pf_ref, pft_ref, flags_ref,
    oown_ref, olon_ref, olat_ref, odia_ref, h_ref, o_ref, dqkv_ref, g_ref, dgain_ref, ds0_ref, ds1_ref,
    qkv_ref, tabs, back,
):
    masks = lane_masks()
    frame = dot(
        pf_ref[...], jnp.concatenate([own_ref[...], lon_ref[...], lat_ref[...], dia_ref[...]], axis=0)
    )
    x = frame[:, 0:512]
    g32 = frame[:, 512:1024]
    gb = g32.astype(BF16)
    g_ref[...] = gb
    lat = idx_ref[1].astype(F32)
    key = frame[:, 1024:1025] * 4.0 + flags_ref[:, 1:2] * (2.0 * lat) + flags_ref[:, 0:1]
    eye = lax.broadcasted_iota(jnp.int32, (144, 256), 0) == lax.broadcasted_iota(
        jnp.int32, (144, 256), 1
    )
    key_row = jnp.sum(jnp.where(eye, key, 0.0), axis=0, keepdims=True)
    allowed = key == key_row
    rel_lo, rel_hi = split_rel(rel_ref)
    gain = gain_ref[1:2, :]

    n, rstd = normalize(x)
    h = (n * gain).astype(BF16)
    h_ref[...] = h
    qkv_ref[...] = dot(h, wqkv_ref[0]).astype(BF16)
    do = dot_nt(gb, wproj_ref[0]).astype(BF16)
    place_table(tab_ref[0, idx_ref[1]], tabs)
    for g in range(4):
        q4, kg, p4 = group_probs(qkv_ref, g, masks, tabs, rel_lo, rel_hi, allowed)
        p4b = p4.astype(BF16)
        vg = pad_keys(qkv_ref[:, 1024 + 128 * g : 1024 + 128 * (g + 1)])
        o_ref[:, 128 * g : 128 * (g + 1)] = fold_heads(dot(p4b, vg), masks).astype(BF16)
        group_back(g, q4, kg, vg, p4, p4b, do, masks, dqkv_ref, ds0_ref, ds1_ref)
    back[:, 0:512] = (x + dot(o_ref[...], wproj_ref[0])).astype(BF16)
    df = finish_back(dqkv_ref, wqkv_ref, n, rstd, gain, g32, dgain_ref)
    back[:, 512:1024] = df.astype(BF16)
    out = dot(pft_ref[...], back[...]).astype(BF16)
    oown_ref[...] = out[0:48]
    olon_ref[...] = out[48:96]
    olat_ref[...] = out[96:144]
    odia_ref[...] = out[144:192]


def weights_kernel(idx_ref, h_ref, o_ref, dqkv_ref, g_ref, keep_ref, send_ref):
    weight_terms(idx_ref, h_ref[...], o_ref[...], dqkv_ref[...], g_ref[...], keep_ref, send_ref)


def third_kernel(
    idx_ref, own_ref, lon_ref, lat_ref, dia_ref, gain_ref, wqkv_ref, wproj_ref,
    n_ref, rstd_ref, qkv_ref, p_ref, o_ref, pst_ref, slab_ref, slabt_ref,
    out_ref, gin_ref, dgain_ref, ds0_ref, ds1_ref, keep_ref, send_ref,
    dqkv_ref,
):
    masks = lane_masks()
    pieces = jnp.concatenate([own_ref[...], lon_ref[...], lat_ref[...], dia_ref[...]], axis=0)
    out = dot(slab_ref[...], pieces[:, 0:512]).astype(BF16)
    g32 = dot(pst_ref[...], pieces[:, 512:1024])
    gb = g32.astype(BF16)
    gain = gain_ref[0:1, :]
    n = n_ref[...]
    do = dot_nt(gb, wproj_ref[0]).astype(BF16)
    for g in range(4):
        q4 = stack_heads(qkv_ref[:, 128 * g : 128 * (g + 1)], masks)
        kg = pad_keys(qkv_ref[:, 512 + 128 * g : 512 + 128 * (g + 1)])
        vg = pad_keys(qkv_ref[:, 1024 + 128 * g : 1024 + 128 * (g + 1)])
        p4b = p_ref[576 * g : 576 * (g + 1), :]
        group_back(g, q4, kg, vg, p4b.astype(F32), p4b, do, masks, dqkv_ref, ds0_ref, ds1_ref)
    df = finish_back(dqkv_ref, wqkv_ref, n, rstd_ref[...], gain, g32, dgain_ref)
    gin = dot(slabt_ref[...], df.astype(BF16)).astype(BF16)
    for l in range(2):
        for r in range(6):
            at = 16 * (l * 6 + r)
            out_ref[0, l, r] = out[at : at + 12]
            gin_ref[0, l, r] = gin[at : at + 12]
    h = (n * gain).astype(BF16)
    weight_terms(idx_ref, h, o_ref[...], dqkv_ref[...], gb, keep_ref, send_ref)


def scatter_kernel(idx_ref, rel_ref, d0_ref, d1_ref, dgain_ref, keep_ref, send_ref):
    iota = lax.broadcasted_iota(jnp.int32, (128, 256), 0)

    def body(i, acc):
        ids = rel_ref[pl.ds(i, 1), :]
        low, high = ids & 127, ids >> 7
        hot = jnp.where(iota == low, 1.0, 0.0).astype(BF16)
        d = jnp.concatenate(
            [d0_ref[pl.ds(i, 16, stride=144), :], d1_ref[pl.ds(i, 16, stride=144), :]], axis=1
        )
        lhs = jnp.concatenate([jnp.where(high == k, d, 0.0) for k in range(6)], axis=0)
        return acc + dot_nt(lhs.astype(BF16), hot)

    acc = lax.fori_loop(0, 144, body, jnp.zeros((96, 128), F32), unroll=8)
    table = jnp.concatenate([acc[16 * k : 16 * (k + 1)] for k in range(6)], axis=1)
    first = lax.broadcasted_iota(jnp.int32, (8, 256), 0) == 0
    halves = []
    for c in range(2):
        gain = jnp.where(first, dgain_ref[:, 256 * c : 256 * (c + 1)], 0.0)
        halves.append(jnp.concatenate([table[8 * c : 8 * (c + 1)], gain], axis=1))
    mine = idx_ref[0] == 0
    keep_ref[...] = jnp.where(mine, halves[0], halves[1])
    send_ref[...] = jnp.where(mine, halves[1], halves[0])


def payload_kernel(k0_ref, r0_ref, k1_ref, r1_ref, t0_ref, u0_ref, t1_ref, u1_ref, out_ref):
    tabs = [t0_ref[...] + u0_ref[...], t1_ref[...] + u1_ref[...]]
    for b, (k_ref, r_ref) in enumerate(((k0_ref, r0_ref), (k1_ref, r1_ref))):
        total = (k_ref[...].astype(F32) + r_ref[...].astype(F32)).astype(BF16)
        for half in range(2):
            out_ref[half, 32 * b : 32 * (b + 1), :] = total[:, 1024 * half : 1024 * (half + 1)]
    for half in range(2):
        rows = jnp.concatenate([tabs[half], jnp.zeros((8, 1024), F32)], axis=0)
        out_ref[half, 64:80, :] = rows.astype(BF16)


def plane_kernel(idx_ref, got_ref, keep_ref, tkeep_ref, send_ref):
    total = got_ref[0, 0:64, :].astype(F32)
    for s in range(1, 16):
        total = total + got_ref[s, 0:64, :].astype(F32)
    tabs = []
    for lat in range(2):
        t = got_ref[lat, 64:80, :].astype(F32)
        for s in range(1, 8):
            t = t + got_ref[2 * s + lat, 64:80, :].astype(F32)
        tabs.append(t[0:8])
    mine = idx_ref[2] == 0
    tab = jnp.concatenate(tabs, axis=0).astype(BF16)
    tkeep_ref[...] = tab
    send_ref[32:48, :] = tab
    for b in range(2):
        lo, hi = total[32 * b : 32 * b + 16], total[32 * b + 16 : 32 * b + 32]
        keep_ref[16 * b : 16 * (b + 1), :] = jnp.where(mine, lo, hi)
        send_ref[16 * b : 16 * (b + 1), :] = jnp.where(mine, hi, lo).astype(BF16)


def ring_kernel(step, idx_ref, keep_ref, tkeep_ref, got_ref, nkeep_ref, ntkeep_ref, send_ref):
    rows = keep_ref.shape[0]
    half = rows // 4
    mine = idx_ref[2 + step] == 0
    total = keep_ref[...] + got_ref[0:rows, :].astype(F32)
    tab = (tkeep_ref[...].astype(F32) + got_ref[32 if rows == 32 else 16 : (48 if rows == 32 else 32), :].astype(F32)).astype(BF16)
    ntkeep_ref[...] = tab
    keeps, sends = [], []
    for b in range(2):
        lo = total[2 * half * b : 2 * half * b + half]
        hi = total[2 * half * b + half : 2 * half * (b + 1)]
        keeps.append(jnp.where(mine, lo, hi))
        sends.append(jnp.where(mine, hi, lo))
    nkeep_ref[...] = jnp.concatenate(keeps, axis=0)
    send = jnp.concatenate(sends, axis=0)
    if half == 4:
        send = jnp.concatenate([send, jnp.zeros((8, 1024), F32)], axis=0)
    send_ref[0:16, :] = send.astype(BF16)
    send_ref[16:32, :] = tab


def last_ring_kernel(keep_ref, tkeep_ref, got_ref, tab_ref, send_ref):
    total = keep_ref[...] + got_ref[0:16, :].astype(F32)[0:8]
    tab = (tkeep_ref[...].astype(F32) + got_ref[16:32, :].astype(F32)).astype(BF16)
    tab_ref[...] = tab
    send_ref[16:32, :] = tab
    send_ref[0:16, :] = jnp.concatenate([total, jnp.zeros((8, 1024), F32)], axis=0).astype(BF16)


def last_kernel(
    factor, idx_ref, own_ref, lat_ref, core_ref, dia_ref, gain_ref, qkv_ref, proj_ref, bias_ref
):
    core0 = idx_ref[0] == 0
    lat0 = idx_ref[1] == 0
    own = own_ref[...].astype(F32)
    got = lat_ref[...].astype(F32)
    low = jnp.where(lat0, own[0:8], got[0:8]) * factor
    high = jnp.where(lat0, got[0:8], own[0:8]) * factor
    for b in range(2):
        qkv_ref[b, :, 0:1024] = low[4 * b : 4 * b + 4]
        qkv_ref[b, :, 1024:1536] = high[4 * b : 4 * b + 4, 0:512]
        proj_ref[b, :, :] = high[4 * b : 4 * b + 4, 512:1024]
    t_own, t_lat = own[16:32], got[16:32]
    t_core, t_dia = core_ref[...].astype(F32), dia_ref[...].astype(F32)
    for b in range(2):
        near = jnp.where(lat0, t_own, t_lat) if b == 0 else jnp.where(lat0, t_lat, t_own)
        far = jnp.where(lat0, t_core, t_dia) if b == 0 else jnp.where(lat0, t_dia, t_core)
        for c in range(2):
            tab = jnp.where(core0, near, far) if c == 0 else jnp.where(core0, far, near)
            tab = tab * factor
            for w in range(2):
                bias_ref[b, w, 8 * c : 8 * (c + 1), :] = tab[8 * w : 8 * w + 8, 0:NREL]
            gain_ref[b : b + 1, 256 * c : 256 * (c + 1)] = tab[0:1, 768:1024] + tab[8:9, 768:1024]


def _whole(shape):
    return pl.BlockSpec(shape, lambda *_: (0,) * len(shape))


SMEM = pl.BlockSpec(memory_space=pltpu.SMEM)


def call(body, outs, *args, specs=None, scratch=(), cost=None):
    specs = specs or {}
    in_specs = [SMEM if (i == 0 and a.dtype == jnp.int32 and a.ndim == 1) else specs.get(i, _whole(a.shape)) for i, a in enumerate(args)]
    return pl.pallas_call(
        body,
        grid=(1,),
        in_specs=in_specs,
        out_specs=[_whole(s) for s, _ in outs],
        out_shape=[jax.ShapeDtypeStruct(s, t) for s, t in outs],
        scratch_shapes=[pltpu.VMEM(s, t) for s, t in scratch],
        compiler_params=pltpu.CompilerParams(vmem_limit_bytes=VMEM),
        cost_estimate=cost,
    )(*args)


def _decode(s):
    out = []
    for n in reversed(SIZES):
        out.append(s % n)
        s //= n
    return tuple(reversed(out))


def _encode(place):
    s = 0
    for v, n in zip(place, SIZES):
        s = s * n + v
    return s


def permute(value, move):
    pairs = [(s, _encode(move(*_decode(s)))) for s in range(256)]
    return lax.ppermute(value, AXES, pairs)


def lon_step(offset, flip):
    def move(yh, x, z, c, yl):
        lon = (((yh * 4 + x) * 8 + z) * 2 + c + offset) % 128
        return (lon // 64, lon // 16 % 4, lon // 2 % 8, lon % 2, yl ^ flip)

    return move


def halo(pieces, offset):
    own, lon, lat, dia = pieces
    return (
        own,
        permute(lon, lon_step(offset, 0)),
        permute(lat, lon_step(0, 1)),
        permute(dia, lon_step(offset, 1)),
    )


def on_device(inputs, grad_out, gains, qkv_weight, proj_weight, bias_table, rel_ids, groups):
    T = {k: jnp.asarray(v) for k, v in TABLES.items()}
    z = lax.axis_index("z")
    idx = jnp.stack([lax.axis_index("c"), lax.axis_index("yl"), z & 1, (z >> 1) & 1, (z >> 2) & 1])
    idx = idx.astype(jnp.int32)

    def block(b, shape):
        return pl.BlockSpec((1,) + shape, lambda *_: (b,) + (0,) * len(shape))

    def weights(b, first):
        return {
            first: block(b, (D, 3 * D)),
            first + 1: block(b, (D, D)),
            first + 2: block(b, (2, HEADS, NREL)),
        }

    piece = ((48, 1152), BF16)
    own, lon, lat, dia, n0, rstd0, qkv0, p0, o0, relp = call(
        first_kernel,
        [piece] * 4
        + [
            ((144, D), F32),
            ((144, 1), F32),
            ((144, 3 * D), BF16),
            ((2304, 256), BF16),
            ((144, D), BF16),
            ((144, 256), jnp.int32),
        ],
        idx, inputs, grad_out, groups, gains, qkv_weight, proj_weight, bias_table, rel_ids,
        T["px"], T["ps"], T["pm"], T["rows"], T["cols"],
        specs=weights(0, 5),
        scratch=[((192, 1024), BF16), ((144, 1152), BF16), ((HEADS, 768), F32)],
    )
    pieces = halo((own, lon, lat, dia), -1)
    back = ((48, 1024), BF16)
    ds_shape = ((2304, 128), F32)
    own, lon, lat, dia, h1, o1, dqkv1, g1, dgain1, ds10, ds11 = call(
        second_kernel,
        [back] * 4
        + [
            ((144, D), BF16),
            ((144, D), BF16),
            ((144, 3 * D), BF16),
            ((144, D), BF16),
            ((1, D), F32),
            ds_shape,
            ds_shape,
        ],
        idx, *pieces, gains, qkv_weight, proj_weight, bias_table, relp, T["pf"], T["pft"], T["flags"],
        specs=weights(1, 6),
        scratch=[((144, 3 * D), BF16), ((HEADS, 768), F32), ((144, 2 * D), BF16)],
    )
    pieces = halo((own, lon, lat, dia), 1)
    wshape = ((256, 4 * D), BF16)
    keep1, send1 = call(weights_kernel, [wshape] * 2, idx, h1, o1, dqkv1, g1)
    other_core = lambda yh, x, z, c, yl: (yh, x, z, 1 - c, yl)
    recv1 = permute(send1, other_core)
    tshape = ((8, 1024), F32)
    tkeep1, tsend1 = call(scatter_kernel, [tshape] * 2, idx, relp, ds10, ds11, dgain1)
    trecv1 = permute(tsend1, other_core)
    outputs, grad_inputs, dgain0, ds00, ds01, keep0, send0 = call(
        third_kernel,
        [
            (inputs.shape, BF16),
            (inputs.shape, BF16),
            ((1, D), F32),
            ds_shape,
            ds_shape,
            wshape,
            wshape,
        ],
        idx, *pieces, gains, qkv_weight, proj_weight, n0, rstd0, qkv0, p0, o0,
        T["pst"], T["slab"], T["slabt"],
        specs={6: block(0, (D, 3 * D)), 7: block(0, (D, D))},
        scratch=[((144, 3 * D), BF16)],
    )
    recv0 = permute(send0, other_core)
    tkeep0, tsend0 = call(scatter_kernel, [tshape] * 2, idx, relp, ds00, ds01, dgain0)
    trecv0 = permute(tsend0, other_core)

    wspec = pl.BlockSpec((32, 4 * D), lambda i: (i, 0))
    tspec = pl.BlockSpec((8, 1024), lambda i: (0, 0))
    payload = pl.pallas_call(
        payload_kernel,
        grid=(8,),
        in_specs=[wspec] * 4 + [tspec] * 4,
        out_specs=pl.BlockSpec((2, 80, 1024), lambda i: (i, 0, 0)),
        out_shape=jax.ShapeDtypeStruct((16, 80, 1024), BF16),
        compiler_params=pltpu.CompilerParams(vmem_limit_bytes=VMEM),
    )(keep0, recv0, keep1, recv1, tkeep0, trecv0, tkeep1, trecv1)
    got = lax.all_to_all(payload, ("yh", "x", "yl"), 0, 0, tiled=True)
    tab16 = ((16, 1024), BF16)
    keep, tab, send = call(
        plane_kernel, [((32, 1024), F32), tab16, ((48, 1024), BF16)], idx, got
    )
    got = permute(send, lambda yh, x, z, c, yl: (yh, x, z ^ 1, c, yl))
    pair = ((32, 1024), BF16)
    keep, tab, send = call(
        functools.partial(ring_kernel, 1), [((16, 1024), F32), tab16, pair], idx, keep, tab, got
    )
    got = permute(send, lambda yh, x, z, c, yl: (yh, x, z ^ 2, c, yl))
    keep, tab, send = call(
        functools.partial(ring_kernel, 2), [((8, 1024), F32), tab16, pair], idx, keep, tab, got
    )
    got = permute(send, lambda yh, x, z, c, yl: (yh, x, z ^ 4, c, yl))
    tab, own = call(last_ring_kernel, [tab16, pair], keep, tab, got)
    from_core = permute(tab, other_core)
    from_dia = permute(tab, lambda yh, x, z, c, yl: (yh, x, z, 1 - c, 1 - yl))
    from_lat = permute(own, lambda yh, x, z, c, yl: (yh, x, z, c, 1 - yl))
    factor = 36864 ** (-0.5)
    grad_gains, grad_qkv, grad_proj, grad_bias = call(
        functools.partial(last_kernel, factor),
        [
            ((2, D), F32),
            ((2, 4, 3 * D), F32),
            ((2, 4, D), F32),
            ((2, 2, HEADS, NREL), F32),
        ],
        idx, own, from_lat, from_core, from_dia,
    )
    return (outputs, grad_inputs, grad_gains, grad_qkv, grad_proj, grad_bias)


def solution(mesh):
    fine = Mesh(mesh.devices.reshape(SIZES), AXES)
    lon = ("yh", "x", "z", "c")
    field = P(None, None, "yl", lon, None)
    rows = P(None, lon, None)
    return jax.shard_map(
        on_device,
        mesh=fine,
        in_specs=(field, field, P(), P(), P(), P(), P(), P(None, "yl", lon)),
        out_specs=(field, field, P(), rows, rows, P()),
        check_vma=False,
    )
```

```python
import functools

import jax
import jax.numpy as jnp
import numpy as np
from jax import lax
from jax.experimental import pallas as pl
from jax.experimental.pallas import tpu as pltpu
from jax.sharding import Mesh, PartitionSpec as P

F32 = jnp.float32
BF16 = jnp.bfloat16
EPSILON = 1e-05
NEGATIVE = -1e30
D = 512
HEADS = 16
NREL = 759
SCALE = 32 ** (-0.5)
AXES = ("yh", "x1", "x0", "z2", "z1", "z0", "c", "yl")
VMEM = 56 << 20

QUADS = ((1, 1), (1, 0), (0, 1), (0, 0))


def _token(rh, ch, l, r, c):
    return (rh * 2 + ch) * 36 + l * 18 + r * 6 + c


def _tables():
    px = np.zeros((144, 144), np.float32)
    ps = np.zeros((192, 144), np.float32)
    pf = np.zeros((144, 192), np.float32)
    pm = np.zeros((144, 144), np.float32)
    rows = np.zeros((144, 12), np.float32)
    cols = np.zeros((144, 12), np.float32)
    flags = np.zeros((144, 2), np.float32)
    for l in range(2):
        for row in range(6):
            for col in range(12):
                rh, r, ch, c = row // 3, row % 3, col // 6, col % 6
                t = _token(rh, ch, l, r, c)
                px[t, (row * 12 + col) * 2 + l] = 1
                pm[t, l * 72 + row * 12 + col] = 1
                rows[t, row * 2 + l] = 1
                cols[t, col] = 1
                flags[t] = (l, rh)
                k = QUADS.index((rh, ch))
                ps[48 * k + (1 - l) * 18 + r * 6 + c, t] = 1
    for k in range(4):
        for i in range(36):
            pf[36 * k + i, 48 * k + i] = 1
    bf = jnp.bfloat16
    return {
        "px": px.astype(bf),
        "ps": ps.astype(bf),
        "pf": pf.astype(bf),
        "pft": pf.T.copy().astype(bf),
        "pst": ps.T.copy().astype(bf),
        "cells": (px.T @ ps.T).astype(bf),
        "pxt": px.T.copy().astype(bf),
        "pm": pm.astype(bf),
        "rows": rows.astype(bf),
        "cols": cols,
        "flags": flags,
    }


TABLES = _tables()


def dot(a, b):
    return lax.dot_general(a, b, (((1,), (0,)), ((), ())), preferred_element_type=F32)


def dot_nt(a, b):
    return lax.dot_general(a, b, (((1,), (1,)), ((), ())), preferred_element_type=F32)


def dot_tn(a, b):
    return lax.dot_general(a, b, (((0,), (0,)), ((), ())), preferred_element_type=F32)


def lane_masks():
    lane = lax.broadcasted_iota(jnp.int32, (1, 128), 1) >> 5
    return [jnp.where(lane == k, 1.0, 0.0).astype(F32) for k in range(4)]


def stack_heads(group, masks):
    return jnp.concatenate([group * m.astype(BF16) for m in masks], axis=0)


def fold_heads(stacked, masks):
    total = stacked[0:144] * masks[0]
    for k in range(1, 4):
        total = total + stacked[144 * k : 144 * (k + 1)] * masks[k]
    return total


def pad_keys(group):
    return jnp.concatenate([group, jnp.zeros((112, 128), BF16)], axis=0)


def normalize(x):
    center = x - jnp.mean(x, axis=-1, keepdims=True)
    rstd = lax.rsqrt(jnp.mean(center * center, axis=-1, keepdims=True) + EPSILON)
    return center * rstd, rstd


def pack_table(tab, words, scales, offsets):
    low = jnp.min(tab, axis=-1, keepdims=True)
    scale = jnp.maximum(jnp.max(tab, axis=-1, keepdims=True) - low, 1e-20) * (1.0 / 65535.0)
    q = jnp.clip(jnp.floor((tab - low) / scale + 0.5), 0.0, 65535.0).astype(jnp.int32)
    high = jnp.concatenate([q[4 * g : 4 * g + 2] for g in range(4)], axis=0)
    rest = jnp.concatenate([q[4 * g + 2 : 4 * g + 4] for g in range(4)], axis=0)
    words[...] = jnp.zeros((8, 768), jnp.int32)
    words[:, 0:NREL] = ((high - 32768) << 16) + rest
    signed = lax.broadcasted_iota(jnp.int32, (HEADS, 1), 0) & 3
    offset = low + jnp.where(signed < 2, 32768.0, 0.0) * scale
    scales[...] = jnp.broadcast_to(scale, (HEADS, 128))
    offsets[...] = jnp.broadcast_to(offset, (HEADS, 128))


def lookup(row, ids):
    acc = None
    for k in range(6):
        part = jnp.broadcast_to(row[:, 128 * k : 128 * (k + 1)], ids.shape)
        got = jnp.take_along_axis(part, ids & 127, axis=1)
        acc = got if k == 0 else jnp.where((ids >> 7) == k, got, acc)
    return acc


def tail_ids(ids):
    lane = lax.broadcasted_iota(jnp.int32, (24, 128), 1)
    total = jnp.where(lane < 16, ids[0:24], 0)
    for k in range(1, 6):
        piece = jnp.where(lane < 16, ids[24 * k : 24 * (k + 1)], 0)
        total = total + pltpu.roll(piece, 16 * k, 1)
    return total


def bias_pair(m, words, scales, offsets, ids, tails):
    row = words[m : m + 1, :]
    main = lookup(row, ids)
    tail = lookup(row, tails)
    parts = [tail] + [pltpu.roll(tail, 128 - 16 * k, 1) for k in range(1, 6)]
    tail = jnp.concatenate(parts, axis=0)
    lane = lax.broadcasted_iota(jnp.int32, (144, 128), 1)
    head = 4 * (m // 2) + m % 2
    out = []
    for h, take in ((head, lambda w: w >> 16), (head + 2, lambda w: w & 65535)):
        scale, offset = scales[h : h + 1, :], offsets[h : h + 1, :]
        a = take(main).astype(F32) * scale + offset
        b = jnp.where(lane < 16, take(tail).astype(F32) * scale + offset, NEGATIVE)
        out.append(jnp.concatenate([a, b], axis=1))
    return out


def fill_bias(table, rel_ref, words, scales, offsets, store):
    pack_table(table, words, scales, offsets)
    ids, tails = rel_ref[:, 0:128], tail_ids(rel_ref[:, 128:256])
    for m in range(8):
        head = 4 * (m // 2) + m % 2
        for h, b in zip((head, head + 2), bias_pair(m, words, scales, offsets, ids, tails)):
            store[144 * h : 144 * (h + 1), :] = b


def group_probs(qkv_ref, g, masks, bias_ref, allowed):
    qg = qkv_ref[:, 128 * g : 128 * (g + 1)]
    kg = pad_keys(qkv_ref[:, 512 + 128 * g : 512 + 128 * (g + 1)])
    q4 = stack_heads(qg, masks)
    s4 = dot_nt(q4, kg) * SCALE
    out = []
    for k in range(4):
        at = 144 * (4 * g + k)
        s = s4[144 * k : 144 * (k + 1)] + bias_ref[at : at + 144, :]
        if allowed is not None:
            s = jnp.where(allowed, s, NEGATIVE)
        e = jnp.exp(s - jnp.max(s, axis=-1, keepdims=True))
        out.append(e * (1.0 / jnp.sum(e, axis=-1, keepdims=True)))
    return q4, kg, jnp.concatenate(out, axis=0)


def group_back(g, q4, kg, vg, p4, p4b, do, masks, dqkv_ref, ds0_ref, ds1_ref):
    do4 = stack_heads(do[:, 128 * g : 128 * (g + 1)], masks)
    dp4 = dot_nt(do4, vg)
    dqkv_ref[:, 1024 + 128 * g : 1024 + 128 * (g + 1)] = dot_tn(p4b, do4)[0:144].astype(BF16)
    ds4 = p4 * (dp4 - jnp.sum(dp4 * p4, axis=-1, keepdims=True))
    ds0_ref[576 * g : 576 * (g + 1), :] = ds4[:, 0:128]
    ds1_ref[576 * g : 576 * (g + 1), :] = ds4[:, 128:256]
    ds4b = ds4.astype(BF16)
    dq = fold_heads(dot(ds4b, kg), masks) * SCALE
    dqkv_ref[:, 128 * g : 128 * (g + 1)] = dq.astype(BF16)
    dk = dot_tn(ds4b, q4)[0:144] * SCALE
    dqkv_ref[:, 512 + 128 * g : 512 + 128 * (g + 1)] = dk.astype(BF16)


def finish_back(dqkv_ref, wqkv_ref, n, rstd, gain, g32, dgain_ref):
    dh = dot_nt(dqkv_ref[...], wqkv_ref[0])
    dgain_ref[...] = jnp.sum(dh * n, axis=0, keepdims=True)
    dn = dh * gain
    return (
        rstd
        * (
            dn
            - jnp.mean(dn, axis=-1, keepdims=True)
            - n * jnp.mean(dn * n, axis=-1, keepdims=True)
        )
        + g32
    )


def weight_terms(idx_ref, h, o, dqkv, g, keep_ref, send_ref):
    core = idx_ref[0]
    p = lax.broadcasted_iota(jnp.int32, (256, 512), 0)
    row = lax.broadcasted_iota(jnp.int32, (256, 512), 1)
    base = p & 3
    base = base + ((((p >> 7) ^ (p >> 5)) & 1) << 6)
    for at, to in ((6, 3), (5, 7), (4, 8), (3, 5), (2, 4)):
        base = base + (((p >> at) & 1) << to)
    for which, ref in ((core, keep_ref), (1 - core, send_ref)):
        pick = jnp.where(row == base + which * 4, 1.0, 0.0).astype(BF16)
        ht = dot_nt(pick, h).astype(BF16)
        ot = dot_nt(pick, o).astype(BF16)
        ref[:, 0:1536] = dot(ht, dqkv).astype(BF16)
        ref[:, 1536:2048] = dot(ot, g).astype(BF16)


def first_kernel(
    idx_ref, x_ref, go_ref, grp_ref, gain_ref, wqkv_ref, wproj_ref, tab_ref, rel_ref,
    px_ref, ps_ref, pm_ref, rows_ref, cols_ref,
    own_ref, lon_ref, lat_ref, dia_ref, n_ref, rstd_ref, qkv_ref, p_ref, o_ref, relp_ref,
    cells, gs, pay, bias, words, scales, offsets,
):
    masks = lane_masks()
    for k in range(72):
        cells[2 * k : 2 * k + 2, 0:512] = x_ref[k].astype(F32)
        cells[2 * k : 2 * k + 2, 512:1024] = go_ref[k].astype(F32)
    both = dot(px_ref[...], cells[...].astype(BF16))
    x = both[:, 0:512]
    pay[:, 512:1024] = both[:, 512:1024].astype(BF16)
    for r in range(6):
        gs[2 * r : 2 * r + 2, :] = grp_ref[r].astype(F32)
    picked = dot(rows_ref[...], gs[...].astype(BF16)) * cols_ref[...]
    group = jnp.sum(picked, axis=-1, keepdims=True)
    pay[:, 1024:1152] = jnp.broadcast_to(group, (144, 128)).astype(BF16)

    rel = rel_ref[...]
    pm = pm_ref[...]
    parts = []
    for part in (rel >> 5, rel & 31):
        half = dot(pm, part.astype(F32).astype(BF16)).astype(BF16)
        parts.append(dot_nt(half, pm).astype(jnp.int32))
    relp_ref[...] = jnp.full((144, 256), 767, jnp.int32)
    relp_ref[:, 0:144] = parts[0] * 32 + parts[1]
    fill_bias(tab_ref[0, idx_ref[1]], relp_ref, words, scales, offsets, bias)

    n, rstd = normalize(x)
    n_ref[...] = n
    rstd_ref[...] = rstd
    h = (n * gain_ref[0:1, :]).astype(BF16)
    qkv_ref[...] = dot(h, wqkv_ref[0]).astype(BF16)
    for g in range(4):
        _, _, p4 = group_probs(qkv_ref, g, masks, bias, None)
        p4b = p4.astype(BF16)
        p_ref[576 * g : 576 * (g + 1), :] = p4b
        vg = pad_keys(qkv_ref[:, 1024 + 128 * g : 1024 + 128 * (g + 1)])
        o_ref[:, 128 * g : 128 * (g + 1)] = fold_heads(dot(p4b, vg), masks).astype(BF16)
    pay[:, 0:512] = (x + dot(o_ref[...], wproj_ref[0])).astype(BF16)
    out = dot(ps_ref[...], pay[...]).astype(BF16)
    own_ref[...] = out[0:48]
    lon_ref[...] = out[48:96]
    lat_ref[...] = out[96:144]
    dia_ref[...] = out[144:192]


def bias_kernel(idx_ref, tab_ref, rel_ref, out_ref, words, scales, offsets):
    fill_bias(tab_ref[0, idx_ref[1]], rel_ref, words, scales, offsets, out_ref)


def second_kernel(
    idx_ref, own_ref, lon_ref, lat_ref, dia_ref, gain_ref, wqkv_ref, wproj_ref, bias_ref,
    pf_ref, pft_ref, flags_ref,
    oown_ref, olon_ref, olat_ref, odia_ref, h_ref, o_ref, dqkv_ref, g_ref, dgain_ref, ds0_ref, ds1_ref,
    qkv_ref, back,
):
    masks = lane_masks()
    frame = dot(
        pf_ref[...], jnp.concatenate([own_ref[...], lon_ref[...], lat_ref[...], dia_ref[...]], axis=0)
    )
    x = frame[:, 0:512]
    g32 = frame[:, 512:1024]
    gb = g32.astype(BF16)
    g_ref[...] = gb
    lat = idx_ref[1].astype(F32)
    key = frame[:, 1024:1025] * 4.0 + flags_ref[:, 1:2] * (2.0 * lat) + flags_ref[:, 0:1]
    eye = lax.broadcasted_iota(jnp.int32, (144, 256), 0) == lax.broadcasted_iota(
        jnp.int32, (144, 256), 1
    )
    key_row = jnp.sum(jnp.where(eye, key, 0.0), axis=0, keepdims=True)
    allowed = key == key_row
    gain = gain_ref[1:2, :]

    n, rstd = normalize(x)
    h = (n * gain).astype(BF16)
    h_ref[...] = h
    qkv_ref[...] = dot(h, wqkv_ref[0]).astype(BF16)
    do = dot_nt(gb, wproj_ref[0]).astype(BF16)
    for g in range(4):
        q4, kg, p4 = group_probs(qkv_ref, g, masks, bias_ref, allowed)
        p4b = p4.astype(BF16)
        vg = pad_keys(qkv_ref[:, 1024 + 128 * g : 1024 + 128 * (g + 1)])
        o_ref[:, 128 * g : 128 * (g + 1)] = fold_heads(dot(p4b, vg), masks).astype(BF16)
        group_back(g, q4, kg, vg, p4, p4b, do, masks, dqkv_ref, ds0_ref, ds1_ref)
    back[:, 0:512] = (x + dot(o_ref[...], wproj_ref[0])).astype(BF16)
    df = finish_back(dqkv_ref, wqkv_ref, n, rstd, gain, g32, dgain_ref)
    back[:, 512:1024] = df.astype(BF16)
    out = dot(pft_ref[...], back[...]).astype(BF16)
    oown_ref[...] = out[0:48]
    olon_ref[...] = out[48:96]
    olat_ref[...] = out[96:144]
    odia_ref[...] = out[144:192]


def weights_kernel(idx_ref, h_ref, o_ref, dqkv_ref, g_ref, keep_ref, send_ref):
    weight_terms(idx_ref, h_ref[...], o_ref[...], dqkv_ref[...], g_ref[...], keep_ref, send_ref)


def third_kernel(
    idx_ref, own_ref, lon_ref, lat_ref, dia_ref, gain_ref, wqkv_ref, wproj_ref,
    n_ref, rstd_ref, qkv_ref, p_ref, o_ref, pst_ref, cells_ref, pxt_ref, after_ref,
    out_ref, gin_ref, dgain_ref, ds0_ref, ds1_ref, keep_ref, send_ref,
    dqkv_ref, outs,
):
    masks = lane_masks()
    pieces = jnp.concatenate([own_ref[...], lon_ref[...], lat_ref[...], dia_ref[...]], axis=0)
    outs[:, 0:512] = dot(cells_ref[...], pieces[:, 0:512])
    g32 = dot(pst_ref[...], pieces[:, 512:1024])
    gb = g32.astype(BF16)
    gain = gain_ref[0:1, :]
    n = n_ref[...]
    do = dot_nt(gb, wproj_ref[0]).astype(BF16)
    for g in range(4):
        q4 = stack_heads(qkv_ref[:, 128 * g : 128 * (g + 1)], masks)
        kg = pad_keys(qkv_ref[:, 512 + 128 * g : 512 + 128 * (g + 1)])
        vg = pad_keys(qkv_ref[:, 1024 + 128 * g : 1024 + 128 * (g + 1)])
        p4b = p_ref[576 * g : 576 * (g + 1), :]
        group_back(g, q4, kg, vg, p4b.astype(F32), p4b, do, masks, dqkv_ref, ds0_ref, ds1_ref)
    df = finish_back(dqkv_ref, wqkv_ref, n, rstd_ref[...], gain, g32, dgain_ref)
    outs[:, 512:1024] = dot(pxt_ref[...], df.astype(BF16))
    for k in range(72):
        out_ref[k] = outs[2 * k : 2 * k + 2, 0:512].astype(BF16)
        gin_ref[k] = outs[2 * k : 2 * k + 2, 512:1024].astype(BF16)
    h = (n * gain).astype(BF16)
    weight_terms(idx_ref, h, o_ref[...], dqkv_ref[...], gb, keep_ref, send_ref)


def scatter_kernel(
    idx_ref, rel_ref, d00_ref, d01_ref, gain0_ref, d10_ref, d11_ref, gain1_ref, after_ref,
    keep_ref, send_ref,
):
    iota = lax.broadcasted_iota(jnp.int32, (128, 256), 0)

    def body(i, acc):
        ids = rel_ref[pl.ds(i, 1), :]
        low, high = ids & 127, ids >> 7
        hot = jnp.where(iota == low, 1.0, 0.0).astype(BF16)
        lhs = []
        for d0_ref, d1_ref in ((d00_ref, d01_ref), (d10_ref, d11_ref)):
            d = jnp.concatenate(
                [d0_ref[pl.ds(i, 16, stride=144), :], d1_ref[pl.ds(i, 16, stride=144), :]], axis=1
            )
            lhs += [jnp.where(high == k, d, 0.0) for k in range(6)]
        return acc + dot_nt(jnp.concatenate(lhs, axis=0).astype(BF16), hot)

    acc = lax.fori_loop(0, 144, body, jnp.zeros((192, 128), F32), unroll=8)
    first = lax.broadcasted_iota(jnp.int32, (8, 256), 0) == 0
    for b, dgain_ref in enumerate((gain0_ref, gain1_ref)):
        table = jnp.concatenate([acc[96 * b + 16 * k : 96 * b + 16 * k + 16] for k in range(6)], axis=1)
        halves = []
        for c in range(2):
            gain = jnp.where(first, dgain_ref[:, 256 * c : 256 * (c + 1)], 0.0)
            halves.append(jnp.concatenate([table[8 * c : 8 * (c + 1)], gain], axis=1))
        keep, send = pick(idx_ref[0], halves[0], halves[1])
        keep_ref[8 * b : 8 * b + 8, :] = keep
        send_ref[8 * b : 8 * b + 8, :] = send


CUTS = ((0, 384), (384, 768), (768, 1024))


def pick(flag, low, high):
    mine = flag == 0
    return jnp.where(mine, low, high), jnp.where(mine, high, low)


def core_kernel(
    idx_ref, k0_ref, r0_ref, k1_ref, r1_ref, ka_ref, sa_ref, kb_ref, sb_ref, kc_ref, sc_ref
):
    x0, z0, yl = idx_ref[2], idx_ref[3], idx_ref[1]
    for b, (k_ref, r_ref) in enumerate(((k0_ref, r0_ref), (k1_ref, r1_ref))):

        def total(r0, r1, c0, c1):
            return k_ref[r0:r1, c0:c1].astype(F32) + r_ref[r0:r1, c0:c1].astype(F32)

        for s in range(2):
            a0 = 1024 * s
            keep, send = pick(x0, total(0, 128, a0, a0 + 384), total(128, 256, a0, a0 + 384))
            to = 768 * b + 384 * s
            ka_ref[:, to : to + 384] = keep.astype(BF16)
            sa_ref[:, to : to + 384] = send.astype(BF16)
            to = 512 * b + 256 * s
            for h in range(2):
                r = 128 * h
                keep, send = pick(
                    z0,
                    total(r, r + 64, a0 + 768, a0 + 1024),
                    total(r + 64, r + 128, a0 + 768, a0 + 1024),
                )
                kc_ref[64 * h : 64 * h + 64, to : to + 256] = keep.astype(BF16)
                sc_ref[64 * h : 64 * h + 64, to : to + 256] = send.astype(BF16)
        keep, send = pick(yl, total(0, 256, 384, 768), total(0, 256, 1408, 1792))
        kb_ref[:, 384 * b : 384 * (b + 1)] = keep.astype(BF16)
        sb_ref[:, 384 * b : 384 * (b + 1)] = send.astype(BF16)


def step_two_kernel(
    idx_ref, ka_ref, ra_ref, kb_ref, rb_ref, kc_ref, rc_ref, t_ref, u_ref,
    nka_ref, nsa_ref, nkb_ref, nsb_ref, nkc_ref, nsc_ref, tk_ref,
):
    x0, z0, yl = idx_ref[2], idx_ref[3], idx_ref[1]
    a = ka_ref[...].astype(F32) + ra_ref[...].astype(F32)
    for b in range(2):
        keep, send = pick(yl, a[:, 768 * b : 768 * b + 384], a[:, 768 * b + 384 : 768 * b + 768])
        nka_ref[:, 384 * b : 384 * (b + 1)] = keep.astype(BF16)
        nsa_ref[:, 384 * b : 384 * (b + 1)] = send.astype(BF16)
    m = kb_ref[...].astype(F32) + rb_ref[...].astype(F32)
    for h in range(2):
        keep, send = pick(z0, m[128 * h : 128 * h + 64], m[128 * h + 64 : 128 * h + 128])
        nkb_ref[64 * h : 64 * h + 64, :] = keep.astype(BF16)
        nsb_ref[64 * h : 64 * h + 64, :] = send.astype(BF16)
    t = t_ref[...] + u_ref[...]
    t0, t1 = t[0:8], t[8:16]
    gains = jnp.concatenate([t0[:, 768:1024], t1[:, 768:1024], jnp.zeros((8, 256), F32)], axis=1)
    table = jnp.concatenate([t0[:, 0:768], t1[:, 0:768], gains, jnp.zeros((8, 768), F32)], axis=0)
    table = table.astype(BF16)
    tk_ref[...] = table
    nsb_ref[128:160, :] = table
    c = kc_ref[...].astype(F32) + rc_ref[...].astype(F32)
    keep, send = pick(x0, c[0:64], c[64:128])
    nkc_ref[...] = keep.astype(BF16)
    nsc_ref[...] = send.astype(BF16)


def step_three_kernel(
    idx_ref, ka_ref, ra_ref, kb_ref, rb_ref, kc_ref, rc_ref, tk_ref,
    nka_ref, nsa_ref, nkb_ref, nsb_ref, nkc_ref, nsc_ref, ntk_ref,
):
    x0, z0, yl = idx_ref[2], idx_ref[3], idx_ref[1]
    a = ka_ref[...].astype(F32) + ra_ref[...].astype(F32)
    keep, send = pick(z0, a[0:64], a[64:128])
    nka_ref[...] = keep.astype(BF16)
    nsa_ref[...] = send.astype(BF16)
    m = kb_ref[...].astype(F32) + rb_ref[0:128, :].astype(F32)
    keep, send = pick(x0, m[0:64], m[64:128])
    nkb_ref[...] = keep.astype(BF16)
    nsb_ref[0:64, :] = send.astype(BF16)
    table = (tk_ref[...].astype(F32) + rb_ref[128:160, :].astype(F32)).astype(BF16)
    ntk_ref[...] = table
    nsb_ref[64:96, :] = table
    c = kc_ref[...].astype(F32) + rc_ref[...].astype(F32)
    for b in range(2):
        keep, send = pick(yl, c[:, 512 * b : 512 * b + 256], c[:, 512 * b + 256 : 512 * b + 512])
        nkc_ref[:, 256 * b : 256 * (b + 1)] = keep.astype(BF16)
        nsc_ref[:, 256 * b : 256 * (b + 1)] = send.astype(BF16)


def spread_kernel(
    idx_ref, ka_ref, ra_ref, kb_ref, rb_ref, kc_ref, rc_ref, tk_ref, *refs
):
    outs, scr = refs[0:4], refs[4]
    a = ka_ref[...].astype(F32) + ra_ref[...].astype(F32)
    m = kb_ref[...].astype(F32) + rb_ref[0:64, :].astype(F32)
    c = kc_ref[...].astype(F32) + rc_ref[...].astype(F32)
    table = tk_ref[...].astype(F32) + rb_ref[64:96, :].astype(F32)
    gains = jnp.concatenate([table[16:24, 0:256], table[16:24, 256:512]], axis=0)
    table = jnp.concatenate([table[0:16], gains], axis=1)
    table = jnp.concatenate([table[0:8], table[8:16]], axis=1).astype(BF16)
    full = []
    for b in range(2):
        cols = slice(384 * b, 384 * (b + 1))
        full += [a[:, cols], m[:, cols], c[:, 256 * b : 256 * (b + 1)]]
    full = jnp.concatenate(full, axis=1).astype(BF16)
    for k in range(4):
        scr[k] = full[16 * k : 16 * k + 16]
    for f in range(4):
        outs[f][0:16, :] = scr[idx_ref[4] ^ f]
        outs[f][16:24, :] = table


def plane_kernel(idx_ref, own_ref, g1_ref, g2_ref, g3_ref, *refs):
    outs, tabs, scr = refs[0:4], refs[4], refs[5]
    got = (own_ref, g1_ref, g2_ref, g3_ref)
    total = got[0][0:16, :].astype(F32)
    for g in got[1:]:
        total = total + g[0:16, :].astype(F32)
    for f in range(4):
        tabs[idx_ref[4] ^ f] = got[f][16:24, :].astype(F32)
    table = tabs[0] + tabs[1] + tabs[2] + tabs[3]
    table = jnp.concatenate([table[:, 0:1024], table[:, 1024:2048]], axis=0)
    for k in range(4):
        rows = total[4 * k : 4 * k + 4]
        rows = jnp.concatenate([rows[:, 0:1024], rows[:, 1024:2048], table], axis=0)
        scr[k] = rows.astype(BF16)
    for f in range(4):
        outs[f][...] = scr[idx_ref[5] ^ f]


def ring_kernel(idx_ref, own_ref, g1_ref, g2_ref, g3_ref, out_ref, tab_ref, scr):
    for f, g in enumerate((own_ref, g1_ref, g2_ref, g3_ref)):
        scr[idx_ref[5] ^ f] = g[...].astype(F32)
    total = scr[0] + scr[1] + scr[2] + scr[3]
    out_ref[...] = total.astype(BF16)
    tab_ref[...] = total[8:24].astype(BF16)


def last_kernel(
    factor, idx_ref, own_ref, lat_ref, core_ref, dia_ref, gain_ref, qkv_ref, proj_ref, bias_ref
):
    core, yl = idx_ref[0], idx_ref[1]
    own = own_ref[...].astype(F32) * factor
    got = lat_ref[...].astype(F32) * factor
    low, high = pick(yl, own[0:8], got[0:8])
    for b in range(2):
        qkv_ref[b, :, 0:1024] = low[4 * b : 4 * b + 4]
        qkv_ref[b, :, 1024:1536] = high[4 * b : 4 * b + 4, 0:512]
        proj_ref[b, :, :] = high[4 * b : 4 * b + 4, 512:1024]
    near = pick(yl, own[8:24], got[8:24])
    far = pick(yl, core_ref[...].astype(F32) * factor, dia_ref[...].astype(F32) * factor)
    tabs = [pick(core, near[w], far[w]) for w in range(2)]
    for c in range(2):
        for w in range(2):
            for b in range(2):
                bias_ref[b, w, 8 * c : 8 * (c + 1), :] = tabs[w][c][8 * b : 8 * b + 8, 0:NREL]
        for b in range(2):
            gain_ref[b : b + 1, 256 * c : 256 * (c + 1)] = (
                tabs[0][c][8 * b : 8 * b + 1, 768:1024] + tabs[1][c][8 * b : 8 * b + 1, 768:1024]
            )


def _whole(shape):
    return pl.BlockSpec(shape, lambda *_: (0,) * len(shape))


SMEM = pl.BlockSpec(memory_space=pltpu.SMEM)


ANY = pl.BlockSpec(memory_space=pl.ANY)


def call(body, outs, *args, specs=None, scratch=(), cost=None):
    specs = dict(specs or {})
    if args[0].dtype == jnp.int32 and args[0].ndim == 1:
        specs[0] = SMEM
    return pl.pallas_call(
        body,
        grid=(1,),
        in_specs=[specs.get(i, _whole(a.shape)) for i, a in enumerate(args)],
        out_specs=[_whole(s) for s, _ in outs],
        out_shape=[jax.ShapeDtypeStruct(s, t) for s, t in outs],
        scratch_shapes=[pltpu.VMEM(s, t) for s, t in scratch],
        compiler_params=pltpu.CompilerParams(vmem_limit_bytes=VMEM),
        cost_estimate=cost,
    )(*args)


def flip(value, *axes):
    mask = sum(1 << (7 - AXES.index(a)) for a in axes)
    return lax.ppermute(value, AXES, [(s, s ^ mask) for s in range(256)])


def lon_step(value, offset, across):
    pairs = [(s, ((s // 2 + offset) % 128) * 2 + (s % 2 ^ across)) for s in range(256)]
    return lax.ppermute(value, AXES, pairs)


def halo(pieces, offset):
    own, lon, lat, dia = pieces
    return (
        own,
        lon_step(lon, offset, 0),
        flip(lat, "yl"),
        lon_step(dia, offset, 1),
    )


def on_device(inputs, grad_out, gains, qkv_weight, proj_weight, bias_table, rel_ids, groups):
    T = {k: jnp.asarray(v) for k, v in TABLES.items()}
    at = {a: lax.axis_index(a) for a in AXES}
    idx = jnp.stack(
        [
            at["c"],
            at["yl"],
            at["x0"] ^ at["x1"],
            at["z0"],
            2 * at["x1"] + at["yh"],
            2 * at["z2"] + at["z1"],
        ]
    ).astype(jnp.int32)
    x_cells, go_cells = [v.transpose(0, 2, 3, 1, 4).reshape(72, 2, D) for v in (inputs, grad_out)]

    def block(b, shape):
        return pl.BlockSpec((1,) + shape, lambda *_: (b,) + (0,) * len(shape))

    def weights(b, first):
        return {
            first: block(b, (D, 3 * D)),
            first + 1: block(b, (D, D)),
            first + 2: block(b, (2, HEADS, NREL)),
        }

    tables = [((8, 768), jnp.int32), ((HEADS, 128), F32), ((HEADS, 128), F32)]
    piece = ((48, 1152), BF16)
    own, lon, lat, dia, n0, rstd0, qkv0, p0, o0, relp = call(
        first_kernel,
        [piece] * 4
        + [
            ((144, D), F32),
            ((144, 1), F32),
            ((144, 3 * D), BF16),
            ((2304, 256), BF16),
            ((144, D), BF16),
            ((144, 256), jnp.int32),
        ],
        idx, x_cells, go_cells, groups.transpose(1, 0, 2), gains, qkv_weight, proj_weight, bias_table, rel_ids,
        T["px"], T["ps"], T["pm"], T["rows"], T["cols"],
        specs=weights(0, 5),
        scratch=[((144, 1024), F32), ((12, 12), F32), ((144, 1152), BF16), ((2304, 256), F32)] + tables,
    )
    pieces = halo((own, lon, lat, dia), -1)
    (bias1,) = call(
        bias_kernel,
        [((2304, 256), F32)],
        idx, bias_table, relp,
        specs={1: block(1, (2, HEADS, NREL))},
        scratch=tables,
    )
    back = ((48, 1024), BF16)
    ds_shape = ((2304, 128), F32)
    own, lon, lat, dia, h1, o1, dqkv1, g1, dgain1, ds10, ds11 = call(
        second_kernel,
        [back] * 4
        + [
            ((144, D), BF16),
            ((144, D), BF16),
            ((144, 3 * D), BF16),
            ((144, D), BF16),
            ((1, D), F32),
            ds_shape,
            ds_shape,
        ],
        idx, *pieces, gains, qkv_weight, proj_weight, bias1, T["pf"], T["pft"], T["flags"],
        specs={6: block(1, (D, 3 * D)), 7: block(1, (D, D))},
        scratch=[((144, 3 * D), BF16), ((144, 2 * D), BF16)],
    )
    pieces = halo((own, lon, lat, dia), 1)
    wshape = ((256, 4 * D), BF16)
    keep1, send1 = call(weights_kernel, [wshape] * 2, idx, h1, o1, dqkv1, g1)
    recv1 = flip(send1, "c")
    cells = ((72, 2, D), BF16)
    outputs, grad_inputs, dgain0, ds00, ds01, keep0, send0 = call(
        third_kernel,
        [cells, cells, ((1, D), F32), ds_shape, ds_shape, wshape, wshape],
        idx, *pieces, gains, qkv_weight, proj_weight, n0, rstd0, qkv0, p0, o0,
        T["pst"], T["cells"], T["pxt"], keep1,
        specs={6: block(0, (D, 3 * D)), 7: block(0, (D, D)), 16: ANY},
        scratch=[((144, 3 * D), BF16), ((144, 2 * D), F32)],
    )
    outputs, grad_inputs = [
        v.reshape(1, 6, 12, 2, D).transpose(0, 3, 1, 2, 4) for v in (outputs, grad_inputs)
    ]
    recv0 = flip(send0, "c")

    def pairs(*shapes):
        return [(s, BF16) for shape in shapes for s in shape]

    ka, sa, kb, sb, kc, sc = call(
        core_kernel,
        pairs([(128, 1536)] * 2, [(256, 768)] * 2, [(128, 1024)] * 2),
        idx, keep0, recv0, keep1, recv1,
    )
    ra, rb, rc = flip(sa, "x0"), flip(sb, "yl"), flip(sc, "z0")
    tshape = ((16, 1024), F32)
    tkeep, tsend = call(
        scatter_kernel,
        [tshape] * 2,
        idx, relp, ds00, ds01, dgain0, ds10, ds11, dgain1, ka,
        specs={8: ANY},
    )
    trecv = flip(tsend, "c")
    ka, sa, kb, sb, kc, sc, tk = call(
        step_two_kernel,
        pairs([(128, 768)] * 2, [(128, 768), (160, 768)], [(64, 1024)] * 2, [(32, 768)]),
        idx, ka, ra, kb, rb, kc, rc, tkeep, trecv,
    )
    ra, rb, rc = flip(sa, "yl"), flip(sb, "z0"), flip(sc, "x0")
    ka, sa, kb, sb, kc, sc, tk = call(
        step_three_kernel,
        pairs([(64, 768)] * 2, [(64, 768), (96, 768)], [(64, 512)] * 2, [(32, 768)]),
        idx, ka, ra, kb, rb, kc, rc, tk,
    )
    ra, rb, rc = flip(sa, "z0"), flip(sb, "x0"), flip(sc, "yl")
    parts = call(
        spread_kernel,
        [((24, 2048), BF16)] * 4,
        idx, ka, ra, kb, rb, kc, rc, tk,
        scratch=[((4, 16, 2048), BF16)],
    )
    parts = call(
        plane_kernel,
        [((24, 1024), BF16)] * 4,
        idx, parts[0], flip(parts[1], "yh"), flip(parts[2], "x1", "x0"),
        flip(parts[3], "x1", "x0", "yh"),
        scratch=[((4, 8, 2048), F32), ((4, 24, 1024), BF16)],
    )
    own, tab = call(
        ring_kernel,
        [((24, 1024), BF16), ((16, 1024), BF16)],
        idx, parts[0], flip(parts[1], "z1"), flip(parts[2], "z2"), flip(parts[3], "z2", "z1"),
        scratch=[((4, 24, 1024), F32)],
    )
    from_core = flip(tab, "c")
    from_dia = flip(tab, "c", "yl")
    from_lat = flip(own, "yl")
    factor = 36864 ** (-0.5)
    grad_gains, grad_qkv, grad_proj, grad_bias = call(
        functools.partial(last_kernel, factor),
        [
            ((2, D), F32),
            ((2, 4, 3 * D), F32),
            ((2, 4, D), F32),
            ((2, 2, HEADS, NREL), F32),
        ],
        idx, own, from_lat, from_core, from_dia,
    )
    return (outputs, grad_inputs, grad_gains, grad_qkv, grad_proj, grad_bias)


def solution(mesh):
    fine = Mesh(mesh.devices.reshape((2,) * 8), AXES)
    lon = AXES[:7]
    field = P(None, None, "yl", lon, None)
    rows = P(None, lon, None)
    return jax.shard_map(
        on_device,
        mesh=fine,
        in_specs=(field, field, P(), P(), P(), P(), P(), P(None, "yl", lon)),
        out_specs=(field, field, P(), rows, rows, P()),
        check_vma=False,
    )
```

```python
import functools

import jax
import jax.numpy as jnp
import numpy as np
from jax import lax
from jax.experimental import pallas as pl
from jax.experimental.pallas import tpu as pltpu
from jax.sharding import Mesh, PartitionSpec as P

F32 = jnp.float32
BF16 = jnp.bfloat16
EPSILON = 1e-05
NEGATIVE = -1e30
D = 512
HEADS = 16
NREL = 759
SCALE = 32 ** (-0.5)
AXES = ("yh", "x1", "x0", "z2", "z1", "z0", "c", "yl")
VMEM = 24 << 20

QUADS = ((1, 1), (1, 0), (0, 1), (0, 0))


def _token(rh, ch, l, r, c):
    return (rh * 2 + ch) * 36 + l * 18 + r * 6 + c


def _tables():
    px = np.zeros((144, 144), np.float32)
    ps = np.zeros((192, 144), np.float32)
    pf = np.zeros((144, 192), np.float32)
    pm = np.zeros((144, 144), np.float32)
    rows = np.zeros((144, 12), np.float32)
    cols = np.zeros((144, 12), np.float32)
    flags = np.zeros((144, 2), np.float32)
    for l in range(2):
        for row in range(6):
            for col in range(12):
                rh, r, ch, c = row // 3, row % 3, col // 6, col % 6
                t = _token(rh, ch, l, r, c)
                px[t, (row * 12 + col) * 2 + l] = 1
                pm[t, l * 72 + row * 12 + col] = 1
                rows[t, row * 2 + l] = 1
                cols[t, col] = 1
                flags[t] = (l, rh)
                k = QUADS.index((rh, ch))
                ps[48 * k + (1 - l) * 18 + r * 6 + c, t] = 1
    for k in range(4):
        for i in range(36):
            pf[36 * k + i, 48 * k + i] = 1
    bf = jnp.bfloat16
    return {
        "px": px.astype(bf),
        "ps": ps.astype(bf),
        "pf": pf.astype(bf),
        "pft": pf.T.copy().astype(bf),
        "pst": ps.T.copy().astype(bf),
        "cells": (px.T @ ps.T).astype(bf),
        "pxt": px.T.copy().astype(bf),
        "pm": pm.astype(bf),
        "rows": rows.astype(bf),
        "cols": cols,
        "flags": flags,
    }


TABLES = _tables()


def dot(a, b):
    return lax.dot_general(a, b, (((1,), (0,)), ((), ())), preferred_element_type=F32)


def dot_nt(a, b):
    return lax.dot_general(a, b, (((1,), (1,)), ((), ())), preferred_element_type=F32)


def dot_tn(a, b):
    return lax.dot_general(a, b, (((0,), (0,)), ((), ())), preferred_element_type=F32)


def lane_masks():
    lane = lax.broadcasted_iota(jnp.int32, (1, 128), 1) >> 5
    return [jnp.where(lane == k, 1.0, 0.0).astype(F32) for k in range(4)]


def stack_heads(group, masks):
    return jnp.concatenate([group * m.astype(BF16) for m in masks], axis=0)


def fold_heads(stacked, masks):
    total = stacked[0:144] * masks[0]
    for k in range(1, 4):
        total = total + stacked[144 * k : 144 * (k + 1)] * masks[k]
    return total


def pad_keys(group):
    return jnp.concatenate([group, jnp.zeros((112, 128), BF16)], axis=0)


def normalize(x):
    center = x - jnp.mean(x, axis=-1, keepdims=True)
    rstd = lax.rsqrt(jnp.mean(center * center, axis=-1, keepdims=True) + EPSILON)
    return center * rstd, rstd


def pack_table(tab, words, scales, offsets):
    low = jnp.min(tab, axis=-1, keepdims=True)
    scale = jnp.maximum(jnp.max(tab, axis=-1, keepdims=True) - low, 1e-20) * (1.0 / 65535.0)
    q = jnp.clip(jnp.floor((tab - low) / scale + 0.5), 0.0, 65535.0).astype(jnp.int32)
    high = jnp.concatenate([q[4 * g : 4 * g + 2] for g in range(4)], axis=0)
    rest = jnp.concatenate([q[4 * g + 2 : 4 * g + 4] for g in range(4)], axis=0)
    words[...] = jnp.zeros((8, 768), jnp.int32)
    words[:, 0:NREL] = ((high - 32768) << 16) + rest
    signed = lax.broadcasted_iota(jnp.int32, (HEADS, 1), 0) & 3
    offset = low + jnp.where(signed < 2, 32768.0, 0.0) * scale
    scales[...] = jnp.broadcast_to(scale, (HEADS, 128))
    offsets[...] = jnp.broadcast_to(offset, (HEADS, 128))


def lookup(row, ids):
    acc = None
    for k in range(6):
        part = jnp.broadcast_to(row[:, 128 * k : 128 * (k + 1)], ids.shape)
        got = jnp.take_along_axis(part, ids & 127, axis=1)
        acc = got if k == 0 else jnp.where((ids >> 7) == k, got, acc)
    return acc


def side_by_side(tail):
    total = tail[0:24]
    for k in range(1, 6):
        total = total + pltpu.roll(tail[24 * k : 24 * (k + 1)], 16 * k, 1)
    return total


def bias_pair(m, words, scales, offsets, ids, tails):
    row = words[m : m + 1, :]
    main = lookup(row, ids)
    tail = lookup(row, tails)
    parts = [tail] + [pltpu.roll(tail, 128 - 16 * k, 1) for k in range(1, 6)]
    tail = jnp.concatenate(parts, axis=0)
    lane = lax.broadcasted_iota(jnp.int32, (144, 128), 1)
    head = 4 * (m // 2) + m % 2
    out = []
    for h, take in ((head, lambda w: w >> 16), (head + 2, lambda w: w & 65535)):
        scale, offset = scales[h : h + 1, :], offsets[h : h + 1, :]
        a = take(main).astype(F32) * scale + offset
        b = jnp.where(lane < 16, take(tail).astype(F32) * scale + offset, NEGATIVE)
        out.append(jnp.concatenate([a, b], axis=1))
    return out


def frame_ids(rel, pm, main_ref, tail_ref):
    parts = []
    for part in (rel >> 5, rel & 31):
        half = dot(pm, part.astype(F32).astype(BF16)).astype(BF16)
        parts.append(dot_nt(half, pm).astype(jnp.int32))
    ids = parts[0] * 32 + parts[1]
    main_ref[...] = ids[:, 0:128]
    tail = jnp.concatenate([ids[:, 128:144], jnp.zeros((144, 112), jnp.int32)], axis=1)
    tail_ref[...] = side_by_side(tail)


def fill_bias(table, main_ref, tail_ref, words, scales, offsets, store):
    pack_table(table, words, scales, offsets)
    ids, tails = main_ref[...], tail_ref[...]
    for m in range(8):
        head = 4 * (m // 2) + m % 2
        for h, b in zip((head, head + 2), bias_pair(m, words, scales, offsets, ids, tails)):
            store[144 * h : 144 * (h + 1), :] = b


def group_probs(qkv_ref, g, masks, bias_ref, allowed):
    qg = qkv_ref[:, 128 * g : 128 * (g + 1)]
    kg = pad_keys(qkv_ref[:, 512 + 128 * g : 512 + 128 * (g + 1)])
    q4 = stack_heads(qg, masks)
    s4 = dot_nt(q4, kg) * SCALE
    out = []
    for k in range(4):
        at = 144 * (4 * g + k)
        s = s4[144 * k : 144 * (k + 1)] + bias_ref[at : at + 144, :]
        if allowed is not None:
            s = jnp.where(allowed, s, NEGATIVE)
        e = jnp.exp(s - jnp.max(s, axis=-1, keepdims=True))
        out.append(e * (1.0 / jnp.sum(e, axis=-1, keepdims=True)))
    return q4, kg, jnp.concatenate(out, axis=0)


def group_back(g, q4, kg, vg, p4, p4b, do, masks, dqkv_ref, ds0_ref, ds1_ref):
    do4 = stack_heads(do[:, 128 * g : 128 * (g + 1)], masks)
    dp4 = dot_nt(do4, vg)
    dqkv_ref[:, 1024 + 128 * g : 1024 + 128 * (g + 1)] = dot_tn(p4b, do4)[0:144].astype(BF16)
    ds4 = p4 * (dp4 - jnp.sum(dp4 * p4, axis=-1, keepdims=True))
    ds0_ref[576 * g : 576 * (g + 1), :] = ds4[:, 0:128]
    for k in range(4):
        at = 24 * (4 * g + k)
        ds1_ref[at : at + 24, :] = side_by_side(ds4[144 * k : 144 * (k + 1), 128:256])
    ds4b = ds4.astype(BF16)
    dq = fold_heads(dot(ds4b, kg), masks) * SCALE
    dqkv_ref[:, 128 * g : 128 * (g + 1)] = dq.astype(BF16)
    dk = dot_tn(ds4b, q4)[0:144] * SCALE
    dqkv_ref[:, 512 + 128 * g : 512 + 128 * (g + 1)] = dk.astype(BF16)


def finish_back(dqkv_ref, wqkv_ref, n, rstd, gain, g32, dgain_ref):
    dh = dot_nt(dqkv_ref[...], wqkv_ref[0])
    dgain_ref[...] = jnp.sum(dh * n, axis=0, keepdims=True)
    dn = dh * gain
    return (
        rstd
        * (
            dn
            - jnp.mean(dn, axis=-1, keepdims=True)
            - n * jnp.mean(dn * n, axis=-1, keepdims=True)
        )
        + g32
    )


def weight_terms(idx_ref, h, o, dqkv, g, keep_ref, send_ref):
    core = idx_ref[0]
    p = lax.broadcasted_iota(jnp.int32, (256, 512), 0)
    row = lax.broadcasted_iota(jnp.int32, (256, 512), 1)
    bit = lambda k: (p >> k) & 1
    hz, h2, h3 = bit(6), bit(3), bit(2)
    z1 = h3 ^ (hz & h2)
    place = (
        (8, bit(4)),
        (7, bit(5)),
        (6, bit(7) ^ bit(5)),
        (5, h2 ^ (hz & (h2 ^ h3))),
        (4, z1),
        (3, z1 ^ hz),
    )
    base = p & 3
    for to, value in place:
        base = base + (value << to)
    for which, ref in ((core, keep_ref), (1 - core, send_ref)):
        pick = jnp.where(row == base + which * 4, 1.0, 0.0).astype(BF16)
        ht = dot_nt(pick, h).astype(BF16)
        ot = dot_nt(pick, o).astype(BF16)
        ref[:, 0:1536] = dot(ht, dqkv).astype(BF16)
        ref[:, 1536:2048] = dot(ot, g).astype(BF16)


def first_kernel(
    x_hbm, go_hbm, grp_hbm, gain_hbm, wqkv_hbm, wproj_hbm, tab_hbm, rel_hbm, const_hbm,
    own_ref, lon_ref, lat_ref, dia_ref, n_ref, rstd_ref, qkv_ref, p_ref, o_ref,
    cells, gs, pay, bias, main_ref, tail_ref, words, scales, offsets,
    x_ref, go_ref, grp_ref, gain_ref, wqkv_ref, wproj_ref, tab_ref, rel_ref, const_ref, sems,
):
    sources = [
        (rel_hbm, rel_ref),
        (tab_hbm.at[0, lax.axis_index("yl")], tab_ref),
        (const_hbm, const_ref),
        (x_hbm, x_ref),
        (go_hbm, go_ref),
        (grp_hbm, grp_ref),
        (gain_hbm, gain_ref),
        (wqkv_hbm.at[0], wqkv_ref),
        (wproj_hbm.at[0], wproj_ref),
    ]
    copies = [pltpu.make_async_copy(a, b, sems.at[k]) for k, (a, b) in enumerate(sources)]
    for copy in copies:
        copy.start()
    for copy in copies[0:3]:
        copy.wait()
    px, ps, pm = const_ref[0, 0:144, 0:144], const_ref[1, :, 0:144], const_ref[2, 0:144, 0:144]
    rows, cols = const_ref[3, 0:144, 0:12], const_ref[4, 0:144, 0:12]

    frame_ids(rel_ref[...], pm, main_ref, tail_ref)
    fill_bias(tab_ref[...], main_ref, tail_ref, words, scales, offsets, bias)

    masks = lane_masks()
    for copy in copies[3:]:
        copy.wait()
    for k in range(72):
        cells[2 * k : 2 * k + 2, 0:512] = x_ref[k].astype(F32)
        cells[2 * k : 2 * k + 2, 512:1024] = go_ref[k].astype(F32)
    both = dot(px, cells[...].astype(BF16))
    x = both[:, 0:512]
    pay[:, 512:1024] = both[:, 512:1024].astype(BF16)
    for r in range(6):
        gs[2 * r : 2 * r + 2, :] = grp_ref[r].astype(F32)
    picked = dot(rows, gs[...].astype(BF16)) * cols.astype(F32)
    group = jnp.sum(picked, axis=-1, keepdims=True)
    pay[:, 1024:1152] = jnp.broadcast_to(group, (144, 128)).astype(BF16)

    n, rstd = normalize(x)
    n_ref[...] = n
    rstd_ref[...] = rstd
    h = (n * gain_ref[0:1, :]).astype(BF16)
    qkv_ref[...] = dot(h, wqkv_ref[...]).astype(BF16)
    for g in range(4):
        _, _, p4 = group_probs(qkv_ref, g, masks, bias, None)
        p4b = p4.astype(BF16)
        p_ref[576 * g : 576 * (g + 1), :] = p4b
        vg = pad_keys(qkv_ref[:, 1024 + 128 * g : 1024 + 128 * (g + 1)])
        o_ref[:, 128 * g : 128 * (g + 1)] = fold_heads(dot(p4b, vg), masks).astype(BF16)
    pay[:, 0:512] = (x + dot(o_ref[...], wproj_ref[...])).astype(BF16)
    out = dot(ps, pay[...]).astype(BF16)
    own_ref[...] = out[0:48]
    lon_ref[...] = out[48:96]
    lat_ref[...] = out[96:144]
    dia_ref[...] = out[144:192]


def bias_kernel(
    idx_ref, tab_ref, rel_ref, pm_ref, out_ref, main_ref, tail_ref, words, scales, offsets
):
    frame_ids(rel_ref[...], pm_ref[0:144, 0:144], main_ref, tail_ref)
    fill_bias(tab_ref[0, idx_ref[1]], main_ref, tail_ref, words, scales, offsets, out_ref)


def second_kernel(
    idx_ref, own_ref, lon_ref, lat_ref, dia_ref, gain_ref, wqkv_ref, wproj_ref, bias_ref,
    const_ref,
    oown_ref, olon_ref, olat_ref, odia_ref, h_ref, o_ref, dqkv_ref, g_ref, dgain_ref, ds0_ref, ds1_ref,
    qkv_ref, back,
):
    masks = lane_masks()
    flags = const_ref[2, 0:144, 0:2].astype(F32)
    frame = dot(
        const_ref[0, 0:144, 0:192], jnp.concatenate([own_ref[...], lon_ref[...], lat_ref[...], dia_ref[...]], axis=0)
    )
    x = frame[:, 0:512]
    g32 = frame[:, 512:1024]
    gb = g32.astype(BF16)
    g_ref[...] = gb
    lat = idx_ref[1].astype(F32)
    key = frame[:, 1024:1025] * 4.0 + flags[:, 1:2] * (2.0 * lat) + flags[:, 0:1]
    eye = lax.broadcasted_iota(jnp.int32, (144, 256), 0) == lax.broadcasted_iota(
        jnp.int32, (144, 256), 1
    )
    key_row = jnp.sum(jnp.where(eye, key, 0.0), axis=0, keepdims=True)
    allowed = key == key_row
    gain = gain_ref[1:2, :]

    n, rstd = normalize(x)
    h = (n * gain).astype(BF16)
    h_ref[...] = h
    qkv_ref[...] = dot(h, wqkv_ref[0]).astype(BF16)
    do = dot_nt(gb, wproj_ref[0]).astype(BF16)
    for g in range(4):
        q4, kg, p4 = group_probs(qkv_ref, g, masks, bias_ref, allowed)
        p4b = p4.astype(BF16)
        vg = pad_keys(qkv_ref[:, 1024 + 128 * g : 1024 + 128 * (g + 1)])
        o_ref[:, 128 * g : 128 * (g + 1)] = fold_heads(dot(p4b, vg), masks).astype(BF16)
        group_back(g, q4, kg, vg, p4, p4b, do, masks, dqkv_ref, ds0_ref, ds1_ref)
    back[:, 0:512] = (x + dot(o_ref[...], wproj_ref[0])).astype(BF16)
    df = finish_back(dqkv_ref, wqkv_ref, n, rstd, gain, g32, dgain_ref)
    back[:, 512:1024] = df.astype(BF16)
    out = dot(const_ref[1, :, 0:144], back[...]).astype(BF16)
    oown_ref[...] = out[0:48]
    olon_ref[...] = out[48:96]
    olat_ref[...] = out[96:144]
    odia_ref[...] = out[144:192]


def weights_kernel(idx_ref, h_ref, o_ref, dqkv_ref, g_ref, keep_ref, send_ref):
    weight_terms(idx_ref, h_ref[...], o_ref[...], dqkv_ref[...], g_ref[...], keep_ref, send_ref)


def third_kernel(
    idx_ref, own_ref, lon_ref, lat_ref, dia_ref, gain_ref, wproj_ref,
    n_ref, qkv_ref, p_ref, o_ref, const_ref, after_ref,
    g_ref, dqkv_ref, ds0_ref, ds1_ref, keep_ref, send_ref,
):
    masks = lane_masks()
    pieces = jnp.concatenate(
        [r[:, 512:1024] for r in (own_ref, lon_ref, lat_ref, dia_ref)], axis=0
    )
    gb = dot(const_ref[0:144, 0:192], pieces).astype(BF16)
    g_ref[...] = gb
    do = dot_nt(gb, wproj_ref[0]).astype(BF16)
    for g in range(4):
        q4 = stack_heads(qkv_ref[:, 128 * g : 128 * (g + 1)], masks)
        kg = pad_keys(qkv_ref[:, 512 + 128 * g : 512 + 128 * (g + 1)])
        vg = pad_keys(qkv_ref[:, 1024 + 128 * g : 1024 + 128 * (g + 1)])
        p4b = p_ref[576 * g : 576 * (g + 1), :]
        group_back(g, q4, kg, vg, p4b.astype(F32), p4b, do, masks, dqkv_ref, ds0_ref, ds1_ref)
    h = (n_ref[...] * gain_ref[0:1, :]).astype(BF16)
    weight_terms(idx_ref, h, o_ref[...], dqkv_ref[...], gb, keep_ref, send_ref)


def finish_kernel(
    own_ref, lon_ref, lat_ref, dia_ref, gain_ref, wqkv_ref, n_ref, rstd_ref, g_ref, dqkv_ref,
    const_ref, after_ref, out_ref, gin_ref, dgain_ref, outs,
):
    pieces = jnp.concatenate([r[:, 0:512] for r in (own_ref, lon_ref, lat_ref, dia_ref)], axis=0)
    outs[:, 0:512] = dot(const_ref[0, 0:144, 0:192], pieces)
    df = finish_back(
        dqkv_ref, wqkv_ref, n_ref[...], rstd_ref[...], gain_ref[0:1, :], g_ref[...].astype(F32), dgain_ref
    )
    outs[:, 512:1024] = dot(const_ref[1, 0:144, 0:144], df.astype(BF16))
    for k in range(72):
        out_ref[k] = outs[2 * k : 2 * k + 2, 0:512].astype(BF16)
        gin_ref[k] = outs[2 * k : 2 * k + 2, 512:1024].astype(BF16)


def scatter_kernel(
    idx_ref, main_ref, tail_ref, m0_ref, t0_ref, gain0_ref, m1_ref, t1_ref, gain1_ref, after_ref,
    keep_ref, send_ref,
):
    iota = lax.broadcasted_iota(jnp.int32, (128, 256), 0)

    def add(ids_ref, d_refs, stride, unroll):
        def body(i, acc):
            ids = jnp.concatenate([ids_ref[pl.ds(2 * i + k, 1), :] for k in range(2)], axis=1)
            low, high = ids & 127, ids >> 7
            hot = jnp.where(iota == low, 1.0, 0.0).astype(BF16)
            lhs = []
            for d_ref in d_refs:
                d = jnp.concatenate(
                    [d_ref[pl.ds(2 * i + k, 16, stride=stride), :] for k in range(2)], axis=1
                )
                lhs += [jnp.where(high == k, d, 0.0) for k in range(6)]
            return acc + dot_nt(jnp.concatenate(lhs, axis=0).astype(BF16), hot)

        return lambda acc: lax.fori_loop(0, stride // 2, body, acc, unroll=unroll)

    acc = add(main_ref, (m0_ref, m1_ref), 144, 8)(jnp.zeros((192, 128), F32))
    acc = add(tail_ref, (t0_ref, t1_ref), 24, 12)(acc)
    first = lax.broadcasted_iota(jnp.int32, (8, 256), 0) == 0
    for b, dgain_ref in enumerate((gain0_ref, gain1_ref)):
        table = [acc[96 * b + 16 * k : 96 * b + 16 * k + 16] for k in range(6)]
        table = jnp.concatenate(table, axis=1)
        halves = []
        for c in range(2):
            gain = jnp.where(first, dgain_ref[:, 256 * c : 256 * (c + 1)], 0.0)
            halves.append(jnp.concatenate([table[8 * c : 8 * (c + 1)], gain], axis=1))
        keep, send = pick(idx_ref[0], halves[0], halves[1])
        keep_ref[8 * b : 8 * b + 8, :] = keep
        send_ref[8 * b : 8 * b + 8, :] = send


CUTS = ((0, 384), (384, 768), (768, 1024))


def pick(flag, low, high):
    mine = flag == 0
    return jnp.where(mine, low, high), jnp.where(mine, high, low)


def core_kernel(
    idx_ref, k0_ref, r0_ref, k1_ref, r1_ref, ka_ref, sa_ref, kb_ref, sb_ref, kc_ref, sc_ref
):
    x0, z0, yl = idx_ref[2], idx_ref[3], idx_ref[1]
    for b, (k_ref, r_ref) in enumerate(((k0_ref, r0_ref), (k1_ref, r1_ref))):

        def total(r0, r1, c0, c1):
            return k_ref[r0:r1, c0:c1].astype(F32) + r_ref[r0:r1, c0:c1].astype(F32)

        for s in range(2):
            a0 = 1024 * s
            keep, send = pick(x0, total(0, 128, a0, a0 + 384), total(128, 256, a0, a0 + 384))
            to = 768 * b + 384 * s
            ka_ref[:, to : to + 384] = keep.astype(BF16)
            sa_ref[:, to : to + 384] = send.astype(BF16)
            to = 512 * b + 256 * s
            for h in range(2):
                r = 128 * h
                keep, send = pick(
                    z0,
                    total(r, r + 64, a0 + 768, a0 + 1024),
                    total(r + 64, r + 128, a0 + 768, a0 + 1024),
                )
                kc_ref[64 * h : 64 * h + 64, to : to + 256] = keep.astype(BF16)
                sc_ref[64 * h : 64 * h + 64, to : to + 256] = send.astype(BF16)
        keep, send = pick(yl, total(0, 256, 384, 768), total(0, 256, 1408, 1792))
        kb_ref[:, 384 * b : 384 * (b + 1)] = keep.astype(BF16)
        sb_ref[:, 384 * b : 384 * (b + 1)] = send.astype(BF16)


def step_two_kernel(
    idx_ref, ka_ref, ra_ref, kb_ref, rb_ref, kc_ref, rc_ref, t_ref, u_ref,
    nka_ref, nsa_ref, nkb_ref, nsb_ref, nkc_ref, nsc_ref, tk_ref,
):
    x0, z0, yl = idx_ref[2], idx_ref[3], idx_ref[1]
    a = ka_ref[...].astype(F32) + ra_ref[...].astype(F32)
    for b in range(2):
        keep, send = pick(yl, a[:, 768 * b : 768 * b + 384], a[:, 768 * b + 384 : 768 * b + 768])
        nka_ref[:, 384 * b : 384 * (b + 1)] = keep.astype(BF16)
        nsa_ref[:, 384 * b : 384 * (b + 1)] = send.astype(BF16)
    m = kb_ref[...].astype(F32) + rb_ref[...].astype(F32)
    for h in range(2):
        keep, send = pick(z0, m[128 * h : 128 * h + 64], m[128 * h + 64 : 128 * h + 128])
        nkb_ref[64 * h : 64 * h + 64, :] = keep.astype(BF16)
        nsb_ref[64 * h : 64 * h + 64, :] = send.astype(BF16)
    c = kc_ref[...].astype(F32) + rc_ref[...].astype(F32)
    keep, send = pick(x0, c[0:64], c[64:128])
    nkc_ref[...] = keep.astype(BF16)
    nsc_ref[0:64, :] = send.astype(BF16)
    table = (t_ref[...] + u_ref[...]).astype(BF16)
    tk_ref[...] = table
    nsc_ref[64:80, :] = table


def step_three_kernel(
    idx_ref, ka_ref, ra_ref, kb_ref, rb_ref, kc_ref, rc_ref, tk_ref,
    nka_ref, nsa_ref, nkb_ref, nsb_ref, nkc_ref, nsc_ref, ntk_ref,
):
    x0, z0, yl = idx_ref[2], idx_ref[3], idx_ref[1]
    a = ka_ref[...].astype(F32) + ra_ref[...].astype(F32)
    keep, send = pick(z0, a[0:64], a[64:128])
    nka_ref[...] = keep.astype(BF16)
    nsa_ref[0:64, :] = send.astype(BF16)
    t = tk_ref[...].astype(F32) + rc_ref[64:80, :].astype(F32)
    gains = jnp.concatenate([t[0:8, 768:1024], t[8:16, 768:1024], jnp.zeros((8, 256), F32)], axis=1)
    table = jnp.concatenate([t[:, 0:768], gains, jnp.zeros((8, 768), F32)], axis=0).astype(BF16)
    ntk_ref[...] = table
    nsa_ref[64:96, :] = table
    m = kb_ref[...].astype(F32) + rb_ref[...].astype(F32)
    keep, send = pick(x0, m[0:64], m[64:128])
    nkb_ref[...] = keep.astype(BF16)
    nsb_ref[...] = send.astype(BF16)
    c = kc_ref[...].astype(F32) + rc_ref[0:64, :].astype(F32)
    for b in range(2):
        keep, send = pick(yl, c[:, 512 * b : 512 * b + 256], c[:, 512 * b + 256 : 512 * b + 512])
        nkc_ref[:, 256 * b : 256 * (b + 1)] = keep.astype(BF16)
        nsc_ref[:, 256 * b : 256 * (b + 1)] = send.astype(BF16)


def spread_kernel(
    idx_ref, ka_ref, ra_ref, kb_ref, rb_ref, kc_ref, rc_ref, tk_ref, *refs
):
    outs, scr = refs[0:4], refs[4]
    a = ka_ref[...].astype(F32) + ra_ref[0:64, :].astype(F32)
    m = kb_ref[...].astype(F32) + rb_ref[...].astype(F32)
    c = kc_ref[...].astype(F32) + rc_ref[...].astype(F32)
    table = tk_ref[...].astype(F32) + ra_ref[64:96, :].astype(F32)
    gains = jnp.concatenate([table[16:24, 0:256], table[16:24, 256:512]], axis=0)
    table = jnp.concatenate([table[0:16], gains], axis=1)
    table = jnp.concatenate([table[0:8], table[8:16]], axis=1).astype(BF16)
    full = []
    for b in range(2):
        cols = slice(384 * b, 384 * (b + 1))
        full += [a[:, cols], m[:, cols], c[:, 256 * b : 256 * (b + 1)]]
    full = jnp.concatenate(full, axis=1).astype(BF16)
    for k in range(4):
        scr[k] = full[16 * k : 16 * k + 16]
    for f in range(4):
        outs[f][0:16, :] = scr[idx_ref[4] ^ f]
        outs[f][16:24, :] = table


def plane_kernel(idx_ref, own_ref, g1_ref, g2_ref, g3_ref, keep_ref, tk_ref, send_ref, tabs):
    got = (own_ref, g1_ref, g2_ref, g3_ref)
    total = got[0][0:16, :].astype(F32)
    for g in got[1:]:
        total = total + g[0:16, :].astype(F32)
    for f in range(4):
        tabs[idx_ref[4] ^ f] = got[f][16:24, :].astype(F32)
    table = tabs[0] + tabs[1] + tabs[2] + tabs[3]
    tk_ref[...] = table.astype(BF16)
    keep, send = pick(idx_ref[5], total[0:8], total[8:16])
    keep_ref[...] = keep
    send_ref[...] = jnp.concatenate([send, table], axis=0).astype(BF16)


def ring_kernel(idx_ref, keep_ref, tk_ref, got_ref, nkeep_ref, ntk_ref, send_ref):
    got = got_ref[...].astype(F32)
    total = keep_ref[...] + got[0:8]
    table = tk_ref[...].astype(F32) + got[8:16]
    table = jnp.concatenate([table[:, 0:1024], table[:, 1024:2048]], axis=0)
    keep, send = pick(idx_ref[6], total[0:4], total[4:8])
    nkeep_ref[...] = jnp.concatenate([keep[:, 0:1024], keep[:, 1024:2048]], axis=0)
    ntk_ref[...] = table.astype(BF16)
    send = [send[:, 0:1024], send[:, 1024:2048], table]
    send_ref[...] = jnp.concatenate(send, axis=0).astype(BF16)


def close_kernel(keep_ref, tk_ref, got_ref, out_ref, tab_ref):
    got = got_ref[...].astype(F32)
    table = tk_ref[...].astype(F32) + got[8:24]
    tab_ref[...] = table.astype(BF16)
    out_ref[...] = jnp.concatenate([keep_ref[...] + got[0:8], table], axis=0).astype(BF16)


def last_kernel(
    factor, idx_ref, own_ref, lat_ref, core_ref, dia_ref, gain_ref, qkv_ref, proj_ref, bias_ref
):
    core, yl = idx_ref[0], idx_ref[1]
    own = own_ref[...].astype(F32) * factor
    got = lat_ref[...].astype(F32) * factor
    low, high = pick(yl, own[0:8], got[0:8])
    for b in range(2):
        qkv_ref[b, :, 0:1024] = low[4 * b : 4 * b + 4]
        qkv_ref[b, :, 1024:1536] = high[4 * b : 4 * b + 4, 0:512]
        proj_ref[b, :, :] = high[4 * b : 4 * b + 4, 512:1024]
    near = pick(yl, own[8:24], got[8:24])
    far = pick(yl, core_ref[...].astype(F32) * factor, dia_ref[...].astype(F32) * factor)
    tabs = [pick(core, near[w], far[w]) for w in range(2)]
    for c in range(2):
        for w in range(2):
            for b in range(2):
                bias_ref[b, w, 8 * c : 8 * (c + 1), :] = tabs[w][c][8 * b : 8 * b + 8, 0:NREL]
        for b in range(2):
            gain_ref[b : b + 1, 256 * c : 256 * (c + 1)] = (
                tabs[0][c][8 * b : 8 * b + 1, 768:1024] + tabs[1][c][8 * b : 8 * b + 1, 768:1024]
            )


def _whole(shape):
    return pl.BlockSpec(shape, lambda *_: (0,) * len(shape))


SMEM = pl.BlockSpec(memory_space=pltpu.SMEM)


ANY = pl.BlockSpec(memory_space=pl.ANY)


HBM = pl.BlockSpec(memory_space=pltpu.HBM)


def call(body, us, outs, *args, specs=None, scratch=(), sems=0, vmem=VMEM):
    specs = dict(specs or {})
    if args[0].dtype == jnp.int32 and args[0].ndim == 1:
        specs[0] = SMEM
    scratch = [pltpu.VMEM(s, t) for s, t in scratch]
    if sems:
        scratch.append(pltpu.SemaphoreType.DMA((sems,)))
    return pl.pallas_call(
        body,
        grid=(1,),
        in_specs=[specs.get(i, _whole(a.shape)) for i, a in enumerate(args)],
        out_specs=[_whole(s) for s, _ in outs],
        out_shape=[jax.ShapeDtypeStruct(s, t) for s, t in outs],
        scratch_shapes=scratch,
        compiler_params=pltpu.CompilerParams(vmem_limit_bytes=vmem),
        cost_estimate=pl.CostEstimate(
            flops=int(us * 1e9), bytes_accessed=int(us * 3.6e6), transcendentals=0
        ),
    )(*args)


def flip(value, *axes):
    mask = sum(1 << (7 - AXES.index(a)) for a in axes)
    return lax.ppermute(value, AXES, [(s, s ^ mask) for s in range(256)])


def z_step(value, move):
    pairs = [(s, s & ~28 | move(s >> 2 & 7) << 2) for s in range(256)]
    return lax.ppermute(value, AXES, pairs)


def lon_step(value, offset, across):
    pairs = [(s, ((s // 2 + offset) % 128) * 2 + (s % 2 ^ across)) for s in range(256)]
    return lax.ppermute(value, AXES, pairs)


def halo(pieces, offset):
    own, lon, lat, dia = pieces
    return (
        own,
        lon_step(lon, offset, 0),
        flip(lat, "yl"),
        lon_step(dia, offset, 1),
    )


def on_device(inputs, grad_out, gains, qkv_weight, proj_weight, bias_table, rel_ids, groups):
    const = np.zeros((11, 192, 256), np.float32)
    names = ("px", "ps", "pm", "rows", "cols", "pf", "pft", "flags", "pst", "cells", "pxt")
    for k, name in enumerate(names):
        part = np.asarray(TABLES[name], np.float32)
        const[k, : part.shape[0], : part.shape[1]] = part
    const = const.astype(jnp.bfloat16)
    at = {a: lax.axis_index(a) for a in AXES}
    hz = at["z0"] ^ at["z1"]
    idx = jnp.stack(
        [
            at["c"],
            at["yl"],
            at["x0"] ^ at["x1"],
            hz,
            2 * at["x1"] + at["yh"],
            at["z2"] ^ (hz & at["z1"]),
            at["z1"] ^ (hz & (at["z1"] ^ at["z2"])),
        ]
    ).astype(jnp.int32)
    x_cells, go_cells = [v.transpose(0, 2, 3, 1, 4).reshape(72, 2, D) for v in (inputs, grad_out)]

    def block(b, shape):
        return pl.BlockSpec((1,) + shape, lambda *_: (b,) + (0,) * len(shape))

    def weights(b, first):
        return {
            first: block(b, (D, 3 * D)),
            first + 1: block(b, (D, D)),
            first + 2: block(b, (2, HEADS, NREL)),
        }

    id_shapes = [((144, 128), jnp.int32), ((24, 128), jnp.int32)]
    tables = [((8, 768), jnp.int32), ((HEADS, 128), F32), ((HEADS, 128), F32)]
    piece = ((48, 1152), BF16)
    own, lon, lat, dia, n0, rstd0, qkv0, p0, o0 = call(
        first_kernel,
        8,
        [piece] * 4
        + [
            ((144, D), F32),
            ((144, 1), F32),
            ((144, 3 * D), BF16),
            ((2304, 256), BF16),
            ((144, D), BF16),
        ],
        x_cells, go_cells, groups.transpose(1, 0, 2), gains, qkv_weight, proj_weight, bias_table, rel_ids,
        jnp.asarray(const[0:5]),
        specs={k: HBM for k in range(9)},
        scratch=[((144, 1024), F32), ((12, 12), F32), ((144, 1152), BF16), ((2304, 256), F32)]
        + id_shapes
        + tables
        + [
            ((72, 2, D), BF16),
            ((72, 2, D), BF16),
            ((6, 2, 12), jnp.int32),
            ((2, D), F32),
            ((D, 3 * D), BF16),
            ((D, D), BF16),
            ((HEADS, NREL), F32),
            ((144, 144), jnp.int32),
            ((5, 192, 256), BF16),
        ],
        sems=9,
        vmem=57 << 20,
    )
    pieces = halo((own, lon, lat, dia), -1)
    bias1, ids, tails = call(
        bias_kernel,
        4,
        [((2304, 256), F32)] + id_shapes,
        idx, bias_table, rel_ids, jnp.asarray(const[2]),
        specs={1: block(1, (2, HEADS, NREL))},
        scratch=tables,
    )
    back = ((48, 1024), BF16)
    ds_shapes = [((2304, 128), F32), ((384, 128), F32)]
    own, lon, lat, dia, h1, o1, dqkv1, g1, dgain1, ds10, ds11 = call(
        second_kernel,
        6,
        [back] * 4
        + [
            ((144, D), BF16),
            ((144, D), BF16),
            ((144, 3 * D), BF16),
            ((144, D), BF16),
            ((1, D), F32),
        ]
        + ds_shapes,
        idx, *pieces, gains, qkv_weight, proj_weight, bias1, jnp.asarray(const[5:8]),
        specs={6: block(1, (D, 3 * D)), 7: block(1, (D, D))},
        scratch=[((144, 3 * D), BF16), ((144, 2 * D), BF16)],
    )
    pieces = halo((own, lon, lat, dia), 1)
    wshape = ((256, 4 * D), BF16)
    keep1, send1 = call(weights_kernel, 2, [wshape] * 2, idx, h1, o1, dqkv1, g1)
    recv1 = flip(send1, "c")

    def pairs(*shapes):
        return [(s, BF16) for shape in shapes for s in shape]

    cells = ((72, 2, D), BF16)
    g0, dqkv0, ds00, ds01, keep0, send0 = call(
        third_kernel,
        4,
        [((144, D), BF16), ((144, 3 * D), BF16)] + ds_shapes + [wshape, wshape],
        idx, *pieces, gains, proj_weight, n0, qkv0, p0, o0, jnp.asarray(const[8]), keep1,
        specs={6: block(0, (D, D)), 12: ANY},
    )
    recv0 = flip(send0, "c")
    outputs, grad_inputs, dgain0 = call(
        finish_kernel,
        2,
        [cells, cells, ((1, D), F32)],
        *pieces, gains, qkv_weight, n0, rstd0, g0, dqkv0, jnp.asarray(const[9:11]), keep0,
        specs={5: block(0, (D, 3 * D)), 11: ANY},
        scratch=[((144, 2 * D), F32)],
    )
    outputs, grad_inputs = [
        v.reshape(1, 6, 12, 2, D).transpose(0, 3, 1, 2, 4) for v in (outputs, grad_inputs)
    ]
    ka, sa, kb, sb, kc, sc = call(
        core_kernel,
        1,
        pairs([(128, 1536)] * 2, [(256, 768)] * 2, [(128, 1024)] * 2),
        idx, keep0, recv0, keep1, recv1,
    )
    ra, rb, rc = flip(sa, "x0"), flip(sb, "yl"), flip(sc, "z0")
    tshape = ((16, 1024), F32)
    tkeep, tsend = call(
        scatter_kernel,
        6,
        [tshape] * 2,
        idx, ids, tails, ds00, ds01, dgain0, ds10, ds11, dgain1, ka,
        specs={9: ANY},
    )
    trecv = flip(tsend, "c")
    ka, sa, kb, sb, kc, sc, tk = call(
        step_two_kernel,
        1,
        pairs([(128, 768)] * 4, [(64, 1024), (80, 1024)], [(16, 1024)]),
        idx, ka, ra, kb, rb, kc, rc, tkeep, trecv,
    )
    ra, rb, rc = flip(sa, "yl"), flip(sb, "z0"), flip(sc, "x0")
    ka, sa, kb, sb, kc, sc, tk = call(
        step_three_kernel,
        1,
        pairs([(64, 768), (96, 768)], [(64, 768)] * 2, [(64, 512)] * 2, [(32, 768)]),
        idx, ka, ra, kb, rb, kc, rc, tk,
    )
    ra, rb, rc = flip(sa, "z0"), flip(sb, "x0"), flip(sc, "yl")
    parts = call(
        spread_kernel,
        1,
        [((24, 2048), BF16)] * 4,
        idx, ka, ra, kb, rb, kc, rc, tk,
        scratch=[((4, 16, 2048), BF16)],
    )
    keep, tab, send = call(
        plane_kernel,
        1,
        [((8, 2048), F32), ((8, 2048), BF16), ((16, 2048), BF16)],
        idx, parts[0], flip(parts[1], "yh"), flip(parts[2], "x1", "x0"),
        flip(parts[3], "x1", "x0", "yh"),
        scratch=[((4, 8, 2048), F32)],
    )
    keep, tab, send = call(
        ring_kernel,
        1,
        [((8, 1024), F32), ((16, 1024), BF16), ((24, 1024), BF16)],
        idx, keep, tab, z_step(send, lambda z: (z + 1) % 8 if z & 1 else (z - 1) % 8),
    )
    own, tab = call(
        close_kernel,
        1,
        [((24, 1024), BF16), ((16, 1024), BF16)],
        keep, tab, z_step(send, lambda z: z ^ (7 if (z ^ z >> 1) & 1 else 3)),
    )
    from_core = flip(tab, "c")
    from_dia = flip(tab, "c", "yl")
    from_lat = flip(own, "yl")
    factor = 36864 ** (-0.5)
    grad_gains, grad_qkv, grad_proj, grad_bias = call(
        functools.partial(last_kernel, factor),
        1,
        [
            ((2, D), F32),
            ((2, 4, 3 * D), F32),
            ((2, 4, D), F32),
            ((2, 2, HEADS, NREL), F32),
        ],
        idx, own, from_lat, from_core, from_dia,
    )
    return (outputs, grad_inputs, grad_gains, grad_qkv, grad_proj, grad_bias)


def solution(mesh):
    fine = Mesh(mesh.devices.reshape((2,) * 8), AXES)
    lon = AXES[:7]
    field = P(None, None, "yl", lon, None)
    rows = P(None, lon, None)
    return jax.shard_map(
        on_device,
        mesh=fine,
        in_specs=(field, field, P(), P(), P(), P(), P(), P(None, "yl", lon)),
        out_specs=(field, field, P(), rows, rows, P()),
        check_vma=False,
    )
```

```python
import functools

import jax
import jax.numpy as jnp
import numpy as np
from jax import lax
from jax.experimental import pallas as pl
from jax.experimental.pallas import tpu as pltpu
from jax.sharding import Mesh, PartitionSpec as P

F32 = jnp.float32
BF16 = jnp.bfloat16
EPSILON = 1e-05
NEGATIVE = -1e30
D = 512
HEADS = 16
NREL = 759
SCALE = 32 ** (-0.5)
AXES = ("yh", "x1", "x0", "z2", "z1", "z0", "c", "yl")
VMEM = 24 << 20

QUADS = ((1, 1), (1, 0), (0, 1), (0, 0))


def _token(rh, ch, l, r, c):
    return (rh * 2 + ch) * 36 + l * 18 + r * 6 + c


def _tables():
    px = np.zeros((144, 144), np.float32)
    ps = np.zeros((160, 144), np.float32)
    pf = np.zeros((144, 160), np.float32)
    pm = np.zeros((144, 144), np.float32)
    rows = np.zeros((144, 12), np.float32)
    cols = np.zeros((144, 12), np.float32)
    flags = np.zeros((144, 2), np.float32)
    into = np.zeros((160, 144), np.float32)
    spot = np.zeros((144, 128), np.float32)
    back = np.zeros((144, 160), np.float32)
    seat = np.zeros((144, 128), np.float32)
    for l in range(2):
        for row in range(6):
            for col in range(12):
                rh, r, ch, c = row // 3, row % 3, col // 6, col % 6
                t = _token(rh, ch, l, r, c)
                px[t, (row * 12 + col) * 2 + l] = 1
                pm[t, l * 72 + row * 12 + col] = 1
                rows[t, row * 2 + l] = 1
                cols[t, col] = 1
                flags[t] = (l, rh)
                k = QUADS.index((rh, ch))
                i = (1 - l) * 18 + r * 6 + c
                ps[40 * k + i, t] = 1
                into[40 * k + 36, t] = 1
                spot[t, i] = 1
    for k in range(4):
        for i in range(36):
            t = 36 * k + i
            pf[t, 40 * k + i] = 1
            back[t, 40 * k + 36] = 1
            seat[t, i] = 1
    first = (px, ps, pm, rows, cols, into, spot)
    second = (pf, pf.T, flags, back, seat)
    return first, second, (ps.T,), (px.T @ ps.T, px.T)


def stacked(parts):
    out = np.zeros((len(parts), 160, 256), np.float32)
    for k, part in enumerate(parts):
        out[k, : part.shape[0], : part.shape[1]] = part
    return out.astype(jnp.bfloat16)


TABLES = [stacked(group) for group in _tables()]


def dot(a, b):
    return lax.dot_general(a, b, (((1,), (0,)), ((), ())), preferred_element_type=F32)


def dot_nt(a, b):
    return lax.dot_general(a, b, (((1,), (1,)), ((), ())), preferred_element_type=F32)


def dot_tn(a, b):
    return lax.dot_general(a, b, (((0,), (0,)), ((), ())), preferred_element_type=F32)


def lane_masks():
    lane = lax.broadcasted_iota(jnp.int32, (1, 128), 1) >> 5
    return [jnp.where(lane == k, 1.0, 0.0).astype(F32) for k in range(4)]


def stack_heads(group, masks):
    return jnp.concatenate([group * m.astype(BF16) for m in masks], axis=0)


def fold_heads(stacked, masks):
    total = stacked[0:144] * masks[0]
    for k in range(1, 4):
        total = total + stacked[144 * k : 144 * (k + 1)] * masks[k]
    return total


def pad_keys(group):
    return jnp.concatenate([group, jnp.zeros((112, 128), BF16)], axis=0)


def normalize(x):
    center = x - jnp.mean(x, axis=-1, keepdims=True)
    rstd = lax.rsqrt(jnp.mean(center * center, axis=-1, keepdims=True) + EPSILON)
    return center * rstd, rstd


def pack_table(tab, words, scales, offsets):
    low = jnp.min(tab, axis=-1, keepdims=True)
    scale = jnp.maximum(jnp.max(tab, axis=-1, keepdims=True) - low, 1e-20) * (1.0 / 65535.0)
    q = jnp.clip(jnp.floor((tab - low) / scale + 0.5), 0.0, 65535.0).astype(jnp.int32)
    high = jnp.concatenate([q[4 * g : 4 * g + 2] for g in range(4)], axis=0)
    rest = jnp.concatenate([q[4 * g + 2 : 4 * g + 4] for g in range(4)], axis=0)
    words[...] = jnp.zeros((8, 768), jnp.int32)
    words[:, 0:NREL] = ((high - 32768) << 16) + rest
    signed = lax.broadcasted_iota(jnp.int32, (HEADS, 1), 0) & 3
    offset = low + jnp.where(signed < 2, 32768.0, 0.0) * scale
    scales[...] = jnp.broadcast_to(scale, (HEADS, 128))
    offsets[...] = jnp.broadcast_to(offset, (HEADS, 128))


def lookup(row, ids):
    acc = None
    for k in range(6):
        part = jnp.broadcast_to(row[:, 128 * k : 128 * (k + 1)], ids.shape)
        got = jnp.take_along_axis(part, ids & 127, axis=1)
        acc = got if k == 0 else jnp.where((ids >> 7) == k, got, acc)
    return acc


def side_by_side(tail):
    total = tail[0:24]
    for k in range(1, 6):
        total = total + pltpu.roll(tail[24 * k : 24 * (k + 1)], 16 * k, 1)
    return total


def bias_pair(m, words, scales, offsets, ids, tails):
    row = words[m : m + 1, :]
    main = lookup(row, ids)
    tail = lookup(row, tails)
    parts = [tail] + [pltpu.roll(tail, 128 - 16 * k, 1) for k in range(1, 6)]
    tail = jnp.concatenate(parts, axis=0)
    lane = lax.broadcasted_iota(jnp.int32, (144, 128), 1)
    head = 4 * (m // 2) + m % 2
    out = []
    for h, take in ((head, lambda w: w >> 16), (head + 2, lambda w: w & 65535)):
        scale, offset = scales[h : h + 1, :], offsets[h : h + 1, :]
        a = take(main).astype(F32) * scale + offset
        b = jnp.where(lane < 16, take(tail).astype(F32) * scale + offset, NEGATIVE)
        out.append(jnp.concatenate([a, b], axis=1))
    return out


def frame_ids(rel, pm, main_ref, tail_ref):
    parts = []
    for part in (rel >> 5, rel & 31):
        half = dot(pm, part.astype(F32).astype(BF16)).astype(BF16)
        parts.append(dot_nt(half, pm).astype(jnp.int32))
    ids = parts[0] * 32 + parts[1]
    main_ref[...] = ids[:, 0:128]
    tail = jnp.concatenate([ids[:, 128:144], jnp.zeros((144, 112), jnp.int32)], axis=1)
    tail_ref[...] = side_by_side(tail)


def fill_bias(table, main_ref, tail_ref, words, scales, offsets, store):
    pack_table(table, words, scales, offsets)
    ids, tails = main_ref[...], tail_ref[...]
    for m in range(8):
        head = 4 * (m // 2) + m % 2
        for h, b in zip((head, head + 2), bias_pair(m, words, scales, offsets, ids, tails)):
            store[144 * h : 144 * (h + 1), :] = b


def group_probs(qkv_ref, g, masks, biases, allowed):
    qg = qkv_ref[:, 128 * g : 128 * (g + 1)]
    kg = pad_keys(qkv_ref[:, 512 + 128 * g : 512 + 128 * (g + 1)])
    q4 = stack_heads(qg, masks)
    s4 = dot_nt(q4, kg) * SCALE
    out = []
    for k in range(4):
        s = s4[144 * k : 144 * (k + 1)] + biases[k]
        if allowed is not None:
            s = jnp.where(allowed, s, NEGATIVE)
        e = jnp.exp(s - jnp.max(s, axis=-1, keepdims=True))
        out.append(e * (1.0 / jnp.sum(e, axis=-1, keepdims=True)))
    return q4, kg, jnp.concatenate(out, axis=0)


def group_back(g, q4, kg, vg, p4, p4b, do, masks, dqkv_ref, ds0_ref, ds1_ref):
    do4 = stack_heads(do[:, 128 * g : 128 * (g + 1)], masks)
    dp4 = dot_nt(do4, vg)
    dqkv_ref[:, 1024 + 128 * g : 1024 + 128 * (g + 1)] = dot_tn(p4b[:, 0:144], do4).astype(BF16)
    ds4 = p4 * (dp4 - jnp.sum(dp4 * p4, axis=-1, keepdims=True))
    ds0_ref[576 * g : 576 * (g + 1), :] = ds4[:, 0:128]
    for k in range(4):
        at = 24 * (4 * g + k)
        ds1_ref[at : at + 24, :] = side_by_side(ds4[144 * k : 144 * (k + 1), 128:256])
    ds4b = ds4.astype(BF16)
    dq = fold_heads(dot(ds4b, kg), masks) * SCALE
    dqkv_ref[:, 128 * g : 128 * (g + 1)] = dq.astype(BF16)
    dk = dot_tn(ds4b[:, 0:144], q4) * SCALE
    dqkv_ref[:, 512 + 128 * g : 512 + 128 * (g + 1)] = dk.astype(BF16)


def finish_back(dqkv_ref, wqkv_ref, n, rstd, gain, g32, dgain_ref):
    dh = dot_nt(dqkv_ref[...], wqkv_ref[0])
    dgain_ref[...] = jnp.sum(dh * n, axis=0, keepdims=True)
    dn = dh * gain
    return (
        rstd
        * (
            dn
            - jnp.mean(dn, axis=-1, keepdims=True)
            - n * jnp.mean(dn * n, axis=-1, keepdims=True)
        )
        + g32
    )


def weight_terms(idx_ref, h, o, dqkv, g, keep_ref, send_ref):
    core = idx_ref[0]
    p = lax.broadcasted_iota(jnp.int32, (256, 512), 0)
    row = lax.broadcasted_iota(jnp.int32, (256, 512), 1)
    bit = lambda k: (p >> k) & 1
    hz, h2, h3 = bit(6), bit(4), bit(2)
    z1 = h3 ^ (hz & h2)
    place = (
        (8, bit(3)),
        (7, bit(5)),
        (6, bit(7) ^ bit(5)),
        (5, h2 ^ (hz & (h2 ^ h3))),
        (4, z1),
        (3, z1 ^ hz),
    )
    base = p & 3
    for to, value in place:
        base = base + (value << to)
    for which, ref in ((core, keep_ref), (1 - core, send_ref)):
        pick = jnp.where(row == base + which * 4, 1.0, 0.0).astype(BF16)
        ht = dot_nt(pick, h).astype(BF16)
        ot = dot_nt(pick, o).astype(BF16)
        ref[:, 0:1536] = dot(ht, dqkv).astype(BF16)
        ref[:, 1536:2048] = dot(ot, g).astype(BF16)


def store_pieces(out, *refs):
    for k, ref in enumerate(refs):
        ref[...] = out[40 * k : 40 * (k + 1)].astype(BF16)


def load_pieces(cols, *refs):
    return jnp.concatenate([ref[:, cols].astype(F32) for ref in refs], axis=0).astype(BF16)


def first_kernel(
    x_hbm, go_hbm, grp_hbm, gain_hbm, wqkv_hbm, wproj_hbm, tab_hbm, rel_hbm, const_hbm,
    own_ref, lon_ref, lat_ref, dia_ref, n_ref, rstd_ref, qkv_ref, p_ref, o_ref,
    cells, gs, pay, bias_ref, main_ref, tail_ref, words, scales, offsets,
    x_ref, go_ref, grp_ref, gain_ref, wqkv_ref, wproj_ref, tab_ref, rel_ref, const_ref, sems,
):
    sources = [
        (rel_hbm, rel_ref),
        (tab_hbm.at[0, lax.axis_index("yl")], tab_ref),
        (const_hbm, const_ref),
        (x_hbm, x_ref),
        (go_hbm, go_ref),
        (grp_hbm, grp_ref),
        (gain_hbm, gain_ref),
        (wqkv_hbm.at[0], wqkv_ref),
        (wproj_hbm.at[0], wproj_ref),
    ]
    copies = [pltpu.make_async_copy(a, b, sems.at[k]) for k, (a, b) in enumerate(sources)]
    for copy in copies:
        copy.start()
    for copy in copies[0:3]:
        copy.wait()
    px, ps, pm = [const_ref[k, 0 : (144, 160, 144)[k], 0:144] for k in range(3)]
    rows, cols = const_ref[3, 0:144, 0:12], const_ref[4, 0:144, 0:12]

    frame_ids(rel_ref[...], pm, main_ref, tail_ref)
    fill_bias(tab_ref[...], main_ref, tail_ref, words, scales, offsets, bias_ref)

    masks = lane_masks()
    for copy in copies[3:8]:
        copy.wait()
    for k in range(72):
        cells[2 * k : 2 * k + 2, 0:512] = x_ref[k].astype(F32)
        cells[2 * k : 2 * k + 2, 512:1024] = go_ref[k].astype(F32)
    both = dot(px, cells[...].astype(BF16))
    x = both[:, 0:512]
    pay[:, 512:1024] = both[:, 512:1024].astype(BF16)
    for r in range(6):
        gs[2 * r : 2 * r + 2, :] = grp_ref[r].astype(F32)
    picked = dot(rows, gs[...].astype(BF16)) * cols.astype(F32)
    group = jnp.sum(picked, axis=-1, keepdims=True)
    spots = (group * const_ref[6, 0:144, 0:128].astype(F32)).astype(BF16)
    group_rows = dot(const_ref[5, :, 0:144], spots)

    n, rstd = normalize(x)
    n_ref[...] = n
    rstd_ref[...] = rstd
    h = (n * gain_ref[0:1, :]).astype(BF16)
    qkv_ref[...] = dot(h, wqkv_ref[...]).astype(BF16)
    for g in range(4):
        biases = [bias_ref[576 * g + 144 * k : 576 * g + 144 * (k + 1), :] for k in range(4)]
        _, _, p4 = group_probs(qkv_ref, g, masks, biases, None)
        p4b = p4.astype(BF16)
        p_ref[576 * g : 576 * (g + 1), :] = p4b
        vg = pad_keys(qkv_ref[:, 1024 + 128 * g : 1024 + 128 * (g + 1)])
        o_ref[:, 128 * g : 128 * (g + 1)] = fold_heads(dot(p4b, vg), masks).astype(BF16)
    copies[8].wait()
    pay[:, 0:512] = (x + dot(o_ref[...], wproj_ref[...])).astype(BF16)
    out = dot(ps, pay[...])
    out = jnp.concatenate([out[:, 0:128] + group_rows, out[:, 128:1024]], axis=1)
    store_pieces(out, own_ref, lon_ref, lat_ref, dia_ref)


def bias_kernel(
    idx_ref, tab_ref, rel_ref, pm_ref, out_ref, main_ref, tail_ref, words, scales, offsets
):
    frame_ids(rel_ref[...], pm_ref[0:144, 0:144], main_ref, tail_ref)
    fill_bias(tab_ref[0, idx_ref[1]], main_ref, tail_ref, words, scales, offsets, out_ref)


def second_kernel(
    idx_ref, own_ref, lon_ref, lat_ref, dia_ref, gain_ref, wqkv_ref, wproj_ref, bias_ref,
    const_ref,
    oown_ref, olon_ref, olat_ref, odia_ref, h_ref, o_ref, dqkv_ref, g_ref, dgain_ref, ds0_ref, ds1_ref,
    qkv_ref, back,
):
    masks = lane_masks()
    flags = const_ref[2, 0:144, 0:2].astype(F32)
    pieces = load_pieces(slice(0, 1024), own_ref, lon_ref, lat_ref, dia_ref)
    frame = dot(const_ref[0, 0:144, 0:160], pieces)
    group = dot(const_ref[3, 0:144, 0:160], pieces[:, 0:128]) * const_ref[4, 0:144, 0:128].astype(F32)
    group = jnp.sum(group, axis=-1, keepdims=True)
    x = frame[:, 0:512]
    g32 = frame[:, 512:1024]
    gb = g32.astype(BF16)
    g_ref[...] = gb
    lat = idx_ref[1].astype(F32)
    key = group * 4.0 + flags[:, 1:2] * (2.0 * lat) + flags[:, 0:1]
    eye = lax.broadcasted_iota(jnp.int32, (144, 256), 0) == lax.broadcasted_iota(
        jnp.int32, (144, 256), 1
    )
    key_row = jnp.sum(jnp.where(eye, key, 0.0), axis=0, keepdims=True)
    allowed = key == key_row
    gain = gain_ref[1:2, :]

    n, rstd = normalize(x)
    h = (n * gain).astype(BF16)
    h_ref[...] = h
    qkv_ref[...] = dot(h, wqkv_ref[0]).astype(BF16)
    do = dot_nt(gb, wproj_ref[0]).astype(BF16)
    for g in range(4):
        biases = [bias_ref[576 * g + 144 * k : 576 * g + 144 * (k + 1), :] for k in range(4)]
        q4, kg, p4 = group_probs(qkv_ref, g, masks, biases, allowed)
        p4b = p4.astype(BF16)
        vg = pad_keys(qkv_ref[:, 1024 + 128 * g : 1024 + 128 * (g + 1)])
        o_ref[:, 128 * g : 128 * (g + 1)] = fold_heads(dot(p4b, vg), masks).astype(BF16)
        group_back(g, q4, kg, vg, p4, p4b, do, masks, dqkv_ref, ds0_ref, ds1_ref)
    back[:, 0:512] = (x + dot(o_ref[...], wproj_ref[0])).astype(BF16)
    df = finish_back(dqkv_ref, wqkv_ref, n, rstd, gain, g32, dgain_ref)
    back[:, 512:1024] = df.astype(BF16)
    store_pieces(dot(const_ref[1, :, 0:144], back[...]), oown_ref, olon_ref, olat_ref, odia_ref)


def weights_kernel(idx_ref, h_ref, o_ref, dqkv_ref, g_ref, keep_ref, send_ref):
    weight_terms(idx_ref, h_ref[...], o_ref[...], dqkv_ref[...], g_ref[...], keep_ref, send_ref)


def third_kernel(
    idx_ref, own_ref, lon_ref, lat_ref, dia_ref, gain_ref, wproj_ref,
    n_ref, qkv_ref, p_ref, o_ref, const_ref, after_ref,
    g_ref, dqkv_ref, ds0_ref, ds1_ref, keep_ref, send_ref,
):
    masks = lane_masks()
    pieces = load_pieces(slice(512, 1024), own_ref, lon_ref, lat_ref, dia_ref)
    gb = dot(const_ref[0, 0:144, 0:160], pieces).astype(BF16)
    g_ref[...] = gb
    do = dot_nt(gb, wproj_ref[0]).astype(BF16)
    for g in range(4):
        q4 = stack_heads(qkv_ref[:, 128 * g : 128 * (g + 1)], masks)
        kg = pad_keys(qkv_ref[:, 512 + 128 * g : 512 + 128 * (g + 1)])
        vg = pad_keys(qkv_ref[:, 1024 + 128 * g : 1024 + 128 * (g + 1)])
        p4b = p_ref[576 * g : 576 * (g + 1), :]
        group_back(g, q4, kg, vg, p4b.astype(F32), p4b, do, masks, dqkv_ref, ds0_ref, ds1_ref)
    h = (n_ref[...] * gain_ref[0:1, :]).astype(BF16)
    weight_terms(idx_ref, h, o_ref[...], dqkv_ref[...], gb, keep_ref, send_ref)


def finish_kernel(
    own_ref, lon_ref, lat_ref, dia_ref, gain_ref, wqkv_ref, n_ref, rstd_ref, g_ref, dqkv_ref,
    const_ref, after_ref, out_ref, gin_ref, dgain_ref, outs,
):
    pieces = load_pieces(slice(0, 512), own_ref, lon_ref, lat_ref, dia_ref)
    outs[:, 0:512] = dot(const_ref[0, 0:144, 0:160], pieces)
    df = finish_back(
        dqkv_ref, wqkv_ref, n_ref[...], rstd_ref[...], gain_ref[0:1, :], g_ref[...].astype(F32), dgain_ref
    )
    outs[:, 512:1024] = dot(const_ref[1, 0:144, 0:144], df.astype(BF16))
    for k in range(72):
        out_ref[k] = outs[2 * k : 2 * k + 2, 0:512].astype(BF16)
        gin_ref[k] = outs[2 * k : 2 * k + 2, 512:1024].astype(BF16)


def scatter_kernel(
    idx_ref, main_ref, tail_ref, m0_ref, t0_ref, gain0_ref, m1_ref, t1_ref, gain1_ref, after_ref,
    keep_ref, send_ref,
):
    iota = lax.broadcasted_iota(jnp.int32, (128, 256), 0)

    def add(ids_ref, d_refs, stride, unroll):
        def body(i, acc):
            ids = jnp.concatenate([ids_ref[pl.ds(2 * i + k, 1), :] for k in range(2)], axis=1)
            low, high = ids & 127, ids >> 7
            hot = jnp.where(iota == low, 1.0, 0.0).astype(BF16)
            lhs = []
            for d_ref in d_refs:
                d = jnp.concatenate(
                    [d_ref[pl.ds(2 * i + k, 16, stride=stride), :] for k in range(2)], axis=1
                )
                lhs += [jnp.where(high == k, d, 0.0) for k in range(6)]
            return acc + dot_nt(jnp.concatenate(lhs, axis=0).astype(BF16), hot)

        return lambda acc: lax.fori_loop(0, stride // 2, body, acc, unroll=unroll)

    acc = add(main_ref, (m0_ref, m1_ref), 144, 8)(jnp.zeros((192, 128), F32))
    acc = add(tail_ref, (t0_ref, t1_ref), 24, 12)(acc)
    first = lax.broadcasted_iota(jnp.int32, (8, 256), 0) == 0
    for b, dgain_ref in enumerate((gain0_ref, gain1_ref)):
        table = [acc[96 * b + 16 * k : 96 * b + 16 * k + 16] for k in range(6)]
        table = jnp.concatenate(table, axis=1)
        halves = []
        for c in range(2):
            gain = jnp.where(first, dgain_ref[:, 256 * c : 256 * (c + 1)], 0.0)
            halves.append(jnp.concatenate([table[8 * c : 8 * (c + 1)], gain], axis=1))
        keep, send = pick(idx_ref[0], halves[0], halves[1])
        keep_ref[8 * b : 8 * b + 8, :] = keep
        send_ref[8 * b : 8 * b + 8, :] = send


CUTS = ((0, 384), (384, 768), (768, 1024))


def pick(flag, low, high):
    mine = flag == 0
    return jnp.where(mine, low, high), jnp.where(mine, high, low)


def core_kernel(
    idx_ref, k0_ref, r0_ref, k1_ref, r1_ref, ka_ref, sa_ref, kb_ref, sb_ref, kc_ref, sc_ref
):
    x0, z0, yl = idx_ref[2], idx_ref[3], idx_ref[1]
    for b, (k_ref, r_ref) in enumerate(((k0_ref, r0_ref), (k1_ref, r1_ref))):

        def total(r0, r1, c0, c1):
            return k_ref[r0:r1, c0:c1].astype(F32) + r_ref[r0:r1, c0:c1].astype(F32)

        for s in range(2):
            a0 = 1024 * s
            keep, send = pick(x0, total(0, 128, a0, a0 + 384), total(128, 256, a0, a0 + 384))
            to = 768 * b + 384 * s
            ka_ref[:, to : to + 384] = keep.astype(BF16)
            sa_ref[:, to : to + 384] = send.astype(BF16)
            to = 512 * b + 256 * s
            for h in range(2):
                r = 128 * h
                keep, send = pick(
                    z0,
                    total(r, r + 64, a0 + 768, a0 + 1024),
                    total(r + 64, r + 128, a0 + 768, a0 + 1024),
                )
                kc_ref[64 * h : 64 * h + 64, to : to + 256] = keep.astype(BF16)
                sc_ref[64 * h : 64 * h + 64, to : to + 256] = send.astype(BF16)
        keep, send = pick(yl, total(0, 256, 384, 768), total(0, 256, 1408, 1792))
        kb_ref[:, 384 * b : 384 * (b + 1)] = keep.astype(BF16)
        sb_ref[:, 384 * b : 384 * (b + 1)] = send.astype(BF16)


def step_two_kernel(
    idx_ref, ka_ref, ra_ref, kb_ref, rb_ref, kc_ref, rc_ref, t_ref, u_ref,
    nka_ref, nsa_ref, nkb_ref, nsb_ref, nkc_ref, nsc_ref, tk_ref,
):
    x0, z0, yl = idx_ref[2], idx_ref[3], idx_ref[1]
    a = ka_ref[...].astype(F32) + ra_ref[...].astype(F32)
    for b in range(2):
        keep, send = pick(yl, a[:, 768 * b : 768 * b + 384], a[:, 768 * b + 384 : 768 * b + 768])
        nka_ref[:, 384 * b : 384 * (b + 1)] = keep.astype(BF16)
        nsa_ref[:, 384 * b : 384 * (b + 1)] = send.astype(BF16)
    m = kb_ref[...].astype(F32) + rb_ref[...].astype(F32)
    for h in range(2):
        keep, send = pick(z0, m[128 * h : 128 * h + 64], m[128 * h + 64 : 128 * h + 128])
        nkb_ref[64 * h : 64 * h + 64, :] = keep.astype(BF16)
        nsb_ref[64 * h : 64 * h + 64, :] = send.astype(BF16)
    c = kc_ref[...].astype(F32) + rc_ref[...].astype(F32)
    keep, send = pick(x0, c[0:64], c[64:128])
    nkc_ref[...] = keep.astype(BF16)
    nsc_ref[0:64, :] = send.astype(BF16)
    table = (t_ref[...] + u_ref[...]).astype(BF16)
    tk_ref[...] = table
    nsc_ref[64:80, :] = table


def step_three_kernel(
    idx_ref, ka_ref, ra_ref, kb_ref, rb_ref, kc_ref, rc_ref, tk_ref,
    nka_ref, nsa_ref, nkb_ref, nsb_ref, nkc_ref, nsc_ref, ntk_ref,
):
    x0, z0, yl = idx_ref[2], idx_ref[3], idx_ref[1]
    a = ka_ref[...].astype(F32) + ra_ref[...].astype(F32)
    keep, send = pick(z0, a[0:64], a[64:128])
    nka_ref[...] = keep.astype(BF16)
    nsa_ref[0:64, :] = send.astype(BF16)
    t = tk_ref[...].astype(F32) + rc_ref[64:80, :].astype(F32)
    gains = jnp.concatenate([t[0:8, 768:1024], t[8:16, 768:1024], jnp.zeros((8, 256), F32)], axis=1)
    table = jnp.concatenate([t[:, 0:768], gains, jnp.zeros((8, 768), F32)], axis=0).astype(BF16)
    ntk_ref[...] = table
    nsa_ref[64:96, :] = table
    m = kb_ref[...].astype(F32) + rb_ref[...].astype(F32)
    keep, send = pick(x0, m[0:64], m[64:128])
    nkb_ref[...] = keep.astype(BF16)
    nsb_ref[...] = send.astype(BF16)
    c = kc_ref[...].astype(F32) + rc_ref[0:64, :].astype(F32)
    for b in range(2):
        keep, send = pick(yl, c[:, 512 * b : 512 * b + 256], c[:, 512 * b + 256 : 512 * b + 512])
        nkc_ref[:, 256 * b : 256 * (b + 1)] = keep.astype(BF16)
        nsc_ref[:, 256 * b : 256 * (b + 1)] = send.astype(BF16)


def spread_kernel(
    idx_ref, ka_ref, ra_ref, kb_ref, rb_ref, kc_ref, rc_ref, tk_ref, *refs
):
    outs, scr = refs[0:4], refs[4]
    a = ka_ref[...].astype(F32) + ra_ref[0:64, :].astype(F32)
    m = kb_ref[...].astype(F32) + rb_ref[...].astype(F32)
    c = kc_ref[...].astype(F32) + rc_ref[...].astype(F32)
    table = tk_ref[...].astype(F32) + ra_ref[64:96, :].astype(F32)
    gains = jnp.concatenate([table[16:24, 0:256], table[16:24, 256:512]], axis=0)
    table = jnp.concatenate([table[0:16], gains], axis=1)
    table = jnp.concatenate([table[0:8], table[8:16]], axis=1).astype(BF16)
    full = []
    for b in range(2):
        cols = slice(384 * b, 384 * (b + 1))
        full += [a[:, cols], m[:, cols], c[:, 256 * b : 256 * (b + 1)]]
    full = jnp.concatenate(full, axis=1).astype(BF16)
    for k in range(4):
        scr[k] = full[16 * k : 16 * k + 16]
    for f in range(4):
        outs[f][0:16, :] = scr[idx_ref[4] ^ f]
        outs[f][16:24, :] = table


def plane_kernel(idx_ref, own_ref, g1_ref, g2_ref, g3_ref, *refs):
    outs, tabs, scr = refs[0:4], refs[4], refs[5]
    got = (own_ref, g1_ref, g2_ref, g3_ref)
    total = got[0][0:16, :].astype(F32)
    for g in got[1:]:
        total = total + g[0:16, :].astype(F32)
    for f in range(4):
        tabs[idx_ref[4] ^ f] = got[f][16:24, :].astype(F32)
    table = tabs[0] + tabs[1] + tabs[2] + tabs[3]
    table = jnp.concatenate([table[:, 0:1024], table[:, 1024:2048]], axis=0)
    for k in range(4):
        rows = total[4 * k : 4 * k + 4]
        rows = jnp.concatenate([rows[:, 0:1024], rows[:, 1024:2048], table], axis=0)
        scr[k] = rows.astype(BF16)
    for f in range(4):
        outs[f][...] = scr[idx_ref[5] ^ f]


def close_kernel(idx_ref, own_ref, g1_ref, g2_ref, g3_ref, out_ref, tab_ref, scr):
    for f, g in enumerate((own_ref, g1_ref, g2_ref, g3_ref)):
        scr[idx_ref[5] ^ f] = g[...].astype(F32)
    total = scr[0] + scr[1] + scr[2] + scr[3]
    out_ref[...] = total.astype(BF16)
    tab_ref[...] = total[8:24].astype(BF16)


def last_kernel(
    factor, idx_ref, own_ref, lat_ref, core_ref, dia_ref, gain_ref, qkv_ref, proj_ref, bias_ref
):
    core, yl = idx_ref[0], idx_ref[1]
    own = own_ref[...].astype(F32) * factor
    got = lat_ref[...].astype(F32) * factor
    low, high = pick(yl, own[0:8], got[0:8])
    for b in range(2):
        qkv_ref[b, :, 0:1024] = low[4 * b : 4 * b + 4]
        qkv_ref[b, :, 1024:1536] = high[4 * b : 4 * b + 4, 0:512]
        proj_ref[b, :, :] = high[4 * b : 4 * b + 4, 512:1024]
    near = pick(yl, own[8:24], got[8:24])
    far = pick(yl, core_ref[...].astype(F32) * factor, dia_ref[...].astype(F32) * factor)
    tabs = [pick(core, near[w], far[w]) for w in range(2)]
    for c in range(2):
        for w in range(2):
            for b in range(2):
                bias_ref[b, w, 8 * c : 8 * (c + 1), :] = tabs[w][c][8 * b : 8 * b + 8, 0:NREL]
        for b in range(2):
            gain_ref[b : b + 1, 256 * c : 256 * (c + 1)] = (
                tabs[0][c][8 * b : 8 * b + 1, 768:1024] + tabs[1][c][8 * b : 8 * b + 1, 768:1024]
            )


def _whole(shape):
    return pl.BlockSpec(shape, lambda *_: (0,) * len(shape))


SMEM = pl.BlockSpec(memory_space=pltpu.SMEM)


ANY = pl.BlockSpec(memory_space=pl.ANY)


HBM = pl.BlockSpec(memory_space=pltpu.HBM)


def call(body, us, outs, *args, specs=None, scratch=(), sems=0, vmem=VMEM):
    specs = dict(specs or {})
    if args[0].dtype == jnp.int32 and args[0].ndim == 1:
        specs[0] = SMEM
    scratch = [pltpu.VMEM(s, t) for s, t in scratch]
    if sems:
        scratch.append(pltpu.SemaphoreType.DMA((sems,)))
    return pl.pallas_call(
        body,
        grid=(1,),
        in_specs=[specs.get(i, _whole(a.shape)) for i, a in enumerate(args)],
        out_specs=[_whole(s) for s, _ in outs],
        out_shape=[jax.ShapeDtypeStruct(s, t) for s, t in outs],
        scratch_shapes=scratch,
        compiler_params=pltpu.CompilerParams(vmem_limit_bytes=vmem),
        cost_estimate=pl.CostEstimate(
            flops=int(us * 1e9), bytes_accessed=int(us * 3.6e6), transcendentals=0
        ),
    )(*args)


def mask_of(axes):
    return sum(1 << (7 - AXES.index(a)) for a in axes)


def flip(value, *axes):
    return lax.ppermute(value, AXES, [(s, s ^ mask_of(axes)) for s in range(256)])


def z_step(value, move, *axes):
    pairs = [(s, (s & ~28 | move(s >> 2 & 7) << 2) ^ mask_of(axes)) for s in range(256)]
    return lax.ppermute(value, AXES, pairs)


def lon_step(value, offset, across):
    pairs = [(s, ((s // 2 + offset) % 128) * 2 + (s % 2 ^ across)) for s in range(256)]
    return lax.ppermute(value, AXES, pairs)


def halo(pieces, offset):
    own, lon, lat, dia = pieces
    return (
        own,
        lon_step(lon, offset, 0),
        flip(lat, "yl"),
        lon_step(dia, offset, 1),
    )


def on_device(inputs, grad_out, gains, qkv_weight, proj_weight, bias_table, rel_ids, groups):
    first_const, second_const, third_const, finish_const = [jnp.asarray(t) for t in TABLES]
    at = {a: lax.axis_index(a) for a in AXES}
    hz = at["z0"] ^ at["z1"]
    idx = jnp.stack(
        [
            at["c"],
            at["yl"],
            at["x0"] ^ at["x1"],
            hz,
            2 * at["x1"] + (at["z2"] ^ (hz & at["z1"])),
            2 * at["yh"] + (at["z1"] ^ (hz & (at["z1"] ^ at["z2"]))),
        ]
    ).astype(jnp.int32)
    x_cells, go_cells = [v.transpose(0, 2, 3, 1, 4).reshape(72, 2, D) for v in (inputs, grad_out)]

    def block(b, shape):
        return pl.BlockSpec((1,) + shape, lambda *_: (b,) + (0,) * len(shape))

    def weights(b, first):
        return {
            first: block(b, (D, 3 * D)),
            first + 1: block(b, (D, D)),
            first + 2: block(b, (2, HEADS, NREL)),
        }

    id_shapes = [((144, 128), jnp.int32), ((24, 128), jnp.int32)]
    tables = [((8, 768), jnp.int32), ((HEADS, 128), F32), ((HEADS, 128), F32)]
    piece = ((40, 1024), BF16)
    own, lon, lat, dia, n0, rstd0, qkv0, p0, o0 = call(
        first_kernel,
        8,
        [piece] * 4
        + [
            ((144, D), F32),
            ((144, 1), F32),
            ((144, 3 * D), BF16),
            ((2304, 256), BF16),
            ((144, D), BF16),
        ],
        x_cells, go_cells, groups.transpose(1, 0, 2), gains, qkv_weight, proj_weight, bias_table, rel_ids,
        first_const,
        specs={k: HBM for k in range(9)},
        scratch=[((144, 1024), F32), ((12, 12), F32), ((144, 1024), BF16), ((2304, 256), F32)]
        + id_shapes
        + tables
        + [
            ((72, 2, D), BF16),
            ((72, 2, D), BF16),
            ((6, 2, 12), jnp.int32),
            ((2, D), F32),
            ((D, 3 * D), BF16),
            ((D, D), BF16),
            ((HEADS, NREL), F32),
            ((144, 144), jnp.int32),
            ((7, 160, 256), BF16),
        ],
        sems=9,
        vmem=57 << 20,
    )
    pieces = halo((own, lon, lat, dia), -1)
    bias1, ids, tails = call(
        bias_kernel,
        4,
        [((2304, 256), F32)] + id_shapes,
        idx, bias_table, rel_ids, jnp.asarray(TABLES[0][2]),
        specs={1: block(1, (2, HEADS, NREL))},
        scratch=tables,
    )
    ds_shapes = [((2304, 128), F32), ((384, 128), F32)]
    own, lon, lat, dia, h1, o1, dqkv1, g1, dgain1, ds10, ds11 = call(
        second_kernel,
        6,
        [piece] * 4
        + [
            ((144, D), BF16),
            ((144, D), BF16),
            ((144, 3 * D), BF16),
            ((144, D), BF16),
            ((1, D), F32),
        ]
        + ds_shapes,
        idx, *pieces, gains, qkv_weight, proj_weight, bias1, second_const,
        specs={6: block(1, (D, 3 * D)), 7: block(1, (D, D))},
        scratch=[((144, 3 * D), BF16), ((144, 2 * D), BF16)],
    )
    pieces = halo((own, lon, lat, dia), 1)
    wshape = ((256, 4 * D), BF16)
    keep1, send1 = call(weights_kernel, 2, [wshape] * 2, idx, h1, o1, dqkv1, g1)
    recv1 = flip(send1, "c")

    def pairs(*shapes):
        return [(s, BF16) for shape in shapes for s in shape]

    cells = ((72, 2, D), BF16)
    g0, dqkv0, ds00, ds01, keep0, send0 = call(
        third_kernel,
        4,
        [((144, D), BF16), ((144, 3 * D), BF16)] + ds_shapes + [wshape, wshape],
        idx, *pieces, gains, proj_weight, n0, qkv0, p0, o0, third_const, keep1,
        specs={6: block(0, (D, D)), 12: ANY},
    )
    recv0 = flip(send0, "c")
    outputs, grad_inputs, dgain0 = call(
        finish_kernel,
        2,
        [cells, cells, ((1, D), F32)],
        *pieces, gains, qkv_weight, n0, rstd0, g0, dqkv0, finish_const, keep0,
        specs={5: block(0, (D, 3 * D)), 11: ANY},
        scratch=[((144, 2 * D), F32)],
    )
    outputs, grad_inputs = [
        v.reshape(1, 6, 12, 2, D).transpose(0, 3, 1, 2, 4) for v in (outputs, grad_inputs)
    ]
    ka, sa, kb, sb, kc, sc = call(
        core_kernel,
        1,
        pairs([(128, 1536)] * 2, [(256, 768)] * 2, [(128, 1024)] * 2),
        idx, keep0, recv0, keep1, recv1,
    )
    ra, rb, rc = flip(sa, "x0"), flip(sb, "yl"), flip(sc, "z0")
    tshape = ((16, 1024), F32)
    tkeep, tsend = call(
        scatter_kernel,
        6,
        [tshape] * 2,
        idx, ids, tails, ds00, ds01, dgain0, ds10, ds11, dgain1, ka,
        specs={9: ANY},
    )
    trecv = flip(tsend, "c")
    ka, sa, kb, sb, kc, sc, tk = call(
        step_two_kernel,
        1,
        pairs([(128, 768)] * 4, [(64, 1024), (80, 1024)], [(16, 1024)]),
        idx, ka, ra, kb, rb, kc, rc, tkeep, trecv,
    )
    ra, rb, rc = flip(sa, "yl"), flip(sb, "z0"), flip(sc, "x0")
    ka, sa, kb, sb, kc, sc, tk = call(
        step_three_kernel,
        1,
        pairs([(64, 768), (96, 768)], [(64, 768)] * 2, [(64, 512)] * 2, [(32, 768)]),
        idx, ka, ra, kb, rb, kc, rc, tk,
    )
    ra, rb, rc = flip(sa, "z0"), flip(sb, "x0"), flip(sc, "yl")
    parts = call(
        spread_kernel,
        1,
        [((24, 2048), BF16)] * 4,
        idx, ka, ra, kb, rb, kc, rc, tk,
        scratch=[((4, 16, 2048), BF16)],
    )
    near = lambda z: (z + 1) % 8 if z & 1 else (z - 1) % 8
    far = lambda z: z ^ (7 if (z ^ z >> 1) & 1 else 3)
    parts = call(
        plane_kernel,
        1,
        [((24, 1024), BF16)] * 4,
        idx, parts[0], z_step(parts[1], near), flip(parts[2], "x1", "x0"),
        z_step(parts[3], near, "x1", "x0"),
        scratch=[((4, 8, 2048), F32), ((4, 24, 1024), BF16)],
    )
    own, tab = call(
        close_kernel,
        1,
        [((24, 1024), BF16), ((16, 1024), BF16)],
        idx, parts[0], z_step(parts[1], far), flip(parts[2], "yh"), z_step(parts[3], far, "yh"),
        scratch=[((4, 24, 1024), F32)],
    )
    from_core = flip(tab, "c")
    from_dia = flip(tab, "c", "yl")
    from_lat = flip(own, "yl")
    factor = 36864 ** (-0.5)
    grad_gains, grad_qkv, grad_proj, grad_bias = call(
        functools.partial(last_kernel, factor),
        1,
        [
            ((2, D), F32),
            ((2, 4, 3 * D), F32),
            ((2, 4, D), F32),
            ((2, 2, HEADS, NREL), F32),
        ],
        idx, own, from_lat, from_core, from_dia,
    )
    return (outputs, grad_inputs, grad_gains, grad_qkv, grad_proj, grad_bias)


def solution(mesh):
    fine = Mesh(mesh.devices.reshape((2,) * 8), AXES)
    lon = AXES[:7]
    field = P(None, None, "yl", lon, None)
    rows = P(None, lon, None)
    return jax.shard_map(
        on_device,
        mesh=fine,
        in_specs=(field, field, P(), P(), P(), P(), P(), P(None, "yl", lon)),
        out_specs=(field, field, P(), rows, rows, P()),
        check_vma=False,
    )
```

```python
import functools

import jax
import jax.numpy as jnp
import numpy as np
from jax import lax
from jax.experimental import pallas as pl
from jax.experimental.pallas import tpu as pltpu
from jax.sharding import Mesh, PartitionSpec as P

F32 = jnp.float32
BF16 = jnp.bfloat16
EPSILON = 1e-05
NEGATIVE = -1e30
D = 512
HEADS = 16
NREL = 759
SCALE = 32 ** (-0.5)
AXES = ("yh", "x1", "x0", "z2", "z1", "z0", "c", "yl")
VMEM = 24 << 20

QUADS = ((1, 1), (1, 0), (0, 1), (0, 0))


def _token(rh, ch, l, r, c):
    return (rh * 2 + ch) * 36 + l * 18 + r * 6 + c


def _tables():
    px = np.zeros((144, 144), np.float32)
    ps = np.zeros((160, 144), np.float32)
    pf = np.zeros((144, 160), np.float32)
    pm = np.zeros((144, 144), np.float32)
    rows = np.zeros((144, 12), np.float32)
    cols = np.zeros((144, 12), np.float32)
    flags = np.zeros((144, 2), np.float32)
    into = np.zeros((160, 144), np.float32)
    spot = np.zeros((144, 128), np.float32)
    back = np.zeros((144, 160), np.float32)
    seat = np.zeros((144, 128), np.float32)
    for l in range(2):
        for row in range(6):
            for col in range(12):
                rh, r, ch, c = row // 3, row % 3, col // 6, col % 6
                t = _token(rh, ch, l, r, c)
                px[t, (row * 12 + col) * 2 + l] = 1
                pm[t, l * 72 + row * 12 + col] = 1
                rows[t, row * 2 + l] = 1
                cols[t, col] = 1
                flags[t] = (l, rh)
                k = QUADS.index((rh, ch))
                i = (1 - l) * 18 + r * 6 + c
                ps[40 * k + i, t] = 1
                into[40 * k + 36, t] = 1
                spot[t, i] = 1
    for k in range(4):
        for i in range(36):
            t = 36 * k + i
            pf[t, 40 * k + i] = 1
            back[t, 40 * k + 36] = 1
            seat[t, i] = 1
    first = (px, ps, pm, rows, cols, into, spot)
    second = (pf, pf.T, flags, back, seat)
    return first, second, (ps.T,), (px.T @ ps.T, px.T)


def stacked(parts):
    out = np.zeros((len(parts), 160, 256), np.float32)
    for k, part in enumerate(parts):
        out[k, : part.shape[0], : part.shape[1]] = part
    return out.astype(jnp.bfloat16)


TABLES = [stacked(group) for group in _tables()]


def dot(a, b):
    return lax.dot_general(a, b, (((1,), (0,)), ((), ())), preferred_element_type=F32)


def dot_nt(a, b):
    return lax.dot_general(a, b, (((1,), (1,)), ((), ())), preferred_element_type=F32)


def dot_tn(a, b):
    return lax.dot_general(a, b, (((0,), (0,)), ((), ())), preferred_element_type=F32)


def lane_masks():
    lane = lax.broadcasted_iota(jnp.int32, (1, 128), 1) >> 5
    return [jnp.where(lane == k, 1.0, 0.0).astype(F32) for k in range(4)]


def stack_heads(group, masks):
    return jnp.concatenate([group * m.astype(BF16) for m in masks], axis=0)


def fold_heads(stacked, masks):
    total = stacked[0:144] * masks[0]
    for k in range(1, 4):
        total = total + stacked[144 * k : 144 * (k + 1)] * masks[k]
    return total


def pad_keys(group):
    return jnp.concatenate([group, jnp.zeros((112, 128), BF16)], axis=0)


def normalize(x):
    center = x - jnp.mean(x, axis=-1, keepdims=True)
    rstd = lax.rsqrt(jnp.mean(center * center, axis=-1, keepdims=True) + EPSILON)
    return center * rstd, rstd


def pack_table(tab, words, scales, offsets):
    low = jnp.min(tab, axis=-1, keepdims=True)
    scale = jnp.maximum(jnp.max(tab, axis=-1, keepdims=True) - low, 1e-20) * (1.0 / 65535.0)
    q = jnp.clip(jnp.floor((tab - low) / scale + 0.5), 0.0, 65535.0).astype(jnp.int32)
    high = jnp.concatenate([q[4 * g : 4 * g + 2] for g in range(4)], axis=0)
    rest = jnp.concatenate([q[4 * g + 2 : 4 * g + 4] for g in range(4)], axis=0)
    words[...] = jnp.zeros((8, 768), jnp.int32)
    words[:, 0:NREL] = ((high - 32768) << 16) + rest
    signed = lax.broadcasted_iota(jnp.int32, (HEADS, 1), 0) & 3
    offset = low + jnp.where(signed < 2, 32768.0, 0.0) * scale
    scales[...] = jnp.broadcast_to(scale, (HEADS, 128))
    offsets[...] = jnp.broadcast_to(offset, (HEADS, 128))


def lookup(row, ids):
    acc = None
    for k in range(6):
        part = jnp.broadcast_to(row[:, 128 * k : 128 * (k + 1)], ids.shape)
        got = jnp.take_along_axis(part, ids & 127, axis=1)
        acc = got if k == 0 else jnp.where((ids >> 7) == k, got, acc)
    return acc


def side_by_side(tail):
    total = tail[0:24]
    for k in range(1, 6):
        total = total + pltpu.roll(tail[24 * k : 24 * (k + 1)], 16 * k, 1)
    return total


def bias_pair(m, words, scales, offsets, ids, tails):
    row = words[m : m + 1, :]
    main = lookup(row, ids)
    tail = lookup(row, tails)
    parts = [tail] + [pltpu.roll(tail, 128 - 16 * k, 1) for k in range(1, 6)]
    tail = jnp.concatenate(parts, axis=0)
    lane = lax.broadcasted_iota(jnp.int32, (144, 128), 1)
    head = 4 * (m // 2) + m % 2
    out = []
    for h, take in ((head, lambda w: w >> 16), (head + 2, lambda w: w & 65535)):
        scale, offset = scales[h : h + 1, :], offsets[h : h + 1, :]
        a = take(main).astype(F32) * scale + offset
        b = jnp.where(lane < 16, take(tail).astype(F32) * scale + offset, NEGATIVE)
        out.append(jnp.concatenate([a, b], axis=1))
    return out


def frame_ids(rel, pm, main_ref, tail_ref):
    parts = []
    for part in (rel >> 5, rel & 31):
        half = dot(pm, part.astype(F32).astype(BF16)).astype(BF16)
        parts.append(dot_nt(half, pm).astype(jnp.int32))
    ids = parts[0] * 32 + parts[1]
    main_ref[...] = ids[:, 0:128]
    tail = jnp.concatenate([ids[:, 128:144], jnp.zeros((144, 112), jnp.int32)], axis=1)
    tail_ref[...] = side_by_side(tail)


def fill_bias(table, main_ref, tail_ref, words, scales, offsets, store):
    pack_table(table, words, scales, offsets)
    ids, tails = main_ref[...], tail_ref[...]
    for m in range(8):
        head = 4 * (m // 2) + m % 2
        for h, b in zip((head, head + 2), bias_pair(m, words, scales, offsets, ids, tails)):
            store[144 * h : 144 * (h + 1), :] = b


def group_probs(qkv_ref, g, masks, biases, allowed):
    qg = qkv_ref[:, 128 * g : 128 * (g + 1)]
    kg = pad_keys(qkv_ref[:, 512 + 128 * g : 512 + 128 * (g + 1)])
    q4 = stack_heads(qg, masks)
    s4 = dot_nt(q4, kg) * SCALE
    out = []
    for k in range(4):
        s = s4[144 * k : 144 * (k + 1)] + biases[k]
        if allowed is not None:
            s = jnp.where(allowed, s, NEGATIVE)
        e = jnp.exp(s - jnp.max(s, axis=-1, keepdims=True))
        out.append(e * (1.0 / jnp.sum(e, axis=-1, keepdims=True)))
    return q4, kg, jnp.concatenate(out, axis=0)


def by_keys(left, right):
    parts = [dot(left[32 * k : 32 * k + 32], right[144 * k : 144 * k + 144]) for k in range(4)]
    return jnp.concatenate(parts, axis=0).T[0:144]


def by_rows(left, right):
    parts = [dot_nt(left[32 * k : 32 * k + 32], right[144 * k : 144 * k + 144]) for k in range(4)]
    return jnp.concatenate(parts, axis=0).T


def group_back(g, qg, q4, kg, vg, p4, p4b, do, masks, dqkv_ref, ds0_ref, ds1_ref):
    do4 = stack_heads(do[:, 128 * g : 128 * (g + 1)], masks)
    dp4 = dot_nt(do4, vg)
    if qg is None:
        dv = dot_tn(p4b[:, 0:144], do4)
    else:
        dv = by_keys(do[:, 128 * g : 128 * (g + 1)].T, p4b)
    dqkv_ref[:, 1024 + 128 * g : 1024 + 128 * (g + 1)] = dv.astype(BF16)
    ds4 = p4 * (dp4 - jnp.sum(dp4 * p4, axis=-1, keepdims=True))
    ds0_ref[576 * g : 576 * (g + 1), :] = ds4[:, 0:128]
    for k in range(4):
        at = 24 * (4 * g + k)
        ds1_ref[at : at + 24, :] = side_by_side(ds4[144 * k : 144 * (k + 1), 128:256])
    ds4b = ds4.astype(BF16)
    dq = fold_heads(dot(ds4b, kg), masks) * SCALE
    dqkv_ref[:, 128 * g : 128 * (g + 1)] = dq.astype(BF16)
    if qg is None:
        dk = dot_tn(ds4b[:, 0:144], q4) * SCALE
    else:
        dk = by_keys(qg.T, ds4b) * SCALE
    dqkv_ref[:, 512 + 128 * g : 512 + 128 * (g + 1)] = dk.astype(BF16)


def finish_back(dqkv_ref, wqkv_ref, n, rstd, gain, g32, dgain_ref):
    dh = dot_nt(dqkv_ref[...], wqkv_ref[0])
    dgain_ref[...] = jnp.sum(dh * n, axis=0, keepdims=True)
    dn = dh * gain
    return (
        rstd
        * (
            dn
            - jnp.mean(dn, axis=-1, keepdims=True)
            - n * jnp.mean(dn * n, axis=-1, keepdims=True)
        )
        + g32
    )


def weight_terms(idx_ref, h, o, dqkv, g, keep_ref, send_ref):
    core = idx_ref[0]
    p = lax.broadcasted_iota(jnp.int32, (256, 512), 0)
    row = lax.broadcasted_iota(jnp.int32, (256, 512), 1)
    bit = lambda k: (p >> k) & 1
    hz, h2, h3 = bit(6), bit(4), bit(2)
    z1 = h3 ^ (hz & h2)
    place = (
        (8, bit(3)),
        (7, bit(5)),
        (6, bit(7) ^ bit(5)),
        (5, h2 ^ (hz & (h2 ^ h3))),
        (4, z1),
        (3, z1 ^ hz),
    )
    base = p & 3
    for to, value in place:
        base = base + (value << to)
    for which, ref in ((core, keep_ref), (1 - core, send_ref)):
        pick = jnp.where(row == base + which * 4, 1.0, 0.0).astype(BF16)
        ht = dot_nt(pick, h).astype(BF16)
        ot = dot_nt(pick, o).astype(BF16)
        ref[:, 0:1536] = dot(ht, dqkv).astype(BF16)
        ref[:, 1536:2048] = dot(ot, g).astype(BF16)


def store_pieces(out, *refs):
    for k, ref in enumerate(refs):
        ref[...] = out[40 * k : 40 * (k + 1)].astype(BF16)


def load_pieces(cols, *refs):
    return jnp.concatenate([ref[:, cols].astype(F32) for ref in refs], axis=0).astype(BF16)


def first_kernel(
    x_hbm, go_hbm, grp_hbm, gain_hbm, wqkv_hbm, wproj_hbm, tab_hbm, rel_hbm, const_hbm,
    own_ref, lon_ref, lat_ref, dia_ref, rstd_ref, n_hbm, qkv_hbm, p_hbm, o_hbm,
    n_ref, qkv_ref, p_ref, o_ref, cells, gs, pay, bias_ref, main_ref, tail_ref, words, scales, offsets,
    x_ref, go_ref, grp_ref, gain_ref, wqkv_ref, wproj_ref, tab_ref, rel_ref, const_ref, sems,
):
    sources = [
        (rel_hbm, rel_ref),
        (tab_hbm.at[0, lax.axis_index("yl")], tab_ref),
        (const_hbm, const_ref),
        (x_hbm, x_ref),
        (go_hbm, go_ref),
        (grp_hbm, grp_ref),
        (gain_hbm, gain_ref),
        (wqkv_hbm.at[0], wqkv_ref),
        (wproj_hbm.at[0], wproj_ref),
    ]
    copies = [pltpu.make_async_copy(a, b, sems.at[k]) for k, (a, b) in enumerate(sources)]
    for copy in copies:
        copy.start()
    results = []

    def send(source, target):
        copy = pltpu.make_async_copy(source, target, sems.at[9 + len(results)])
        copy.start()
        results.append(copy)

    for copy in copies[0:3]:
        copy.wait()
    px, ps, pm = [const_ref[k, 0 : (144, 160, 144)[k], 0:144] for k in range(3)]
    rows, cols = const_ref[3, 0:144, 0:12], const_ref[4, 0:144, 0:12]

    frame_ids(rel_ref[...], pm, main_ref, tail_ref)
    fill_bias(tab_ref[...], main_ref, tail_ref, words, scales, offsets, bias_ref)

    masks = lane_masks()
    for copy in copies[3:8]:
        copy.wait()
    for k in range(72):
        cells[2 * k : 2 * k + 2, 0:512] = x_ref[k].astype(F32)
        cells[2 * k : 2 * k + 2, 512:1024] = go_ref[k].astype(F32)
    both = dot(px, cells[...].astype(BF16))
    x = both[:, 0:512]
    pay[:, 512:1024] = both[:, 512:1024].astype(BF16)
    for r in range(6):
        gs[2 * r : 2 * r + 2, :] = grp_ref[r].astype(F32)
    picked = dot(rows, gs[...].astype(BF16)) * cols.astype(F32)
    group = jnp.sum(picked, axis=-1, keepdims=True)
    spots = (group * const_ref[6, 0:144, 0:128].astype(F32)).astype(BF16)
    group_rows = dot(const_ref[5, :, 0:144], spots)

    n, rstd = normalize(x)
    n_ref[...] = n
    send(n_ref, n_hbm)
    rstd_ref[...] = rstd
    h = (n * gain_ref[0:1, :]).astype(BF16)
    qkv_ref[...] = dot(h, wqkv_ref[...]).astype(BF16)
    send(qkv_ref, qkv_hbm)
    for g in range(4):
        biases = [bias_ref[576 * g + 144 * k : 576 * g + 144 * (k + 1), :] for k in range(4)]
        _, _, p4 = group_probs(qkv_ref, g, masks, biases, None)
        p4b = p4.astype(BF16)
        p_ref[576 * g : 576 * (g + 1), :] = p4b
        send(p_ref.at[576 * g : 576 * (g + 1)], p_hbm.at[576 * g : 576 * (g + 1)])
        vg = pad_keys(qkv_ref[:, 1024 + 128 * g : 1024 + 128 * (g + 1)])
        o_ref[:, 128 * g : 128 * (g + 1)] = fold_heads(dot(p4b, vg), masks).astype(BF16)
    send(o_ref, o_hbm)
    copies[8].wait()
    pay[:, 0:512] = (x + dot(o_ref[...], wproj_ref[...])).astype(BF16)
    out = dot(ps, pay[...])
    out = jnp.concatenate([out[:, 0:128] + group_rows, out[:, 128:1024]], axis=1)
    store_pieces(out, own_ref, lon_ref, lat_ref, dia_ref)
    for copy in results:
        copy.wait()


def bias_kernel(
    idx_ref, tab_ref, rel_ref, pm_ref, out_ref, main_ref, tail_ref, words, scales, offsets
):
    frame_ids(rel_ref[...], pm_ref[0:144, 0:144], main_ref, tail_ref)
    fill_bias(tab_ref[0, idx_ref[1]], main_ref, tail_ref, words, scales, offsets, out_ref)


def second_kernel(
    idx_ref, own_ref, lon_ref, lat_ref, dia_ref, gain_ref, wqkv_ref, wproj_ref, bias_ref,
    const_ref,
    oown_ref, olon_ref, olat_ref, odia_ref, h_ref, o_ref, dqkv_ref, g_ref, dgain_ref, ds0_ref, ds1_ref,
    qkv_ref, back,
):
    masks = lane_masks()
    flags = const_ref[2, 0:144, 0:2].astype(F32)
    pieces = load_pieces(slice(0, 1024), own_ref, lon_ref, lat_ref, dia_ref)
    frame = dot(const_ref[0, 0:144, 0:160], pieces)
    group = dot(const_ref[3, 0:144, 0:160], pieces[:, 0:128]) * const_ref[4, 0:144, 0:128].astype(F32)
    group = jnp.sum(group, axis=-1, keepdims=True)
    x = frame[:, 0:512]
    g32 = frame[:, 512:1024]
    gb = g32.astype(BF16)
    g_ref[...] = gb
    lat = idx_ref[1].astype(F32)
    key = group * 4.0 + flags[:, 1:2] * (2.0 * lat) + flags[:, 0:1]
    eye = lax.broadcasted_iota(jnp.int32, (144, 256), 0) == lax.broadcasted_iota(
        jnp.int32, (144, 256), 1
    )
    key_row = jnp.sum(jnp.where(eye, key, 0.0), axis=0, keepdims=True)
    allowed = key == key_row
    gain = gain_ref[1:2, :]

    n, rstd = normalize(x)
    h = (n * gain).astype(BF16)
    h_ref[...] = h
    qkv_ref[...] = dot(h, wqkv_ref[0]).astype(BF16)
    do = dot_nt(gb, wproj_ref[0]).astype(BF16)
    for g in range(4):
        biases = [bias_ref[576 * g + 144 * k : 576 * g + 144 * (k + 1), :] for k in range(4)]
        q4, kg, p4 = group_probs(qkv_ref, g, masks, biases, allowed)
        p4b = p4.astype(BF16)
        vg = pad_keys(qkv_ref[:, 1024 + 128 * g : 1024 + 128 * (g + 1)])
        o_ref[:, 128 * g : 128 * (g + 1)] = fold_heads(dot(p4b, vg), masks).astype(BF16)
        group_back(g, None, q4, kg, vg, p4, p4b, do, masks, dqkv_ref, ds0_ref, ds1_ref)
    back[:, 0:512] = (x + dot(o_ref[...], wproj_ref[0])).astype(BF16)
    df = finish_back(dqkv_ref, wqkv_ref, n, rstd, gain, g32, dgain_ref)
    back[:, 512:1024] = df.astype(BF16)
    store_pieces(dot(const_ref[1, :, 0:144], back[...]), oown_ref, olon_ref, olat_ref, odia_ref)


def weights_kernel(idx_ref, h_ref, o_ref, dqkv_ref, g_ref, keep_ref, send_ref):
    weight_terms(idx_ref, h_ref[...], o_ref[...], dqkv_ref[...], g_ref[...], keep_ref, send_ref)


def third_kernel(
    idx_ref, own_ref, lon_ref, lat_ref, dia_ref, gain_ref, wproj_ref,
    n_ref, qkv_ref, p_ref, o_ref, const_ref, after_ref,
    g_ref, dqkv_ref, ds0_ref, ds1_ref, keep_ref, send_ref,
):
    masks = lane_masks()
    pieces = load_pieces(slice(512, 1024), own_ref, lon_ref, lat_ref, dia_ref)
    gb = dot(const_ref[0, 0:144, 0:160], pieces).astype(BF16)
    g_ref[...] = gb
    do = dot_nt(gb, wproj_ref[0]).astype(BF16)
    for g in range(4):
        q4 = stack_heads(qkv_ref[:, 128 * g : 128 * (g + 1)], masks)
        kg = pad_keys(qkv_ref[:, 512 + 128 * g : 512 + 128 * (g + 1)])
        vg = pad_keys(qkv_ref[:, 1024 + 128 * g : 1024 + 128 * (g + 1)])
        p4b = p_ref[576 * g : 576 * (g + 1), :]
        group_back(g, qkv_ref[:, 128 * g : 128 * (g + 1)], q4, kg, vg, p4b.astype(F32), p4b, do, masks, dqkv_ref, ds0_ref, ds1_ref)
    h = (n_ref[...] * gain_ref[0:1, :]).astype(BF16)
    weight_terms(idx_ref, h, o_ref[...], dqkv_ref[...], gb, keep_ref, send_ref)


def finish_kernel(
    own_ref, lon_ref, lat_ref, dia_ref, gain_ref, wqkv_ref, n_ref, rstd_ref, g_ref, dqkv_ref,
    const_ref, after_ref, out_ref, gin_ref, dgain_ref, outs,
):
    pieces = load_pieces(slice(0, 512), own_ref, lon_ref, lat_ref, dia_ref)
    outs[:, 0:512] = dot(const_ref[0, 0:144, 0:160], pieces)
    df = finish_back(
        dqkv_ref, wqkv_ref, n_ref[...], rstd_ref[...], gain_ref[0:1, :], g_ref[...].astype(F32), dgain_ref
    )
    outs[:, 512:1024] = dot(const_ref[1, 0:144, 0:144], df.astype(BF16))
    for k in range(72):
        out_ref[k] = outs[2 * k : 2 * k + 2, 0:512].astype(BF16)
        gin_ref[k] = outs[2 * k : 2 * k + 2, 512:1024].astype(BF16)


def scatter_kernel(
    idx_ref, main_ref, tail_ref, m0_ref, t0_ref, gain0_ref, m1_ref, t1_ref, gain1_ref, after_ref,
    keep_ref, send_ref,
):
    iota = lax.broadcasted_iota(jnp.int32, (128, 256), 0)

    def add(ids_ref, d_refs, stride, unroll):
        def body(i, acc):
            ids = jnp.concatenate([ids_ref[pl.ds(2 * i + k, 1), :] for k in range(2)], axis=1)
            low, high = ids & 127, ids >> 7
            hot = jnp.where(iota == low, 1.0, 0.0).astype(BF16)
            lhs = []
            for d_ref in d_refs:
                d = jnp.concatenate(
                    [d_ref[pl.ds(2 * i + k, 16, stride=stride), :] for k in range(2)], axis=1
                )
                lhs += [jnp.where(high == k, d, 0.0) for k in range(6)]
            return acc + dot_nt(jnp.concatenate(lhs, axis=0).astype(BF16), hot)

        return lambda acc: lax.fori_loop(0, stride // 2, body, acc, unroll=unroll)

    acc = add(main_ref, (m0_ref, m1_ref), 144, 8)(jnp.zeros((192, 128), F32))
    acc = add(tail_ref, (t0_ref, t1_ref), 24, 12)(acc)
    first = lax.broadcasted_iota(jnp.int32, (8, 256), 0) == 0
    for b, dgain_ref in enumerate((gain0_ref, gain1_ref)):
        table = [acc[96 * b + 16 * k : 96 * b + 16 * k + 16] for k in range(6)]
        table = jnp.concatenate(table, axis=1)
        halves = []
        for c in range(2):
            gain = jnp.where(first, dgain_ref[:, 256 * c : 256 * (c + 1)], 0.0)
            halves.append(jnp.concatenate([table[8 * c : 8 * (c + 1)], gain], axis=1))
        keep, send = pick(idx_ref[0], halves[0], halves[1])
        keep_ref[8 * b : 8 * b + 8, :] = keep
        send_ref[8 * b : 8 * b + 8, :] = send


CUTS = ((0, 384), (384, 768), (768, 1024))


def pick(flag, low, high):
    mine = flag == 0
    return jnp.where(mine, low, high), jnp.where(mine, high, low)


def core_kernel(
    idx_ref, k0_ref, r0_ref, k1_ref, r1_ref, ka_ref, sa_ref, kb_ref, sb_ref, kc_ref, sc_ref
):
    x0, z0, yl = idx_ref[2], idx_ref[3], idx_ref[1]
    for b, (k_ref, r_ref) in enumerate(((k0_ref, r0_ref), (k1_ref, r1_ref))):

        def total(r0, r1, c0, c1):
            return k_ref[r0:r1, c0:c1].astype(F32) + r_ref[r0:r1, c0:c1].astype(F32)

        for s in range(2):
            a0 = 1024 * s
            keep, send = pick(x0, total(0, 128, a0, a0 + 384), total(128, 256, a0, a0 + 384))
            to = 768 * b + 384 * s
            ka_ref[:, to : to + 384] = keep.astype(BF16)
            sa_ref[:, to : to + 384] = send.astype(BF16)
            to = 512 * b + 256 * s
            for h in range(2):
                r = 128 * h
                keep, send = pick(
                    z0,
                    total(r, r + 64, a0 + 768, a0 + 1024),
                    total(r + 64, r + 128, a0 + 768, a0 + 1024),
                )
                kc_ref[64 * h : 64 * h + 64, to : to + 256] = keep.astype(BF16)
                sc_ref[64 * h : 64 * h + 64, to : to + 256] = send.astype(BF16)
        keep, send = pick(yl, total(0, 256, 384, 768), total(0, 256, 1408, 1792))
        kb_ref[:, 384 * b : 384 * (b + 1)] = keep.astype(BF16)
        sb_ref[:, 384 * b : 384 * (b + 1)] = send.astype(BF16)


def step_two_kernel(
    idx_ref, ka_ref, ra_ref, kb_ref, rb_ref, kc_ref, rc_ref, t_ref, u_ref,
    nka_ref, nsa_ref, nkb_ref, nsb_ref, nkc_ref, nsc_ref, tk_ref,
):
    x0, z0, yl = idx_ref[2], idx_ref[3], idx_ref[1]
    a = ka_ref[...].astype(F32) + ra_ref[...].astype(F32)
    for b in range(2):
        keep, send = pick(yl, a[:, 768 * b : 768 * b + 384], a[:, 768 * b + 384 : 768 * b + 768])
        nka_ref[:, 384 * b : 384 * (b + 1)] = keep.astype(BF16)
        nsa_ref[:, 384 * b : 384 * (b + 1)] = send.astype(BF16)
    m = kb_ref[...].astype(F32) + rb_ref[...].astype(F32)
    for h in range(2):
        keep, send = pick(z0, m[128 * h : 128 * h + 64], m[128 * h + 64 : 128 * h + 128])
        nkb_ref[64 * h : 64 * h + 64, :] = keep.astype(BF16)
        nsb_ref[64 * h : 64 * h + 64, :] = send.astype(BF16)
    c = kc_ref[...].astype(F32) + rc_ref[...].astype(F32)
    keep, send = pick(x0, c[0:64], c[64:128])
    nkc_ref[...] = keep.astype(BF16)
    nsc_ref[0:64, :] = send.astype(BF16)
    table = (t_ref[...] + u_ref[...]).astype(BF16)
    tk_ref[...] = table
    nsc_ref[64:80, :] = table


def step_three_kernel(
    idx_ref, ka_ref, ra_ref, kb_ref, rb_ref, kc_ref, rc_ref, tk_ref,
    nka_ref, nsa_ref, nkb_ref, nsb_ref, nkc_ref, nsc_ref, ntk_ref,
):
    x0, z0, yl = idx_ref[2], idx_ref[3], idx_ref[1]
    a = ka_ref[...].astype(F32) + ra_ref[...].astype(F32)
    keep, send = pick(z0, a[0:64], a[64:128])
    nka_ref[...] = keep.astype(BF16)
    nsa_ref[0:64, :] = send.astype(BF16)
    t = tk_ref[...].astype(F32) + rc_ref[64:80, :].astype(F32)
    gains = jnp.concatenate([t[0:8, 768:1024], t[8:16, 768:1024], jnp.zeros((8, 256), F32)], axis=1)
    table = jnp.concatenate([t[:, 0:768], gains, jnp.zeros((8, 768), F32)], axis=0).astype(BF16)
    ntk_ref[...] = table
    nsa_ref[64:96, :] = table
    m = kb_ref[...].astype(F32) + rb_ref[...].astype(F32)
    keep, send = pick(x0, m[0:64], m[64:128])
    nkb_ref[...] = keep.astype(BF16)
    nsb_ref[...] = send.astype(BF16)
    c = kc_ref[...].astype(F32) + rc_ref[0:64, :].astype(F32)
    for b in range(2):
        keep, send = pick(yl, c[:, 512 * b : 512 * b + 256], c[:, 512 * b + 256 : 512 * b + 512])
        nkc_ref[:, 256 * b : 256 * (b + 1)] = keep.astype(BF16)
        nsc_ref[:, 256 * b : 256 * (b + 1)] = send.astype(BF16)


def spread_kernel(
    idx_ref, ka_ref, ra_ref, kb_ref, rb_ref, kc_ref, rc_ref, tk_ref, *refs
):
    outs, scr = refs[0:4], refs[4]
    a = ka_ref[...].astype(F32) + ra_ref[0:64, :].astype(F32)
    m = kb_ref[...].astype(F32) + rb_ref[...].astype(F32)
    c = kc_ref[...].astype(F32) + rc_ref[...].astype(F32)
    table = tk_ref[...].astype(F32) + ra_ref[64:96, :].astype(F32)
    gains = jnp.concatenate([table[16:24, 0:256], table[16:24, 256:512]], axis=0)
    table = jnp.concatenate([table[0:16], gains], axis=1)
    table = jnp.concatenate([table[0:8], table[8:16]], axis=1).astype(BF16)
    full = []
    for b in range(2):
        cols = slice(384 * b, 384 * (b + 1))
        full += [a[:, cols], m[:, cols], c[:, 256 * b : 256 * (b + 1)]]
    full = jnp.concatenate(full, axis=1).astype(BF16)
    for k in range(4):
        scr[k] = full[16 * k : 16 * k + 16]
    for f in range(4):
        outs[f][0:16, :] = scr[idx_ref[4] ^ f]
        outs[f][16:24, :] = table


def plane_kernel(idx_ref, own_ref, g1_ref, g2_ref, g3_ref, *refs):
    outs, tabs, scr = refs[0:4], refs[4], refs[5]
    got = (own_ref, g1_ref, g2_ref, g3_ref)
    total = got[0][0:16, :].astype(F32)
    for g in got[1:]:
        total = total + g[0:16, :].astype(F32)
    for f in range(4):
        tabs[idx_ref[4] ^ f] = got[f][16:24, :].astype(F32)
    table = tabs[0] + tabs[1] + tabs[2] + tabs[3]
    table = jnp.concatenate([table[:, 0:1024], table[:, 1024:2048]], axis=0)
    for k in range(4):
        rows = total[4 * k : 4 * k + 4]
        rows = jnp.concatenate([rows[:, 0:1024], rows[:, 1024:2048], table], axis=0)
        scr[k] = rows.astype(BF16)
    for f in range(4):
        outs[f][...] = scr[idx_ref[5] ^ f]


def close_kernel(idx_ref, own_ref, g1_ref, g2_ref, g3_ref, out_ref, tab_ref, scr):
    for f, g in enumerate((own_ref, g1_ref, g2_ref, g3_ref)):
        scr[idx_ref[5] ^ f] = g[...].astype(F32)
    total = scr[0] + scr[1] + scr[2] + scr[3]
    out_ref[...] = total.astype(BF16)
    tab_ref[...] = total[8:24].astype(BF16)


def last_kernel(
    factor, idx_ref, own_ref, lat_ref, core_ref, dia_ref, gain_ref, qkv_ref, proj_ref, bias_ref
):
    core, yl = idx_ref[0], idx_ref[1]
    own = own_ref[...].astype(F32) * factor
    got = lat_ref[...].astype(F32) * factor
    low, high = pick(yl, own[0:8], got[0:8])
    for b in range(2):
        qkv_ref[b, :, 0:1024] = low[4 * b : 4 * b + 4]
        qkv_ref[b, :, 1024:1536] = high[4 * b : 4 * b + 4, 0:512]
        proj_ref[b, :, :] = high[4 * b : 4 * b + 4, 512:1024]
    near = pick(yl, own[8:24], got[8:24])
    far = pick(yl, core_ref[...].astype(F32) * factor, dia_ref[...].astype(F32) * factor)
    tabs = [pick(core, near[w], far[w]) for w in range(2)]
    for c in range(2):
        for w in range(2):
            for b in range(2):
                bias_ref[b, w, 8 * c : 8 * (c + 1), :] = tabs[w][c][8 * b : 8 * b + 8, 0:NREL]
        for b in range(2):
            gain_ref[b : b + 1, 256 * c : 256 * (c + 1)] = (
                tabs[0][c][8 * b : 8 * b + 1, 768:1024] + tabs[1][c][8 * b : 8 * b + 1, 768:1024]
            )


def _whole(shape):
    return pl.BlockSpec(shape, lambda *_: (0,) * len(shape))


SMEM = pl.BlockSpec(memory_space=pltpu.SMEM)


ANY = pl.BlockSpec(memory_space=pl.ANY)


HBM = pl.BlockSpec(memory_space=pltpu.HBM)


def call(body, us, outs, *args, specs=None, scratch=(), sems=0, vmem=VMEM, hbm_outs=()):
    specs = dict(specs or {})
    if args[0].dtype == jnp.int32 and args[0].ndim == 1:
        specs[0] = SMEM
    scratch = [pltpu.VMEM(s, t) for s, t in scratch]
    if sems:
        scratch.append(pltpu.SemaphoreType.DMA((sems,)))
    return pl.pallas_call(
        body,
        grid=(1,),
        in_specs=[specs.get(i, _whole(a.shape)) for i, a in enumerate(args)],
        out_specs=[HBM if k in hbm_outs else _whole(s) for k, (s, _) in enumerate(outs)],
        out_shape=[jax.ShapeDtypeStruct(s, t) for s, t in outs],
        scratch_shapes=scratch,
        compiler_params=pltpu.CompilerParams(vmem_limit_bytes=vmem),
        cost_estimate=pl.CostEstimate(
            flops=int(us * 1e9), bytes_accessed=int(us * 3.6e6), transcendentals=0
        ),
    )(*args)


def mask_of(axes):
    return sum(1 << (7 - AXES.index(a)) for a in axes)


def flip(value, *axes):
    return lax.ppermute(value, AXES, [(s, s ^ mask_of(axes)) for s in range(256)])


def z_step(value, move, *axes):
    pairs = [(s, (s & ~28 | move(s >> 2 & 7) << 2) ^ mask_of(axes)) for s in range(256)]
    return lax.ppermute(value, AXES, pairs)


def lon_step(value, offset, across):
    pairs = [(s, ((s // 2 + offset) % 128) * 2 + (s % 2 ^ across)) for s in range(256)]
    return lax.ppermute(value, AXES, pairs)


def halo(pieces, offset):
    own, lon, lat, dia = pieces
    return (
        own,
        lon_step(lon, offset, 0),
        flip(lat, "yl"),
        lon_step(dia, offset, 1),
    )


def on_device(inputs, grad_out, gains, qkv_weight, proj_weight, bias_table, rel_ids, groups):
    first_const, second_const, third_const, finish_const = [jnp.asarray(t) for t in TABLES]
    at = {a: lax.axis_index(a) for a in AXES}
    hz = at["z0"] ^ at["z1"]
    idx = jnp.stack(
        [
            at["c"],
            at["yl"],
            at["x0"] ^ at["x1"],
            hz,
            2 * at["x1"] + (at["z2"] ^ (hz & at["z1"])),
            2 * at["yh"] + (at["z1"] ^ (hz & (at["z1"] ^ at["z2"]))),
        ]
    ).astype(jnp.int32)
    x_cells, go_cells = [v.transpose(0, 2, 3, 1, 4).reshape(72, 2, D) for v in (inputs, grad_out)]

    def block(b, shape):
        return pl.BlockSpec((1,) + shape, lambda *_: (b,) + (0,) * len(shape))

    def weights(b, first):
        return {
            first: block(b, (D, 3 * D)),
            first + 1: block(b, (D, D)),
            first + 2: block(b, (2, HEADS, NREL)),
        }

    id_shapes = [((144, 128), jnp.int32), ((24, 128), jnp.int32)]
    tables = [((8, 768), jnp.int32), ((HEADS, 128), F32), ((HEADS, 128), F32)]
    piece = ((40, 1024), BF16)
    saved = [((144, D), F32), ((144, 3 * D), BF16), ((2304, 256), BF16), ((144, D), BF16)]
    own, lon, lat, dia, rstd0, n0, qkv0, p0, o0 = call(
        first_kernel,
        8,
        [piece] * 4
        + [
            ((144, 1), F32),
        ]
        + saved,
        x_cells, go_cells, groups.transpose(1, 0, 2), gains, qkv_weight, proj_weight, bias_table, rel_ids,
        first_const,
        specs={k: HBM for k in range(9)},
        scratch=saved
        + [((144, 1024), F32), ((12, 12), F32), ((144, 1024), BF16), ((2304, 256), F32)]
        + id_shapes
        + tables
        + [
            ((72, 2, D), BF16),
            ((72, 2, D), BF16),
            ((6, 2, 12), jnp.int32),
            ((2, D), F32),
            ((D, 3 * D), BF16),
            ((D, D), BF16),
            ((HEADS, NREL), F32),
            ((144, 144), jnp.int32),
            ((7, 160, 256), BF16),
        ],
        sems=16,
        hbm_outs=range(5, 9),
        vmem=57 << 20,
    )
    pieces = halo((own, lon, lat, dia), -1)
    bias1, ids, tails = call(
        bias_kernel,
        4,
        [((2304, 256), F32)] + id_shapes,
        idx, bias_table, rel_ids, jnp.asarray(TABLES[0][2]),
        specs={1: block(1, (2, HEADS, NREL))},
        scratch=tables,
    )
    ds_shapes = [((2304, 128), F32), ((384, 128), F32)]
    own, lon, lat, dia, h1, o1, dqkv1, g1, dgain1, ds10, ds11 = call(
        second_kernel,
        6,
        [piece] * 4
        + [
            ((144, D), BF16),
            ((144, D), BF16),
            ((144, 3 * D), BF16),
            ((144, D), BF16),
            ((1, D), F32),
        ]
        + ds_shapes,
        idx, *pieces, gains, qkv_weight, proj_weight, bias1, second_const,
        specs={6: block(1, (D, 3 * D)), 7: block(1, (D, D))},
        scratch=[((144, 3 * D), BF16), ((144, 2 * D), BF16)],
    )
    pieces = halo((own, lon, lat, dia), 1)
    wshape = ((256, 4 * D), BF16)
    keep1, send1 = call(weights_kernel, 2, [wshape] * 2, idx, h1, o1, dqkv1, g1)
    recv1 = flip(send1, "c")

    def pairs(*shapes):
        return [(s, BF16) for shape in shapes for s in shape]

    cells = ((72, 2, D), BF16)
    g0, dqkv0, ds00, ds01, keep0, send0 = call(
        third_kernel,
        4,
        [((144, D), BF16), ((144, 3 * D), BF16)] + ds_shapes + [wshape, wshape],
        idx, *pieces, gains, proj_weight, n0, qkv0, p0, o0, third_const, keep1,
        specs={6: block(0, (D, D)), 12: ANY},
    )
    recv0 = flip(send0, "c")
    outputs, grad_inputs, dgain0 = call(
        finish_kernel,
        2,
        [cells, cells, ((1, D), F32)],
        *pieces, gains, qkv_weight, n0, rstd0, g0, dqkv0, finish_const, keep0,
        specs={5: block(0, (D, 3 * D)), 11: ANY},
        scratch=[((144, 2 * D), F32)],
    )
    outputs, grad_inputs = [
        v.reshape(1, 6, 12, 2, D).transpose(0, 3, 1, 2, 4) for v in (outputs, grad_inputs)
    ]
    ka, sa, kb, sb, kc, sc = call(
        core_kernel,
        1,
        pairs([(128, 1536)] * 2, [(256, 768)] * 2, [(128, 1024)] * 2),
        idx, keep0, recv0, keep1, recv1,
    )
    ra, rb, rc = flip(sa, "x0"), flip(sb, "yl"), flip(sc, "z0")
    tshape = ((16, 1024), F32)
    tkeep, tsend = call(
        scatter_kernel,
        6,
        [tshape] * 2,
        idx, ids, tails, ds00, ds01, dgain0, ds10, ds11, dgain1, ka,
        specs={9: ANY},
    )
    trecv = flip(tsend, "c")
    ka, sa, kb, sb, kc, sc, tk = call(
        step_two_kernel,
        1,
        pairs([(128, 768)] * 4, [(64, 1024), (80, 1024)], [(16, 1024)]),
        idx, ka, ra, kb, rb, kc, rc, tkeep, trecv,
    )
    ra, rb, rc = flip(sa, "yl"), flip(sb, "z0"), flip(sc, "x0")
    ka, sa, kb, sb, kc, sc, tk = call(
        step_three_kernel,
        1,
        pairs([(64, 768), (96, 768)], [(64, 768)] * 2, [(64, 512)] * 2, [(32, 768)]),
        idx, ka, ra, kb, rb, kc, rc, tk,
    )
    ra, rb, rc = flip(sa, "z0"), flip(sb, "x0"), flip(sc, "yl")
    parts = call(
        spread_kernel,
        1,
        [((24, 2048), BF16)] * 4,
        idx, ka, ra, kb, rb, kc, rc, tk,
        scratch=[((4, 16, 2048), BF16)],
    )
    near = lambda z: (z + 1) % 8 if z & 1 else (z - 1) % 8
    far = lambda z: z ^ (7 if (z ^ z >> 1) & 1 else 3)
    parts = call(
        plane_kernel,
        1,
        [((24, 1024), BF16)] * 4,
        idx, parts[0], z_step(parts[1], near), flip(parts[2], "x1", "x0"),
        z_step(parts[3], near, "x1", "x0"),
        scratch=[((4, 8, 2048), F32), ((4, 24, 1024), BF16)],
    )
    own, tab = call(
        close_kernel,
        1,
        [((24, 1024), BF16), ((16, 1024), BF16)],
        idx, parts[0], z_step(parts[1], far), flip(parts[2], "yh"), z_step(parts[3], far, "yh"),
        scratch=[((4, 24, 1024), F32)],
    )
    from_core = flip(tab, "c")
    from_dia = flip(tab, "c", "yl")
    from_lat = flip(own, "yl")
    factor = 36864 ** (-0.5)
    grad_gains, grad_qkv, grad_proj, grad_bias = call(
        functools.partial(last_kernel, factor),
        1,
        [
            ((2, D), F32),
            ((2, 4, 3 * D), F32),
            ((2, 4, D), F32),
            ((2, 2, HEADS, NREL), F32),
        ],
        idx, own, from_lat, from_core, from_dia,
    )
    return (outputs, grad_inputs, grad_gains, grad_qkv, grad_proj, grad_bias)


def solution(mesh):
    fine = Mesh(mesh.devices.reshape((2,) * 8), AXES)
    lon = AXES[:7]
    field = P(None, None, "yl", lon, None)
    rows = P(None, lon, None)
    return jax.shard_map(
        on_device,
        mesh=fine,
        in_specs=(field, field, P(), P(), P(), P(), P(), P(None, "yl", lon)),
        out_specs=(field, field, P(), rows, rows, P()),
        check_vma=False,
    )
```

```python
import functools

import jax
import jax.numpy as jnp
import numpy as np
from jax import lax
from jax.experimental import pallas as pl
from jax.experimental.pallas import tpu as pltpu
from jax.sharding import Mesh, PartitionSpec as P

F32 = jnp.float32
BF16 = jnp.bfloat16
EPSILON = 1e-05
NEGATIVE = -1e30
D = 512
HEADS = 16
NREL = 759
SCALE = 32 ** (-0.5)
AXES = ("yh", "x1", "x0", "z2", "z1", "z0", "c", "yl")
VMEM = 24 << 20

QUADS = ((1, 1), (1, 0), (0, 1), (0, 0))


def _token(rh, ch, l, r, c):
    return (rh * 2 + ch) * 36 + l * 18 + r * 6 + c


def _tables():
    px = np.zeros((144, 144), np.float32)
    ps = np.zeros((160, 144), np.float32)
    pf = np.zeros((144, 160), np.float32)
    pm = np.zeros((144, 144), np.float32)
    rows = np.zeros((144, 12), np.float32)
    cols = np.zeros((144, 12), np.float32)
    flags = np.zeros((144, 2), np.float32)
    into = np.zeros((160, 144), np.float32)
    spot = np.zeros((144, 128), np.float32)
    back = np.zeros((144, 160), np.float32)
    seat = np.zeros((144, 128), np.float32)
    for l in range(2):
        for row in range(6):
            for col in range(12):
                rh, r, ch, c = row // 3, row % 3, col // 6, col % 6
                t = _token(rh, ch, l, r, c)
                px[t, (row * 12 + col) * 2 + l] = 1
                pm[t, l * 72 + row * 12 + col] = 1
                rows[t, row * 2 + l] = 1
                cols[t, col] = 1
                flags[t] = (l, rh)
                k = QUADS.index((rh, ch))
                i = (1 - l) * 18 + r * 6 + c
                ps[40 * k + i, t] = 1
                into[40 * k + 36, t] = 1
                spot[t, i] = 1
    for k in range(4):
        for i in range(36):
            t = 36 * k + i
            pf[t, 40 * k + i] = 1
            back[t, 40 * k + 36] = 1
            seat[t, i] = 1
    first = (px, ps, pm, rows, cols, into, spot)
    second = (pf, pf.T, flags, back, seat)
    return first, second, (ps.T,), (px.T @ ps.T, px.T)


def stacked(parts):
    out = np.zeros((len(parts), 160, 256), np.float32)
    for k, part in enumerate(parts):
        out[k, : part.shape[0], : part.shape[1]] = part
    return out.astype(jnp.bfloat16)


TABLES = [stacked(group) for group in _tables()]


def dot(a, b):
    return lax.dot_general(a, b, (((1,), (0,)), ((), ())), preferred_element_type=F32)


def dot_nt(a, b):
    return lax.dot_general(a, b, (((1,), (1,)), ((), ())), preferred_element_type=F32)


def dot_tn(a, b):
    return lax.dot_general(a, b, (((0,), (0,)), ((), ())), preferred_element_type=F32)


def lane_masks():
    lane = lax.broadcasted_iota(jnp.int32, (1, 128), 1) >> 5
    return [jnp.where(lane == k, 1.0, 0.0).astype(F32) for k in range(4)]


def stack_heads(group, masks):
    return jnp.concatenate([group * m.astype(BF16) for m in masks], axis=0)


def fold_heads(stacked, masks):
    total = stacked[0:144] * masks[0]
    for k in range(1, 4):
        total = total + stacked[144 * k : 144 * (k + 1)] * masks[k]
    return total


def pad_keys(group):
    return jnp.concatenate([group, jnp.zeros((112, 128), BF16)], axis=0)


def normalize(x):
    center = x - jnp.mean(x, axis=-1, keepdims=True)
    rstd = lax.rsqrt(jnp.mean(center * center, axis=-1, keepdims=True) + EPSILON)
    return center * rstd, rstd


def pack_table(tab, words, scales, offsets):
    low = jnp.min(tab, axis=-1, keepdims=True)
    scale = jnp.maximum(jnp.max(tab, axis=-1, keepdims=True) - low, 1e-20) * (1.0 / 65535.0)
    q = jnp.clip(jnp.floor((tab - low) / scale + 0.5), 0.0, 65535.0).astype(jnp.int32)
    high = jnp.concatenate([q[4 * g : 4 * g + 2] for g in range(4)], axis=0)
    rest = jnp.concatenate([q[4 * g + 2 : 4 * g + 4] for g in range(4)], axis=0)
    words[...] = jnp.zeros((8, 768), jnp.int32)
    words[:, 0:NREL] = ((high - 32768) << 16) + rest
    signed = lax.broadcasted_iota(jnp.int32, (HEADS, 1), 0) & 3
    offset = low + jnp.where(signed < 2, 32768.0, 0.0) * scale
    scales[...] = jnp.broadcast_to(scale, (HEADS, 128))
    offsets[...] = jnp.broadcast_to(offset, (HEADS, 128))


def lookup(row, ids):
    acc = None
    for k in range(6):
        part = jnp.broadcast_to(row[:, 128 * k : 128 * (k + 1)], ids.shape)
        got = jnp.take_along_axis(part, ids & 127, axis=1)
        acc = got if k == 0 else jnp.where((ids >> 7) == k, got, acc)
    return acc


def side_by_side(tail):
    total = tail[0:24]
    for k in range(1, 6):
        total = total + pltpu.roll(tail[24 * k : 24 * (k + 1)], 16 * k, 1)
    return total


def bias_pair(m, words, scales, offsets, ids, tails):
    row = words[m : m + 1, :]
    main = lookup(row, ids)
    tail = lookup(row, tails)
    parts = [tail] + [pltpu.roll(tail, 128 - 16 * k, 1) for k in range(1, 6)]
    tail = jnp.concatenate(parts, axis=0)
    lane = lax.broadcasted_iota(jnp.int32, (144, 128), 1)
    head = 4 * (m // 2) + m % 2
    out = []
    for h, take in ((head, lambda w: w >> 16), (head + 2, lambda w: w & 65535)):
        scale, offset = scales[h : h + 1, :], offsets[h : h + 1, :]
        a = take(main).astype(F32) * scale + offset
        b = jnp.where(lane < 16, take(tail).astype(F32) * scale + offset, NEGATIVE)
        out.append(jnp.concatenate([a, b], axis=1))
    return out


def frame_ids(rel, pm, main_ref, tail_ref):
    parts = []
    for part in (rel >> 5, rel & 31):
        half = dot(pm, part.astype(F32).astype(BF16)).astype(BF16)
        parts.append(dot_nt(half, pm).astype(jnp.int32))
    ids = parts[0] * 32 + parts[1]
    main_ref[...] = ids[:, 0:128]
    tail = jnp.concatenate([ids[:, 128:144], jnp.zeros((144, 112), jnp.int32)], axis=1)
    tail_ref[...] = side_by_side(tail)


def fill_bias(table, main_ref, tail_ref, words, scales, offsets, store):
    pack_table(table, words, scales, offsets)
    ids, tails = main_ref[...], tail_ref[...]
    for m in range(8):
        head = 4 * (m // 2) + m % 2
        for h, b in zip((head, head + 2), bias_pair(m, words, scales, offsets, ids, tails)):
            store[144 * h : 144 * (h + 1), :] = b


def group_probs(qkv_ref, g, masks, biases, allowed):
    qg = qkv_ref[:, 128 * g : 128 * (g + 1)]
    kg = pad_keys(qkv_ref[:, 512 + 128 * g : 512 + 128 * (g + 1)])
    q4 = stack_heads(qg, masks)
    s4 = dot_nt(q4, kg) * SCALE
    out = []
    for k in range(4):
        s = s4[144 * k : 144 * (k + 1)] + biases[k]
        if allowed is not None:
            s = jnp.where(allowed, s, NEGATIVE)
        e = jnp.exp(s - jnp.max(s, axis=-1, keepdims=True))
        out.append(e * (1.0 / jnp.sum(e, axis=-1, keepdims=True)))
    return q4, kg, jnp.concatenate(out, axis=0)


def by_keys(left, right):
    parts = [dot(left[32 * k : 32 * k + 32], right[144 * k : 144 * k + 144]) for k in range(4)]
    return jnp.concatenate(parts, axis=0).T[0:144]


def by_rows(left, right):
    parts = [dot_nt(left[32 * k : 32 * k + 32], right[144 * k : 144 * k + 144]) for k in range(4)]
    return jnp.concatenate(parts, axis=0).T


def group_back(g, qg, q4, kg, vg, p4, p4b, do, masks, dqkv_ref, ds0_ref, ds1_ref):
    do4 = stack_heads(do[:, 128 * g : 128 * (g + 1)], masks)
    dp4 = dot_nt(do4, vg)
    if qg is None:
        dv = dot_tn(p4b[:, 0:144], do4)
    else:
        dv = by_keys(do[:, 128 * g : 128 * (g + 1)].T, p4b)
    dqkv_ref[:, 1024 + 128 * g : 1024 + 128 * (g + 1)] = dv.astype(BF16)
    ds4 = p4 * (dp4 - jnp.sum(dp4 * p4, axis=-1, keepdims=True))
    ds0_ref[576 * g : 576 * (g + 1), :] = ds4[:, 0:128]
    for k in range(4):
        at = 24 * (4 * g + k)
        ds1_ref[at : at + 24, :] = side_by_side(ds4[144 * k : 144 * (k + 1), 128:256])
    ds4b = ds4.astype(BF16)
    dq = fold_heads(dot(ds4b, kg), masks) * SCALE
    dqkv_ref[:, 128 * g : 128 * (g + 1)] = dq.astype(BF16)
    if qg is None:
        dk = dot_tn(ds4b[:, 0:144], q4) * SCALE
    else:
        dk = by_keys(qg.T, ds4b) * SCALE
    dqkv_ref[:, 512 + 128 * g : 512 + 128 * (g + 1)] = dk.astype(BF16)


def finish_back(dqkv_ref, wqkv_ref, n, rstd, gain, g32, dgain_ref):
    dh = dot_nt(dqkv_ref[...], wqkv_ref[0])
    dgain_ref[...] = jnp.sum(dh * n, axis=0, keepdims=True)
    dn = dh * gain
    return (
        rstd
        * (
            dn
            - jnp.mean(dn, axis=-1, keepdims=True)
            - n * jnp.mean(dn * n, axis=-1, keepdims=True)
        )
        + g32
    )


def weight_terms(which, *targets):
    p = lax.broadcasted_iota(jnp.int32, (256, 512), 0)
    row = lax.broadcasted_iota(jnp.int32, (256, 512), 1)
    bit = lambda k: (p >> k) & 1
    hz, h2, h3 = bit(6), bit(4), bit(2)
    z1 = h3 ^ (hz & h2)
    place = (
        (8, bit(3)),
        (7, bit(5)),
        (6, bit(7) ^ bit(5)),
        (5, h2 ^ (hz & (h2 ^ h3))),
        (4, z1),
        (3, z1 ^ hz),
    )
    base = p & 3
    for to, value in place:
        base = base + (value << to)
    pick = jnp.where(row == base + which * 4, 1.0, 0.0).astype(BF16)
    for h, o, dqkv, g, ref in targets:
        ht = dot_nt(pick, h).astype(BF16)
        ot = dot_nt(pick, o).astype(BF16)
        ref[:, 0:1536] = dot(ht, dqkv).astype(BF16)
        ref[:, 1536:2048] = dot(ot, g).astype(BF16)


def store_pieces(out, *refs):
    for k, ref in enumerate(refs):
        ref[...] = out[40 * k : 40 * (k + 1)].astype(BF16)


def load_pieces(cols, *refs):
    return jnp.concatenate([ref[:, cols].astype(F32) for ref in refs], axis=0).astype(BF16)


def first_kernel(
    x_hbm, go_hbm, grp_hbm, gain_hbm, wqkv_hbm, wproj_hbm, tab_hbm, rel_hbm, const_hbm,
    own_ref, lon_ref, lat_ref, dia_ref, rstd_ref, n_hbm, qkv_hbm, p_hbm, o_hbm,
    n_ref, qkv_ref, p_ref, o_ref, cells, gs, pay, bias_ref, main_ref, tail_ref, words, scales, offsets,
    x_ref, go_ref, grp_ref, gain_ref, wqkv_ref, wproj_ref, tab_ref, rel_ref, const_ref, sems,
):
    sources = [
        (rel_hbm, rel_ref),
        (tab_hbm.at[0, lax.axis_index("yl")], tab_ref),
        (const_hbm, const_ref),
        (x_hbm, x_ref),
        (go_hbm, go_ref),
        (grp_hbm, grp_ref),
        (gain_hbm, gain_ref),
        (wqkv_hbm.at[0], wqkv_ref),
        (wproj_hbm.at[0], wproj_ref),
    ]
    copies = [pltpu.make_async_copy(a, b, sems.at[k]) for k, (a, b) in enumerate(sources)]
    for copy in copies:
        copy.start()
    results = []

    def send(source, target):
        copy = pltpu.make_async_copy(source, target, sems.at[9 + len(results)])
        copy.start()
        results.append(copy)

    for copy in copies[0:3]:
        copy.wait()
    px, ps, pm = [const_ref[k, 0 : (144, 160, 144)[k], 0:144] for k in range(3)]
    rows, cols = const_ref[3, 0:144, 0:12], const_ref[4, 0:144, 0:12]

    frame_ids(rel_ref[...], pm, main_ref, tail_ref)
    fill_bias(tab_ref[...], main_ref, tail_ref, words, scales, offsets, bias_ref)

    masks = lane_masks()
    for copy in copies[3:8]:
        copy.wait()
    for k in range(72):
        cells[2 * k : 2 * k + 2, 0:512] = x_ref[k].astype(F32)
        cells[2 * k : 2 * k + 2, 512:1024] = go_ref[k].astype(F32)
    both = dot(px, cells[...].astype(BF16))
    x = both[:, 0:512]
    pay[:, 512:1024] = both[:, 512:1024].astype(BF16)
    for r in range(6):
        gs[2 * r : 2 * r + 2, :] = grp_ref[r].astype(F32)
    picked = dot(rows, gs[...].astype(BF16)) * cols.astype(F32)
    group = jnp.sum(picked, axis=-1, keepdims=True)
    spots = (group * const_ref[6, 0:144, 0:128].astype(F32)).astype(BF16)
    group_rows = dot(const_ref[5, :, 0:144], spots)

    n, rstd = normalize(x)
    n_ref[...] = n
    send(n_ref, n_hbm)
    rstd_ref[...] = rstd
    h = (n * gain_ref[0:1, :]).astype(BF16)
    qkv_ref[...] = dot(h, wqkv_ref[...]).astype(BF16)
    send(qkv_ref, qkv_hbm)
    for g in range(4):
        biases = [bias_ref[576 * g + 144 * k : 576 * g + 144 * (k + 1), :] for k in range(4)]
        _, _, p4 = group_probs(qkv_ref, g, masks, biases, None)
        p4b = p4.astype(BF16)
        p_ref[576 * g : 576 * (g + 1), :] = p4b
        send(p_ref.at[576 * g : 576 * (g + 1)], p_hbm.at[576 * g : 576 * (g + 1)])
        vg = pad_keys(qkv_ref[:, 1024 + 128 * g : 1024 + 128 * (g + 1)])
        o_ref[:, 128 * g : 128 * (g + 1)] = fold_heads(dot(p4b, vg), masks).astype(BF16)
    send(o_ref, o_hbm)
    copies[8].wait()
    pay[:, 0:512] = (x + dot(o_ref[...], wproj_ref[...])).astype(BF16)
    out = dot(ps, pay[...])
    out = jnp.concatenate([out[:, 0:128] + group_rows, out[:, 128:1024]], axis=1)
    store_pieces(out, own_ref, lon_ref, lat_ref, dia_ref)
    for copy in results:
        copy.wait()


def bias_kernel(
    idx_ref, tab_ref, rel_ref, pm_ref, out_ref, main_ref, tail_ref, words, scales, offsets
):
    frame_ids(rel_ref[...], pm_ref[0:144, 0:144], main_ref, tail_ref)
    fill_bias(tab_ref[0, idx_ref[1]], main_ref, tail_ref, words, scales, offsets, out_ref)


def second_kernel(
    idx_ref, own_ref, lon_ref, lat_ref, dia_ref, gain_ref, wqkv_ref, wproj_ref, bias_ref,
    const_ref,
    oown_ref, olon_ref, olat_ref, odia_ref, h_ref, o_ref, dqkv_ref, g_ref, dgain_ref, ds0_ref, ds1_ref,
    qkv_ref, back,
):
    masks = lane_masks()
    flags = const_ref[2, 0:144, 0:2].astype(F32)
    pieces = load_pieces(slice(0, 1024), own_ref, lon_ref, lat_ref, dia_ref)
    frame = dot(const_ref[0, 0:144, 0:160], pieces)
    group = dot(const_ref[3, 0:144, 0:160], pieces[:, 0:128]) * const_ref[4, 0:144, 0:128].astype(F32)
    group = jnp.sum(group, axis=-1, keepdims=True)
    x = frame[:, 0:512]
    g32 = frame[:, 512:1024]
    gb = g32.astype(BF16)
    g_ref[...] = gb
    lat = idx_ref[1].astype(F32)
    key = group * 4.0 + flags[:, 1:2] * (2.0 * lat) + flags[:, 0:1]
    eye = lax.broadcasted_iota(jnp.int32, (144, 256), 0) == lax.broadcasted_iota(
        jnp.int32, (144, 256), 1
    )
    key_row = jnp.sum(jnp.where(eye, key, 0.0), axis=0, keepdims=True)
    allowed = key == key_row
    gain = gain_ref[1:2, :]

    n, rstd = normalize(x)
    h = (n * gain).astype(BF16)
    h_ref[...] = h
    qkv_ref[...] = dot(h, wqkv_ref[0]).astype(BF16)
    do = dot_nt(gb, wproj_ref[0]).astype(BF16)
    for g in range(4):
        biases = [bias_ref[576 * g + 144 * k : 576 * g + 144 * (k + 1), :] for k in range(4)]
        q4, kg, p4 = group_probs(qkv_ref, g, masks, biases, allowed)
        p4b = p4.astype(BF16)
        vg = pad_keys(qkv_ref[:, 1024 + 128 * g : 1024 + 128 * (g + 1)])
        o_ref[:, 128 * g : 128 * (g + 1)] = fold_heads(dot(p4b, vg), masks).astype(BF16)
        group_back(g, None, q4, kg, vg, p4, p4b, do, masks, dqkv_ref, ds0_ref, ds1_ref)
    back[:, 0:512] = (x + dot(o_ref[...], wproj_ref[0])).astype(BF16)
    df = finish_back(dqkv_ref, wqkv_ref, n, rstd, gain, g32, dgain_ref)
    back[:, 512:1024] = df.astype(BF16)
    store_pieces(dot(const_ref[1, :, 0:144], back[...]), oown_ref, olon_ref, olat_ref, odia_ref)


def send_kernel(idx_ref, h_ref, o_ref, dqkv_ref, g_ref, send_ref):
    target = h_ref[...], o_ref[...], dqkv_ref[...], g_ref[...], send_ref
    weight_terms(1 - idx_ref[0], target)


def third_kernel(
    idx_ref, own_ref, lon_ref, lat_ref, dia_ref, gain_ref, wproj_ref,
    n_ref, qkv_ref, p_ref, o_ref, const_ref, after_ref,
    g_ref, h_ref, dqkv_ref, ds0_ref, ds1_ref, send_ref,
):
    masks = lane_masks()
    pieces = load_pieces(slice(512, 1024), own_ref, lon_ref, lat_ref, dia_ref)
    gb = dot(const_ref[0, 0:144, 0:160], pieces).astype(BF16)
    g_ref[...] = gb
    do = dot_nt(gb, wproj_ref[0]).astype(BF16)
    for g in range(4):
        q4 = stack_heads(qkv_ref[:, 128 * g : 128 * (g + 1)], masks)
        kg = pad_keys(qkv_ref[:, 512 + 128 * g : 512 + 128 * (g + 1)])
        vg = pad_keys(qkv_ref[:, 1024 + 128 * g : 1024 + 128 * (g + 1)])
        p4b = p_ref[576 * g : 576 * (g + 1), :]
        group_back(g, qkv_ref[:, 128 * g : 128 * (g + 1)], q4, kg, vg, p4b.astype(F32), p4b, do, masks, dqkv_ref, ds0_ref, ds1_ref)
    h = (n_ref[...] * gain_ref[0:1, :]).astype(BF16)
    h_ref[...] = h
    weight_terms(1 - idx_ref[0], (h, o_ref[...], dqkv_ref[...], gb, send_ref))


def keep_kernel(idx_ref, *refs):
    blocks = [[r[...] for r in refs[4 * b : 4 * b + 4]] + [refs[8 + b]] for b in range(2)]
    weight_terms(idx_ref[0], *blocks)


def finish_kernel(
    own_ref, lon_ref, lat_ref, dia_ref, gain_ref, wqkv_ref, n_ref, rstd_ref, g_ref, dqkv_ref,
    const_ref, after_ref, out_ref, gin_ref, dgain_ref, outs,
):
    pieces = load_pieces(slice(0, 512), own_ref, lon_ref, lat_ref, dia_ref)
    outs[:, 0:512] = dot(const_ref[0, 0:144, 0:160], pieces)
    df = finish_back(
        dqkv_ref, wqkv_ref, n_ref[...], rstd_ref[...], gain_ref[0:1, :], g_ref[...].astype(F32), dgain_ref
    )
    outs[:, 512:1024] = dot(const_ref[1, 0:144, 0:144], df.astype(BF16))
    for k in range(72):
        out_ref[k] = outs[2 * k : 2 * k + 2, 0:512].astype(BF16)
        gin_ref[k] = outs[2 * k : 2 * k + 2, 512:1024].astype(BF16)


def scatter_kernel(
    idx_ref, main_ref, tail_ref, m0_ref, t0_ref, gain0_ref, m1_ref, t1_ref, gain1_ref, after_ref,
    keep_ref, send_ref,
):
    iota = lax.broadcasted_iota(jnp.int32, (128, 256), 0)

    def add(ids_ref, d_refs, stride, unroll):
        def body(i, acc):
            ids = jnp.concatenate([ids_ref[pl.ds(2 * i + k, 1), :] for k in range(2)], axis=1)
            low, high = ids & 127, ids >> 7
            hot = jnp.where(iota == low, 1.0, 0.0).astype(BF16)
            lhs = []
            for d_ref in d_refs:
                d = jnp.concatenate(
                    [d_ref[pl.ds(2 * i + k, 16, stride=stride), :] for k in range(2)], axis=1
                )
                lhs += [jnp.where(high == k, d, 0.0) for k in range(6)]
            return acc + dot_nt(jnp.concatenate(lhs, axis=0).astype(BF16), hot)

        return lambda acc: lax.fori_loop(0, stride // 2, body, acc, unroll=unroll)

    acc = add(main_ref, (m0_ref, m1_ref), 144, 8)(jnp.zeros((192, 128), F32))
    acc = add(tail_ref, (t0_ref, t1_ref), 24, 12)(acc)
    first = lax.broadcasted_iota(jnp.int32, (8, 256), 0) == 0
    for b, dgain_ref in enumerate((gain0_ref, gain1_ref)):
        table = [acc[96 * b + 16 * k : 96 * b + 16 * k + 16] for k in range(6)]
        table = jnp.concatenate(table, axis=1)
        halves = []
        for c in range(2):
            gain = jnp.where(first, dgain_ref[:, 256 * c : 256 * (c + 1)], 0.0)
            halves.append(jnp.concatenate([table[8 * c : 8 * (c + 1)], gain], axis=1))
        keep, send = pick(idx_ref[0], halves[0], halves[1])
        keep_ref[8 * b : 8 * b + 8, :] = keep
        send_ref[8 * b : 8 * b + 8, :] = send


CUTS = ((0, 384), (384, 768), (768, 1024))


def pick(flag, low, high):
    mine = flag == 0
    return jnp.where(mine, low, high), jnp.where(mine, high, low)


def core_kernel(
    idx_ref, k0_ref, r0_ref, k1_ref, r1_ref, ka_ref, sa_ref, kb_ref, sb_ref, kc_ref, sc_ref
):
    x0, z0, yl = idx_ref[2], idx_ref[3], idx_ref[1]
    for b, (k_ref, r_ref) in enumerate(((k0_ref, r0_ref), (k1_ref, r1_ref))):

        def total(r0, r1, c0, c1):
            return k_ref[r0:r1, c0:c1].astype(F32) + r_ref[r0:r1, c0:c1].astype(F32)

        for s in range(2):
            a0 = 1024 * s
            keep, send = pick(x0, total(0, 128, a0, a0 + 384), total(128, 256, a0, a0 + 384))
            to = 768 * b + 384 * s
            ka_ref[:, to : to + 384] = keep.astype(BF16)
            sa_ref[:, to : to + 384] = send.astype(BF16)
            to = 512 * b + 256 * s
            for h in range(2):
                r = 128 * h
                keep, send = pick(
                    z0,
                    total(r, r + 64, a0 + 768, a0 + 1024),
                    total(r + 64, r + 128, a0 + 768, a0 + 1024),
                )
                kc_ref[64 * h : 64 * h + 64, to : to + 256] = keep.astype(BF16)
                sc_ref[64 * h : 64 * h + 64, to : to + 256] = send.astype(BF16)
        keep, send = pick(yl, total(0, 256, 384, 768), total(0, 256, 1408, 1792))
        kb_ref[:, 384 * b : 384 * (b + 1)] = keep.astype(BF16)
        sb_ref[:, 384 * b : 384 * (b + 1)] = send.astype(BF16)


def step_two_kernel(
    idx_ref, ka_ref, ra_ref, kb_ref, rb_ref, kc_ref, rc_ref, t_ref, u_ref,
    nka_ref, nsa_ref, nkb_ref, nsb_ref, nkc_ref, nsc_ref, tk_ref,
):
    x0, z0, yl = idx_ref[2], idx_ref[3], idx_ref[1]
    a = ka_ref[...].astype(F32) + ra_ref[...].astype(F32)
    for b in range(2):
        keep, send = pick(yl, a[:, 768 * b : 768 * b + 384], a[:, 768 * b + 384 : 768 * b + 768])
        nka_ref[:, 384 * b : 384 * (b + 1)] = keep.astype(BF16)
        nsa_ref[:, 384 * b : 384 * (b + 1)] = send.astype(BF16)
    m = kb_ref[...].astype(F32) + rb_ref[...].astype(F32)
    for h in range(2):
        keep, send = pick(z0, m[128 * h : 128 * h + 64], m[128 * h + 64 : 128 * h + 128])
        nkb_ref[64 * h : 64 * h + 64, :] = keep.astype(BF16)
        nsb_ref[64 * h : 64 * h + 64, :] = send.astype(BF16)
    c = kc_ref[...].astype(F32) + rc_ref[...].astype(F32)
    keep, send = pick(x0, c[0:64], c[64:128])
    nkc_ref[...] = keep.astype(BF16)
    nsc_ref[0:64, :] = send.astype(BF16)
    table = (t_ref[...] + u_ref[...]).astype(BF16)
    tk_ref[...] = table
    nsc_ref[64:80, :] = table


def step_three_kernel(
    idx_ref, ka_ref, ra_ref, kb_ref, rb_ref, kc_ref, rc_ref, tk_ref,
    nka_ref, nsa_ref, nkb_ref, nsb_ref, nkc_ref, nsc_ref, ntk_ref,
):
    x0, z0, yl = idx_ref[2], idx_ref[3], idx_ref[1]
    a = ka_ref[...].astype(F32) + ra_ref[...].astype(F32)
    keep, send = pick(z0, a[0:64], a[64:128])
    nka_ref[...] = keep.astype(BF16)
    nsa_ref[0:64, :] = send.astype(BF16)
    t = tk_ref[...].astype(F32) + rc_ref[64:80, :].astype(F32)
    gains = jnp.concatenate([t[0:8, 768:1024], t[8:16, 768:1024], jnp.zeros((8, 256), F32)], axis=1)
    table = jnp.concatenate([t[:, 0:768], gains, jnp.zeros((8, 768), F32)], axis=0).astype(BF16)
    ntk_ref[...] = table
    nsa_ref[64:96, :] = table
    m = kb_ref[...].astype(F32) + rb_ref[...].astype(F32)
    keep, send = pick(x0, m[0:64], m[64:128])
    nkb_ref[...] = keep.astype(BF16)
    nsb_ref[...] = send.astype(BF16)
    c = kc_ref[...].astype(F32) + rc_ref[0:64, :].astype(F32)
    for b in range(2):
        keep, send = pick(yl, c[:, 512 * b : 512 * b + 256], c[:, 512 * b + 256 : 512 * b + 512])
        nkc_ref[:, 256 * b : 256 * (b + 1)] = keep.astype(BF16)
        nsc_ref[:, 256 * b : 256 * (b + 1)] = send.astype(BF16)


def spread_kernel(
    idx_ref, ka_ref, ra_ref, kb_ref, rb_ref, kc_ref, rc_ref, tk_ref, *refs
):
    outs, scr = refs[0:4], refs[4]
    a = ka_ref[...].astype(F32) + ra_ref[0:64, :].astype(F32)
    m = kb_ref[...].astype(F32) + rb_ref[...].astype(F32)
    c = kc_ref[...].astype(F32) + rc_ref[...].astype(F32)
    table = tk_ref[...].astype(F32) + ra_ref[64:96, :].astype(F32)
    gains = jnp.concatenate([table[16:24, 0:256], table[16:24, 256:512]], axis=0)
    table = jnp.concatenate([table[0:16], gains], axis=1)
    table = jnp.concatenate([table[0:8], table[8:16]], axis=1).astype(BF16)
    full = []
    for b in range(2):
        cols = slice(384 * b, 384 * (b + 1))
        full += [a[:, cols], m[:, cols], c[:, 256 * b : 256 * (b + 1)]]
    full = jnp.concatenate(full, axis=1).astype(BF16)
    for k in range(4):
        scr[k] = full[16 * k : 16 * k + 16]
    for f in range(4):
        outs[f][0:16, :] = scr[idx_ref[4] ^ f]
        outs[f][16:24, :] = table


def plane_kernel(idx_ref, own_ref, g1_ref, g2_ref, g3_ref, *refs):
    outs, tabs, scr = refs[0:4], refs[4], refs[5]
    got = (own_ref, g1_ref, g2_ref, g3_ref)
    total = got[0][0:16, :].astype(F32)
    for g in got[1:]:
        total = total + g[0:16, :].astype(F32)
    for f in range(4):
        tabs[idx_ref[4] ^ f] = got[f][16:24, :].astype(F32)
    table = tabs[0] + tabs[1] + tabs[2] + tabs[3]
    table = jnp.concatenate([table[:, 0:1024], table[:, 1024:2048]], axis=0)
    for k in range(4):
        rows = total[4 * k : 4 * k + 4]
        rows = jnp.concatenate([rows[:, 0:1024], rows[:, 1024:2048], table], axis=0)
        scr[k] = rows.astype(BF16)
    for f in range(4):
        outs[f][...] = scr[idx_ref[5] ^ f]


def close_kernel(idx_ref, own_ref, g1_ref, g2_ref, g3_ref, out_ref, tab_ref, scr):
    for f, g in enumerate((own_ref, g1_ref, g2_ref, g3_ref)):
        scr[idx_ref[5] ^ f] = g[...].astype(F32)
    total = scr[0] + scr[1] + scr[2] + scr[3]
    out_ref[...] = total.astype(BF16)
    tab_ref[...] = total[8:24].astype(BF16)


def last_kernel(
    factor, idx_ref, own_ref, lat_ref, core_ref, dia_ref, gain_ref, qkv_ref, proj_ref, bias_ref
):
    core, yl = idx_ref[0], idx_ref[1]
    own = own_ref[...].astype(F32) * factor
    got = lat_ref[...].astype(F32) * factor
    low, high = pick(yl, own[0:8], got[0:8])
    for b in range(2):
        qkv_ref[b, :, 0:1024] = low[4 * b : 4 * b + 4]
        qkv_ref[b, :, 1024:1536] = high[4 * b : 4 * b + 4, 0:512]
        proj_ref[b, :, :] = high[4 * b : 4 * b + 4, 512:1024]
    near = pick(yl, own[8:24], got[8:24])
    far = pick(yl, core_ref[...].astype(F32) * factor, dia_ref[...].astype(F32) * factor)
    tabs = [pick(core, near[w], far[w]) for w in range(2)]
    for c in range(2):
        for w in range(2):
            for b in range(2):
                bias_ref[b, w, 8 * c : 8 * (c + 1), :] = tabs[w][c][8 * b : 8 * b + 8, 0:NREL]
        for b in range(2):
            gain_ref[b : b + 1, 256 * c : 256 * (c + 1)] = (
                tabs[0][c][8 * b : 8 * b + 1, 768:1024] + tabs[1][c][8 * b : 8 * b + 1, 768:1024]
            )


def _whole(shape):
    return pl.BlockSpec(shape, lambda *_: (0,) * len(shape))


SMEM = pl.BlockSpec(memory_space=pltpu.SMEM)


ANY = pl.BlockSpec(memory_space=pl.ANY)


HBM = pl.BlockSpec(memory_space=pltpu.HBM)


def call(body, us, outs, *args, specs=None, scratch=(), sems=0, vmem=VMEM, hbm_outs=()):
    specs = dict(specs or {})
    if args[0].dtype == jnp.int32 and args[0].ndim == 1:
        specs[0] = SMEM
    scratch = [pltpu.VMEM(s, t) for s, t in scratch]
    if sems:
        scratch.append(pltpu.SemaphoreType.DMA((sems,)))
    return pl.pallas_call(
        body,
        grid=(1,),
        in_specs=[specs.get(i, _whole(a.shape)) for i, a in enumerate(args)],
        out_specs=[HBM if k in hbm_outs else _whole(s) for k, (s, _) in enumerate(outs)],
        out_shape=[jax.ShapeDtypeStruct(s, t) for s, t in outs],
        scratch_shapes=scratch,
        compiler_params=pltpu.CompilerParams(vmem_limit_bytes=vmem),
        cost_estimate=pl.CostEstimate(
            flops=int(us * 1e9), bytes_accessed=int(us * 3.6e6), transcendentals=0
        ),
    )(*args)


def mask_of(axes):
    return sum(1 << (7 - AXES.index(a)) for a in axes)


def flip(value, *axes):
    return lax.ppermute(value, AXES, [(s, s ^ mask_of(axes)) for s in range(256)])


def z_step(value, move, *axes):
    pairs = [(s, (s & ~28 | move(s >> 2 & 7) << 2) ^ mask_of(axes)) for s in range(256)]
    return lax.ppermute(value, AXES, pairs)


def lon_step(value, offset, across):
    pairs = [(s, ((s // 2 + offset) % 128) * 2 + (s % 2 ^ across)) for s in range(256)]
    return lax.ppermute(value, AXES, pairs)


def halo(pieces, offset):
    own, lon, lat, dia = pieces
    return (
        own,
        lon_step(lon, offset, 0),
        flip(lat, "yl"),
        lon_step(dia, offset, 1),
    )


def on_device(inputs, grad_out, gains, qkv_weight, proj_weight, bias_table, rel_ids, groups):
    first_const, second_const, third_const, finish_const = [jnp.asarray(t) for t in TABLES]
    at = {a: lax.axis_index(a) for a in AXES}
    hz = at["z0"] ^ at["z1"]
    idx = jnp.stack(
        [
            at["c"],
            at["yl"],
            at["x0"] ^ at["x1"],
            hz,
            2 * at["x1"] + (at["z2"] ^ (hz & at["z1"])),
            2 * at["yh"] + (at["z1"] ^ (hz & (at["z1"] ^ at["z2"]))),
        ]
    ).astype(jnp.int32)
    x_cells, go_cells = [v.transpose(0, 2, 3, 1, 4).reshape(72, 2, D) for v in (inputs, grad_out)]

    def block(b, shape):
        return pl.BlockSpec((1,) + shape, lambda *_: (b,) + (0,) * len(shape))

    def weights(b, first):
        return {
            first: block(b, (D, 3 * D)),
            first + 1: block(b, (D, D)),
            first + 2: block(b, (2, HEADS, NREL)),
        }

    id_shapes = [((144, 128), jnp.int32), ((24, 128), jnp.int32)]
    tables = [((8, 768), jnp.int32), ((HEADS, 128), F32), ((HEADS, 128), F32)]
    piece = ((40, 1024), BF16)
    saved = [((144, D), F32), ((144, 3 * D), BF16), ((2304, 256), BF16), ((144, D), BF16)]
    own, lon, lat, dia, rstd0, n0, qkv0, p0, o0 = call(
        first_kernel,
        8,
        [piece] * 4
        + [
            ((144, 1), F32),
        ]
        + saved,
        x_cells, go_cells, groups.transpose(1, 0, 2), gains, qkv_weight, proj_weight, bias_table, rel_ids,
        first_const,
        specs={k: HBM for k in range(9)},
        scratch=saved
        + [((144, 1024), F32), ((12, 12), F32), ((144, 1024), BF16), ((2304, 256), F32)]
        + id_shapes
        + tables
        + [
            ((72, 2, D), BF16),
            ((72, 2, D), BF16),
            ((6, 2, 12), jnp.int32),
            ((2, D), F32),
            ((D, 3 * D), BF16),
            ((D, D), BF16),
            ((HEADS, NREL), F32),
            ((144, 144), jnp.int32),
            ((7, 160, 256), BF16),
        ],
        sems=16,
        hbm_outs=range(5, 9),
        vmem=57 << 20,
    )
    pieces = halo((own, lon, lat, dia), -1)
    bias1, ids, tails = call(
        bias_kernel,
        4,
        [((2304, 256), F32)] + id_shapes,
        idx, bias_table, rel_ids, jnp.asarray(TABLES[0][2]),
        specs={1: block(1, (2, HEADS, NREL))},
        scratch=tables,
    )
    ds_shapes = [((2304, 128), F32), ((384, 128), F32)]
    own, lon, lat, dia, h1, o1, dqkv1, g1, dgain1, ds10, ds11 = call(
        second_kernel,
        6,
        [piece] * 4
        + [
            ((144, D), BF16),
            ((144, D), BF16),
            ((144, 3 * D), BF16),
            ((144, D), BF16),
            ((1, D), F32),
        ]
        + ds_shapes,
        idx, *pieces, gains, qkv_weight, proj_weight, bias1, second_const,
        specs={6: block(1, (D, 3 * D)), 7: block(1, (D, D))},
        scratch=[((144, 3 * D), BF16), ((144, 2 * D), BF16)],
    )
    pieces = halo((own, lon, lat, dia), 1)
    wshape = ((256, 4 * D), BF16)
    (send1,) = call(send_kernel, 1, [wshape], idx, h1, o1, dqkv1, g1)
    recv1 = flip(send1, "c")

    def pairs(*shapes):
        return [(s, BF16) for shape in shapes for s in shape]

    cells = ((72, 2, D), BF16)
    g0, h0, dqkv0, ds00, ds01, send0 = call(
        third_kernel,
        4,
        [((144, D), BF16)] * 2 + [((144, 3 * D), BF16)] + ds_shapes + [wshape],
        idx, *pieces, gains, proj_weight, n0, qkv0, p0, o0, third_const, send1,
        specs={6: block(0, (D, D)), 12: ANY},
    )
    recv0 = flip(send0, "c")
    keep0, keep1 = call(
        keep_kernel, 2, [wshape] * 2, idx, h0, o0, dqkv0, g0, h1, o1, dqkv1, g1
    )
    ka, sa, kb, sb, kc, sc = call(
        core_kernel,
        1,
        pairs([(128, 1536)] * 2, [(256, 768)] * 2, [(128, 1024)] * 2),
        idx, keep0, recv0, keep1, recv1,
    )
    ra, rb, rc = flip(sa, "x0"), flip(sb, "yl"), flip(sc, "z0")
    outputs, grad_inputs, dgain0 = call(
        finish_kernel,
        2,
        [cells, cells, ((1, D), F32)],
        *pieces, gains, qkv_weight, n0, rstd0, g0, dqkv0, finish_const, ka,
        specs={5: block(0, (D, 3 * D)), 11: ANY},
        scratch=[((144, 2 * D), F32)],
    )
    outputs, grad_inputs = [
        v.reshape(1, 6, 12, 2, D).transpose(0, 3, 1, 2, 4) for v in (outputs, grad_inputs)
    ]
    tshape = ((16, 1024), F32)
    tkeep, tsend = call(
        scatter_kernel,
        6,
        [tshape] * 2,
        idx, ids, tails, ds00, ds01, dgain0, ds10, ds11, dgain1, ka,
        specs={9: ANY},
    )
    trecv = flip(tsend, "c")
    ka, sa, kb, sb, kc, sc, tk = call(
        step_two_kernel,
        1,
        pairs([(128, 768)] * 4, [(64, 1024), (80, 1024)], [(16, 1024)]),
        idx, ka, ra, kb, rb, kc, rc, tkeep, trecv,
    )
    ra, rb, rc = flip(sa, "yl"), flip(sb, "z0"), flip(sc, "x0")
    ka, sa, kb, sb, kc, sc, tk = call(
        step_three_kernel,
        1,
        pairs([(64, 768), (96, 768)], [(64, 768)] * 2, [(64, 512)] * 2, [(32, 768)]),
        idx, ka, ra, kb, rb, kc, rc, tk,
    )
    ra, rb, rc = flip(sa, "z0"), flip(sb, "x0"), flip(sc, "yl")
    parts = call(
        spread_kernel,
        1,
        [((24, 2048), BF16)] * 4,
        idx, ka, ra, kb, rb, kc, rc, tk,
        scratch=[((4, 16, 2048), BF16)],
    )
    near = lambda z: (z + 1) % 8 if z & 1 else (z - 1) % 8
    far = lambda z: z ^ (7 if (z ^ z >> 1) & 1 else 3)
    parts = call(
        plane_kernel,
        1,
        [((24, 1024), BF16)] * 4,
        idx, parts[0], z_step(parts[1], near), flip(parts[2], "x1", "x0"),
        z_step(parts[3], near, "x1", "x0"),
        scratch=[((4, 8, 2048), F32), ((4, 24, 1024), BF16)],
    )
    own, tab = call(
        close_kernel,
        1,
        [((24, 1024), BF16), ((16, 1024), BF16)],
        idx, parts[0], z_step(parts[1], far), flip(parts[2], "yh"), z_step(parts[3], far, "yh"),
        scratch=[((4, 24, 1024), F32)],
    )
    from_core = flip(tab, "c")
    from_dia = flip(tab, "c", "yl")
    from_lat = flip(own, "yl")
    factor = 36864 ** (-0.5)
    grad_gains, grad_qkv, grad_proj, grad_bias = call(
        functools.partial(last_kernel, factor),
        1,
        [
            ((2, D), F32),
            ((2, 4, 3 * D), F32),
            ((2, 4, D), F32),
            ((2, 2, HEADS, NREL), F32),
        ],
        idx, own, from_lat, from_core, from_dia,
    )
    return (outputs, grad_inputs, grad_gains, grad_qkv, grad_proj, grad_bias)


def solution(mesh):
    fine = Mesh(mesh.devices.reshape((2,) * 8), AXES)
    lon = AXES[:7]
    field = P(None, None, "yl", lon, None)
    rows = P(None, lon, None)
    return jax.shard_map(
        on_device,
        mesh=fine,
        in_specs=(field, field, P(), P(), P(), P(), P(), P(None, "yl", lon)),
        out_specs=(field, field, P(), rows, rows, P()),
        check_vma=False,
    )
```

```python
import functools

import jax
import jax.numpy as jnp
import numpy as np
from jax import lax
from jax.experimental import pallas as pl
from jax.experimental.pallas import tpu as pltpu
from jax.sharding import Mesh, PartitionSpec as P

F32 = jnp.float32
BF16 = jnp.bfloat16
EPSILON = 1e-05
NEGATIVE = -1e30
D = 512
HEADS = 16
NREL = 759
SCALE = 32 ** (-0.5)
AXES = ("yh", "x1", "x0", "z2", "z1", "z0", "c", "yl")
VMEM = 24 << 20

QUADS = ((1, 1), (1, 0), (0, 1), (0, 0))


def _token(rh, ch, l, r, c):
    return (rh * 2 + ch) * 36 + l * 18 + r * 6 + c


def _tables():
    px = np.zeros((144, 144), np.float32)
    ps = np.zeros((160, 144), np.float32)
    pf = np.zeros((144, 160), np.float32)
    pm = np.zeros((144, 144), np.float32)
    rows = np.zeros((144, 12), np.float32)
    cols = np.zeros((144, 12), np.float32)
    flags = np.zeros((144, 2), np.float32)
    into = np.zeros((160, 144), np.float32)
    spot = np.zeros((144, 128), np.float32)
    back = np.zeros((144, 160), np.float32)
    seat = np.zeros((144, 128), np.float32)
    for l in range(2):
        for row in range(6):
            for col in range(12):
                rh, r, ch, c = row // 3, row % 3, col // 6, col % 6
                t = _token(rh, ch, l, r, c)
                px[t, (row * 12 + col) * 2 + l] = 1
                pm[t, l * 72 + row * 12 + col] = 1
                rows[t, row * 2 + l] = 1
                cols[t, col] = 1
                flags[t] = (l, rh)
                k = QUADS.index((rh, ch))
                i = (1 - l) * 18 + r * 6 + c
                ps[40 * k + i, t] = 1
                into[40 * k + 36, t] = 1
                spot[t, i] = 1
    for k in range(4):
        for i in range(36):
            t = 36 * k + i
            pf[t, 40 * k + i] = 1
            back[t, 40 * k + 36] = 1
            seat[t, i] = 1
    first = (px, ps, pm, rows, cols, into, spot)
    second = (pf, pf.T, flags, back, seat)
    return first, second, (ps.T,), (px.T @ ps.T, px.T)


def stacked(parts):
    out = np.zeros((len(parts), 160, 256), np.float32)
    for k, part in enumerate(parts):
        out[k, : part.shape[0], : part.shape[1]] = part
    return out.astype(jnp.bfloat16)


TABLES = [stacked(group) for group in _tables()]


def dot(a, b):
    return lax.dot_general(a, b, (((1,), (0,)), ((), ())), preferred_element_type=F32)


def dot_nt(a, b):
    return lax.dot_general(a, b, (((1,), (1,)), ((), ())), preferred_element_type=F32)


def dot_tn(a, b):
    return lax.dot_general(a, b, (((0,), (0,)), ((), ())), preferred_element_type=F32)


def lane_masks():
    lane = lax.broadcasted_iota(jnp.int32, (1, 128), 1) >> 5
    return [jnp.where(lane == k, 1.0, 0.0).astype(F32) for k in range(4)]


def stack_heads(group, masks):
    return jnp.concatenate([group * m.astype(BF16) for m in masks], axis=0)


def fold_heads(stacked, masks):
    total = stacked[0:144] * masks[0]
    for k in range(1, 4):
        total = total + stacked[144 * k : 144 * (k + 1)] * masks[k]
    return total


def pad_keys(group):
    return jnp.concatenate([group, jnp.zeros((112, 128), BF16)], axis=0)


def normalize(x):
    center = x - jnp.mean(x, axis=-1, keepdims=True)
    rstd = lax.rsqrt(jnp.mean(center * center, axis=-1, keepdims=True) + EPSILON)
    return center * rstd, rstd


def pack_table(tab, words, scales, offsets):
    low = jnp.min(tab, axis=-1, keepdims=True)
    scale = jnp.maximum(jnp.max(tab, axis=-1, keepdims=True) - low, 1e-20) * (1.0 / 65535.0)
    q = jnp.clip(jnp.floor((tab - low) / scale + 0.5), 0.0, 65535.0).astype(jnp.int32)
    high = jnp.concatenate([q[4 * g : 4 * g + 2] for g in range(4)], axis=0)
    rest = jnp.concatenate([q[4 * g + 2 : 4 * g + 4] for g in range(4)], axis=0)
    words[...] = jnp.zeros((8, 768), jnp.int32)
    words[:, 0:NREL] = ((high - 32768) << 16) + rest
    signed = lax.broadcasted_iota(jnp.int32, (HEADS, 1), 0) & 3
    offset = low + jnp.where(signed < 2, 32768.0, 0.0) * scale
    scales[...] = jnp.broadcast_to(scale, (HEADS, 128))
    offsets[...] = jnp.broadcast_to(offset, (HEADS, 128))


def lookup(row, ids):
    acc = None
    for k in range(6):
        part = jnp.broadcast_to(row[:, 128 * k : 128 * (k + 1)], ids.shape)
        got = jnp.take_along_axis(part, ids & 127, axis=1)
        acc = got if k == 0 else jnp.where((ids >> 7) == k, got, acc)
    return acc


def side_by_side(tail):
    total = tail[0:24]
    for k in range(1, 6):
        total = total + pltpu.roll(tail[24 * k : 24 * (k + 1)], 16 * k, 1)
    return total


def bias_pair(m, words, scales, offsets, ids, tails):
    row = words[m : m + 1, :]
    main = lookup(row, ids)
    tail = lookup(row, tails)
    parts = [tail] + [pltpu.roll(tail, 128 - 16 * k, 1) for k in range(1, 6)]
    tail = jnp.concatenate(parts, axis=0)
    lane = lax.broadcasted_iota(jnp.int32, (144, 128), 1)
    head = 4 * (m // 2) + m % 2
    out = []
    for h, take in ((head, lambda w: w >> 16), (head + 2, lambda w: w & 65535)):
        scale, offset = scales[h : h + 1, :], offsets[h : h + 1, :]
        a = take(main).astype(F32) * scale + offset
        b = jnp.where(lane < 16, take(tail).astype(F32) * scale + offset, NEGATIVE)
        out.append(jnp.concatenate([a, b], axis=1))
    return out


def frame_ids(rel, pm, main_ref, tail_ref):
    parts = []
    for part in (rel >> 5, rel & 31):
        half = dot(pm, part.astype(F32).astype(BF16)).astype(BF16)
        parts.append(dot_nt(half, pm).astype(jnp.int32))
    ids = parts[0] * 32 + parts[1]
    main_ref[...] = ids[:, 0:128]
    tail = jnp.concatenate([ids[:, 128:144], jnp.zeros((144, 112), jnp.int32)], axis=1)
    tail_ref[...] = side_by_side(tail)


def fill_bias(table, main_ref, tail_ref, words, scales, offsets, store):
    pack_table(table, words, scales, offsets)
    ids, tails = main_ref[...], tail_ref[...]
    for m in range(8):
        head = 4 * (m // 2) + m % 2
        for h, b in zip((head, head + 2), bias_pair(m, words, scales, offsets, ids, tails)):
            store[144 * h : 144 * (h + 1), :] = b


def group_probs(qkv_ref, g, masks, biases, allowed):
    qg = qkv_ref[:, 128 * g : 128 * (g + 1)]
    kg = pad_keys(qkv_ref[:, 512 + 128 * g : 512 + 128 * (g + 1)])
    q4 = stack_heads(qg, masks)
    s4 = dot_nt(q4, kg) * SCALE
    out = []
    for k in range(4):
        s = s4[144 * k : 144 * (k + 1)] + biases[k]
        if allowed is not None:
            s = jnp.where(allowed, s, NEGATIVE)
        e = jnp.exp(s - jnp.max(s, axis=-1, keepdims=True))
        out.append(e * (1.0 / jnp.sum(e, axis=-1, keepdims=True)))
    return q4, kg, jnp.concatenate(out, axis=0)


def by_keys(left, right):
    parts = [dot(left[32 * k : 32 * k + 32], right[144 * k : 144 * k + 144]) for k in range(4)]
    return jnp.concatenate(parts, axis=0).T[0:144]


def by_rows(left, right):
    parts = [dot_nt(left[32 * k : 32 * k + 32], right[144 * k : 144 * k + 144]) for k in range(4)]
    return jnp.concatenate(parts, axis=0).T


def group_back(g, qg, q4, kg, vg, p4, p4b, do, masks, dqkv_ref, ds0_ref, ds1_ref):
    do4 = stack_heads(do[:, 128 * g : 128 * (g + 1)], masks)
    dp4 = dot_nt(do4, vg)
    if qg is None:
        dv = dot_tn(p4b[:, 0:144], do4)
    else:
        dv = by_keys(do[:, 128 * g : 128 * (g + 1)].T, p4b)
    dqkv_ref[:, 1024 + 128 * g : 1024 + 128 * (g + 1)] = dv.astype(BF16)
    ds4 = p4 * (dp4 - jnp.sum(dp4 * p4, axis=-1, keepdims=True))
    ds0_ref[576 * g : 576 * (g + 1), :] = ds4[:, 0:128]
    for k in range(4):
        at = 24 * (4 * g + k)
        ds1_ref[at : at + 24, :] = side_by_side(ds4[144 * k : 144 * (k + 1), 128:256])
    ds4b = ds4.astype(BF16)
    dq = fold_heads(dot(ds4b, kg), masks) * SCALE
    dqkv_ref[:, 128 * g : 128 * (g + 1)] = dq.astype(BF16)
    if qg is None:
        dk = dot_tn(ds4b[:, 0:144], q4) * SCALE
    else:
        dk = by_keys(qg.T, ds4b) * SCALE
    dqkv_ref[:, 512 + 128 * g : 512 + 128 * (g + 1)] = dk.astype(BF16)


def finish_back(dqkv_ref, wqkv_ref, n, rstd, gain, g32, dgain_ref):
    dh = dot_nt(dqkv_ref[...], wqkv_ref[0])
    dgain_ref[...] = jnp.sum(dh * n, axis=0, keepdims=True)
    dn = dh * gain
    return (
        rstd
        * (
            dn
            - jnp.mean(dn, axis=-1, keepdims=True)
            - n * jnp.mean(dn * n, axis=-1, keepdims=True)
        )
        + g32
    )


def weight_terms(h, o, dqkv, g, *targets):
    p = lax.broadcasted_iota(jnp.int32, (256, 512), 0)
    row = lax.broadcasted_iota(jnp.int32, (256, 512), 1)
    bit = lambda k: (p >> k) & 1
    hz, h2, h3 = bit(6), bit(4), bit(2)
    z1 = h3 ^ (hz & h2)
    place = (
        (8, bit(3)),
        (7, bit(5)),
        (6, bit(7) ^ bit(5)),
        (5, h2 ^ (hz & (h2 ^ h3))),
        (4, z1),
        (3, z1 ^ hz),
    )
    base = p & 3
    for to, value in place:
        base = base + (value << to)
    for which, ref in targets:
        pick = jnp.where(row == base + which * 4, 1.0, 0.0).astype(BF16)
        ht = dot_nt(pick, h).astype(BF16)
        ot = dot_nt(pick, o).astype(BF16)
        ref[:, 0:1536] = dot(ht, dqkv).astype(BF16)
        ref[:, 1536:2048] = dot(ot, g).astype(BF16)


def store_pieces(out, *refs):
    for k, ref in enumerate(refs):
        ref[...] = out[40 * k : 40 * (k + 1)].astype(BF16)


def load_pieces(cols, *refs):
    return jnp.concatenate([ref[:, cols].astype(F32) for ref in refs], axis=0).astype(BF16)


def first_kernel(
    x_hbm, go_hbm, grp_hbm, gain_hbm, wqkv_hbm, wproj_hbm, tab_hbm, rel_hbm, const_hbm,
    own_ref, lon_ref, lat_ref, dia_ref, rstd_ref, n_hbm, qkv_hbm, p_hbm, o_hbm,
    n_ref, qkv_ref, p_ref, o_ref, cells, gs, pay, bias_ref, main_ref, tail_ref, words, scales, offsets,
    x_ref, go_ref, grp_ref, gain_ref, wqkv_ref, wproj_ref, tab_ref, rel_ref, const_ref, sems,
):
    sources = [
        (rel_hbm, rel_ref),
        (tab_hbm.at[0, lax.axis_index("yl")], tab_ref),
        (const_hbm, const_ref),
        (x_hbm, x_ref),
        (go_hbm, go_ref),
        (grp_hbm, grp_ref),
        (gain_hbm, gain_ref),
        (wqkv_hbm.at[0], wqkv_ref),
        (wproj_hbm.at[0], wproj_ref),
    ]
    copies = [pltpu.make_async_copy(a, b, sems.at[k]) for k, (a, b) in enumerate(sources)]
    for copy in copies:
        copy.start()
    results = []

    def send(source, target):
        copy = pltpu.make_async_copy(source, target, sems.at[9 + len(results)])
        copy.start()
        results.append(copy)

    for copy in copies[0:3]:
        copy.wait()
    px, ps, pm = [const_ref[k, 0 : (144, 160, 144)[k], 0:144] for k in range(3)]
    rows, cols = const_ref[3, 0:144, 0:12], const_ref[4, 0:144, 0:12]

    frame_ids(rel_ref[...], pm, main_ref, tail_ref)
    fill_bias(tab_ref[...], main_ref, tail_ref, words, scales, offsets, bias_ref)

    masks = lane_masks()
    for copy in copies[3:8]:
        copy.wait()
    for k in range(72):
        cells[2 * k : 2 * k + 2, 0:512] = x_ref[k].astype(F32)
        cells[2 * k : 2 * k + 2, 512:1024] = go_ref[k].astype(F32)
    both = dot(px, cells[...].astype(BF16))
    x = both[:, 0:512]
    pay[:, 512:1024] = both[:, 512:1024].astype(BF16)
    for r in range(6):
        gs[2 * r : 2 * r + 2, :] = grp_ref[r].astype(F32)
    picked = dot(rows, gs[...].astype(BF16)) * cols.astype(F32)
    group = jnp.sum(picked, axis=-1, keepdims=True)
    spots = (group * const_ref[6, 0:144, 0:128].astype(F32)).astype(BF16)
    group_rows = dot(const_ref[5, :, 0:144], spots)

    n, rstd = normalize(x)
    n_ref[...] = n
    send(n_ref, n_hbm)
    rstd_ref[...] = rstd
    h = (n * gain_ref[0:1, :]).astype(BF16)
    qkv_ref[...] = dot(h, wqkv_ref[...]).astype(BF16)
    send(qkv_ref, qkv_hbm)
    for g in range(4):
        biases = [bias_ref[576 * g + 144 * k : 576 * g + 144 * (k + 1), :] for k in range(4)]
        _, _, p4 = group_probs(qkv_ref, g, masks, biases, None)
        p4b = p4.astype(BF16)
        p_ref[576 * g : 576 * (g + 1), :] = p4b
        send(p_ref.at[576 * g : 576 * (g + 1)], p_hbm.at[576 * g : 576 * (g + 1)])
        vg = pad_keys(qkv_ref[:, 1024 + 128 * g : 1024 + 128 * (g + 1)])
        o_ref[:, 128 * g : 128 * (g + 1)] = fold_heads(dot(p4b, vg), masks).astype(BF16)
    send(o_ref, o_hbm)
    copies[8].wait()
    pay[:, 0:512] = (x + dot(o_ref[...], wproj_ref[...])).astype(BF16)
    out = dot(ps, pay[...])
    out = jnp.concatenate([out[:, 0:128] + group_rows, out[:, 128:1024]], axis=1)
    store_pieces(out, own_ref, lon_ref, lat_ref, dia_ref)
    for copy in results:
        copy.wait()


def bias_kernel(
    idx_ref, tab_ref, rel_ref, pm_ref, out_ref, main_ref, tail_ref, words, scales, offsets
):
    frame_ids(rel_ref[...], pm_ref[0:144, 0:144], main_ref, tail_ref)
    fill_bias(tab_ref[0, idx_ref[1]], main_ref, tail_ref, words, scales, offsets, out_ref)


def second_kernel(
    idx_ref, own_ref, lon_ref, lat_ref, dia_ref, gain_ref, wqkv_ref, wproj_ref, bias_ref,
    const_ref,
    oown_ref, olon_ref, olat_ref, odia_ref, h_ref, o_ref, dqkv_ref, g_ref, dgain_ref, ds0_ref, ds1_ref,
    qkv_ref, back,
):
    masks = lane_masks()
    flags = const_ref[2, 0:144, 0:2].astype(F32)
    pieces = load_pieces(slice(0, 1024), own_ref, lon_ref, lat_ref, dia_ref)
    frame = dot(const_ref[0, 0:144, 0:160], pieces)
    group = dot(const_ref[3, 0:144, 0:160], pieces[:, 0:128]) * const_ref[4, 0:144, 0:128].astype(F32)
    group = jnp.sum(group, axis=-1, keepdims=True)
    x = frame[:, 0:512]
    g32 = frame[:, 512:1024]
    gb = g32.astype(BF16)
    g_ref[...] = gb
    lat = idx_ref[1].astype(F32)
    key = group * 4.0 + flags[:, 1:2] * (2.0 * lat) + flags[:, 0:1]
    eye = lax.broadcasted_iota(jnp.int32, (144, 256), 0) == lax.broadcasted_iota(
        jnp.int32, (144, 256), 1
    )
    key_row = jnp.sum(jnp.where(eye, key, 0.0), axis=0, keepdims=True)
    allowed = key == key_row
    gain = gain_ref[1:2, :]

    n, rstd = normalize(x)
    h = (n * gain).astype(BF16)
    h_ref[...] = h
    qkv_ref[...] = dot(h, wqkv_ref[0]).astype(BF16)
    do = dot_nt(gb, wproj_ref[0]).astype(BF16)
    for g in range(4):
        biases = [bias_ref[576 * g + 144 * k : 576 * g + 144 * (k + 1), :] for k in range(4)]
        q4, kg, p4 = group_probs(qkv_ref, g, masks, biases, allowed)
        p4b = p4.astype(BF16)
        vg = pad_keys(qkv_ref[:, 1024 + 128 * g : 1024 + 128 * (g + 1)])
        o_ref[:, 128 * g : 128 * (g + 1)] = fold_heads(dot(p4b, vg), masks).astype(BF16)
        group_back(g, None, q4, kg, vg, p4, p4b, do, masks, dqkv_ref, ds0_ref, ds1_ref)
    back[:, 0:512] = (x + dot(o_ref[...], wproj_ref[0])).astype(BF16)
    df = finish_back(dqkv_ref, wqkv_ref, n, rstd, gain, g32, dgain_ref)
    back[:, 512:1024] = df.astype(BF16)
    store_pieces(dot(const_ref[1, :, 0:144], back[...]), oown_ref, olon_ref, olat_ref, odia_ref)


def weights_kernel(idx_ref, h_ref, o_ref, dqkv_ref, g_ref, keep_ref, send_ref):
    core = idx_ref[0]
    targets = (core, keep_ref), (1 - core, send_ref)
    weight_terms(h_ref[...], o_ref[...], dqkv_ref[...], g_ref[...], *targets)


def third_kernel(
    idx_ref, own_ref, lon_ref, lat_ref, dia_ref, gain_ref, wproj_ref,
    n_ref, qkv_ref, p_ref, o_ref, const_ref, after_ref,
    g_ref, h_ref, dqkv_ref, ds0_ref, ds1_ref, send_ref,
):
    masks = lane_masks()
    pieces = load_pieces(slice(512, 1024), own_ref, lon_ref, lat_ref, dia_ref)
    gb = dot(const_ref[0, 0:144, 0:160], pieces).astype(BF16)
    g_ref[...] = gb
    do = dot_nt(gb, wproj_ref[0]).astype(BF16)
    for g in range(4):
        q4 = stack_heads(qkv_ref[:, 128 * g : 128 * (g + 1)], masks)
        kg = pad_keys(qkv_ref[:, 512 + 128 * g : 512 + 128 * (g + 1)])
        vg = pad_keys(qkv_ref[:, 1024 + 128 * g : 1024 + 128 * (g + 1)])
        p4b = p_ref[576 * g : 576 * (g + 1), :]
        group_back(g, qkv_ref[:, 128 * g : 128 * (g + 1)], q4, kg, vg, p4b.astype(F32), p4b, do, masks, dqkv_ref, ds0_ref, ds1_ref)
    h = (n_ref[...] * gain_ref[0:1, :]).astype(BF16)
    h_ref[...] = h
    weight_terms(h, o_ref[...], dqkv_ref[...], gb, (1 - idx_ref[0], send_ref))


def keep_kernel(idx_ref, h_ref, o_ref, dqkv_ref, g_ref, keep_ref):
    weight_terms(h_ref[...], o_ref[...], dqkv_ref[...], g_ref[...], (idx_ref[0], keep_ref))


def finish_kernel(
    own_ref, lon_ref, lat_ref, dia_ref, gain_ref, wqkv_ref, n_ref, rstd_ref, g_ref, dqkv_ref,
    const_ref, after_ref, out_ref, gin_ref, dgain_ref, outs,
):
    pieces = load_pieces(slice(0, 512), own_ref, lon_ref, lat_ref, dia_ref)
    outs[:, 0:512] = dot(const_ref[0, 0:144, 0:160], pieces)
    df = finish_back(
        dqkv_ref, wqkv_ref, n_ref[...], rstd_ref[...], gain_ref[0:1, :], g_ref[...].astype(F32), dgain_ref
    )
    outs[:, 512:1024] = dot(const_ref[1, 0:144, 0:144], df.astype(BF16))
    for k in range(72):
        out_ref[k] = outs[2 * k : 2 * k + 2, 0:512].astype(BF16)
        gin_ref[k] = outs[2 * k : 2 * k + 2, 512:1024].astype(BF16)


def scatter_kernel(
    idx_ref, main_ref, tail_ref, m0_ref, t0_ref, gain0_ref, m1_ref, t1_ref, gain1_ref, after_ref,
    keep_ref, send_ref,
):
    iota = lax.broadcasted_iota(jnp.int32, (128, 256), 0)

    def add(ids_ref, d_refs, stride, unroll):
        def body(i, acc):
            ids = jnp.concatenate([ids_ref[pl.ds(2 * i + k, 1), :] for k in range(2)], axis=1)
            low, high = ids & 127, ids >> 7
            hot = jnp.where(iota == low, 1.0, 0.0).astype(BF16)
            lhs = []
            for d_ref in d_refs:
                d = jnp.concatenate(
                    [d_ref[pl.ds(2 * i + k, 16, stride=stride), :] for k in range(2)], axis=1
                )
                lhs += [jnp.where(high == k, d, 0.0) for k in range(6)]
            return acc + dot_nt(jnp.concatenate(lhs, axis=0).astype(BF16), hot)

        return lambda acc: lax.fori_loop(0, stride // 2, body, acc, unroll=unroll)

    acc = add(main_ref, (m0_ref, m1_ref), 144, 8)(jnp.zeros((192, 128), F32))
    acc = add(tail_ref, (t0_ref, t1_ref), 24, 12)(acc)
    first = lax.broadcasted_iota(jnp.int32, (8, 256), 0) == 0
    for b, dgain_ref in enumerate((gain0_ref, gain1_ref)):
        table = [acc[96 * b + 16 * k : 96 * b + 16 * k + 16] for k in range(6)]
        table = jnp.concatenate(table, axis=1)
        halves = []
        for c in range(2):
            gain = jnp.where(first, dgain_ref[:, 256 * c : 256 * (c + 1)], 0.0)
            halves.append(jnp.concatenate([table[8 * c : 8 * (c + 1)], gain], axis=1))
        keep, send = pick(idx_ref[0], halves[0], halves[1])
        keep_ref[8 * b : 8 * b + 8, :] = keep
        send_ref[8 * b : 8 * b + 8, :] = send


CUTS = ((0, 384), (384, 768), (768, 1024))


def pick(flag, low, high):
    mine = flag == 0
    return jnp.where(mine, low, high), jnp.where(mine, high, low)


def core_kernel(
    idx_ref, k0_ref, r0_ref, k1_ref, r1_ref, ka_ref, sa_ref, kb_ref, sb_ref, kc_ref, sc_ref
):
    x0, z0, yl = idx_ref[2], idx_ref[3], idx_ref[1]
    for b, (k_ref, r_ref) in enumerate(((k0_ref, r0_ref), (k1_ref, r1_ref))):

        def total(r0, r1, c0, c1):
            return k_ref[r0:r1, c0:c1].astype(F32) + r_ref[r0:r1, c0:c1].astype(F32)

        for s in range(2):
            a0 = 1024 * s
            keep, send = pick(x0, total(0, 128, a0, a0 + 384), total(128, 256, a0, a0 + 384))
            to = 768 * b + 384 * s
            ka_ref[:, to : to + 384] = keep.astype(BF16)
            sa_ref[:, to : to + 384] = send.astype(BF16)
            to = 512 * b + 256 * s
            for h in range(2):
                r = 128 * h
                keep, send = pick(
                    z0,
                    total(r, r + 64, a0 + 768, a0 + 1024),
                    total(r + 64, r + 128, a0 + 768, a0 + 1024),
                )
                kc_ref[64 * h : 64 * h + 64, to : to + 256] = keep.astype(BF16)
                sc_ref[64 * h : 64 * h + 64, to : to + 256] = send.astype(BF16)
        keep, send = pick(yl, total(0, 256, 384, 768), total(0, 256, 1408, 1792))
        kb_ref[:, 384 * b : 384 * (b + 1)] = keep.astype(BF16)
        sb_ref[:, 384 * b : 384 * (b + 1)] = send.astype(BF16)


def step_two_kernel(
    idx_ref, ka_ref, ra_ref, kb_ref, rb_ref, kc_ref, rc_ref, t_ref, u_ref,
    nka_ref, nsa_ref, nkb_ref, nsb_ref, nkc_ref, nsc_ref, tk_ref,
):
    x0, z0, yl = idx_ref[2], idx_ref[3], idx_ref[1]
    a = ka_ref[...].astype(F32) + ra_ref[...].astype(F32)
    for b in range(2):
        keep, send = pick(yl, a[:, 768 * b : 768 * b + 384], a[:, 768 * b + 384 : 768 * b + 768])
        nka_ref[:, 384 * b : 384 * (b + 1)] = keep.astype(BF16)
        nsa_ref[:, 384 * b : 384 * (b + 1)] = send.astype(BF16)
    m = kb_ref[...].astype(F32) + rb_ref[...].astype(F32)
    for h in range(2):
        keep, send = pick(z0, m[128 * h : 128 * h + 64], m[128 * h + 64 : 128 * h + 128])
        nkb_ref[64 * h : 64 * h + 64, :] = keep.astype(BF16)
        nsb_ref[64 * h : 64 * h + 64, :] = send.astype(BF16)
    c = kc_ref[...].astype(F32) + rc_ref[...].astype(F32)
    keep, send = pick(x0, c[0:64], c[64:128])
    nkc_ref[...] = keep.astype(BF16)
    nsc_ref[0:64, :] = send.astype(BF16)
    table = (t_ref[...] + u_ref[...]).astype(BF16)
    tk_ref[...] = table
    nsc_ref[64:80, :] = table


def step_three_kernel(
    idx_ref, ka_ref, ra_ref, kb_ref, rb_ref, kc_ref, rc_ref, tk_ref,
    nka_ref, nsa_ref, nkb_ref, nsb_ref, nkc_ref, nsc_ref, ntk_ref,
):
    x0, z0, yl = idx_ref[2], idx_ref[3], idx_ref[1]
    a = ka_ref[...].astype(F32) + ra_ref[...].astype(F32)
    keep, send = pick(z0, a[0:64], a[64:128])
    nka_ref[...] = keep.astype(BF16)
    nsa_ref[0:64, :] = send.astype(BF16)
    t = tk_ref[...].astype(F32) + rc_ref[64:80, :].astype(F32)
    gains = jnp.concatenate([t[0:8, 768:1024], t[8:16, 768:1024], jnp.zeros((8, 256), F32)], axis=1)
    table = jnp.concatenate([t[:, 0:768], gains, jnp.zeros((8, 768), F32)], axis=0).astype(BF16)
    ntk_ref[...] = table
    nsa_ref[64:96, :] = table
    m = kb_ref[...].astype(F32) + rb_ref[...].astype(F32)
    keep, send = pick(x0, m[0:64], m[64:128])
    nkb_ref[...] = keep.astype(BF16)
    nsb_ref[...] = send.astype(BF16)
    c = kc_ref[...].astype(F32) + rc_ref[0:64, :].astype(F32)
    for b in range(2):
        keep, send = pick(yl, c[:, 512 * b : 512 * b + 256], c[:, 512 * b + 256 : 512 * b + 512])
        nkc_ref[:, 256 * b : 256 * (b + 1)] = keep.astype(BF16)
        nsc_ref[:, 256 * b : 256 * (b + 1)] = send.astype(BF16)


def spread_kernel(
    idx_ref, ka_ref, ra_ref, kb_ref, rb_ref, kc_ref, rc_ref, tk_ref, *refs
):
    outs, scr = refs[0:4], refs[4]
    a = ka_ref[...].astype(F32) + ra_ref[0:64, :].astype(F32)
    m = kb_ref[...].astype(F32) + rb_ref[...].astype(F32)
    c = kc_ref[...].astype(F32) + rc_ref[...].astype(F32)
    table = tk_ref[...].astype(F32) + ra_ref[64:96, :].astype(F32)
    gains = jnp.concatenate([table[16:24, 0:256], table[16:24, 256:512]], axis=0)
    table = jnp.concatenate([table[0:16], gains], axis=1)
    table = jnp.concatenate([table[0:8], table[8:16]], axis=1).astype(BF16)
    full = []
    for b in range(2):
        cols = slice(384 * b, 384 * (b + 1))
        full += [a[:, cols], m[:, cols], c[:, 256 * b : 256 * (b + 1)]]
    full = jnp.concatenate(full, axis=1).astype(BF16)
    for k in range(4):
        scr[k] = full[16 * k : 16 * k + 16]
    for f in range(4):
        outs[f][0:16, :] = scr[idx_ref[4] ^ f]
        outs[f][16:24, :] = table


def plane_kernel(idx_ref, own_ref, g1_ref, g2_ref, g3_ref, *refs):
    outs, tabs, scr = refs[0:4], refs[4], refs[5]
    got = (own_ref, g1_ref, g2_ref, g3_ref)
    total = got[0][0:16, :].astype(F32)
    for g in got[1:]:
        total = total + g[0:16, :].astype(F32)
    for f in range(4):
        tabs[idx_ref[4] ^ f] = got[f][16:24, :].astype(F32)
    table = tabs[0] + tabs[1] + tabs[2] + tabs[3]
    table = jnp.concatenate([table[:, 0:1024], table[:, 1024:2048]], axis=0)
    for k in range(4):
        rows = total[4 * k : 4 * k + 4]
        rows = jnp.concatenate([rows[:, 0:1024], rows[:, 1024:2048], table], axis=0)
        scr[k] = rows.astype(BF16)
    for f in range(4):
        outs[f][...] = scr[idx_ref[5] ^ f]


def close_kernel(idx_ref, own_ref, g1_ref, g2_ref, g3_ref, out_ref, tab_ref, scr):
    for f, g in enumerate((own_ref, g1_ref, g2_ref, g3_ref)):
        scr[idx_ref[5] ^ f] = g[...].astype(F32)
    total = scr[0] + scr[1] + scr[2] + scr[3]
    out_ref[...] = total.astype(BF16)
    tab_ref[...] = total[8:24].astype(BF16)


def last_kernel(
    factor, idx_ref, own_ref, lat_ref, core_ref, dia_ref, gain_ref, qkv_ref, proj_ref, bias_ref
):
    core, yl = idx_ref[0], idx_ref[1]
    own = own_ref[...].astype(F32) * factor
    got = lat_ref[...].astype(F32) * factor
    low, high = pick(yl, own[0:8], got[0:8])
    for b in range(2):
        qkv_ref[b, :, 0:1024] = low[4 * b : 4 * b + 4]
        qkv_ref[b, :, 1024:1536] = high[4 * b : 4 * b + 4, 0:512]
        proj_ref[b, :, :] = high[4 * b : 4 * b + 4, 512:1024]
    near = pick(yl, own[8:24], got[8:24])
    far = pick(yl, core_ref[...].astype(F32) * factor, dia_ref[...].astype(F32) * factor)
    tabs = [pick(core, near[w], far[w]) for w in range(2)]
    for c in range(2):
        for w in range(2):
            for b in range(2):
                bias_ref[b, w, 8 * c : 8 * (c + 1), :] = tabs[w][c][8 * b : 8 * b + 8, 0:NREL]
        for b in range(2):
            gain_ref[b : b + 1, 256 * c : 256 * (c + 1)] = (
                tabs[0][c][8 * b : 8 * b + 1, 768:1024] + tabs[1][c][8 * b : 8 * b + 1, 768:1024]
            )


def _whole(shape):
    return pl.BlockSpec(shape, lambda *_: (0,) * len(shape))


SMEM = pl.BlockSpec(memory_space=pltpu.SMEM)


ANY = pl.BlockSpec(memory_space=pl.ANY)


HBM = pl.BlockSpec(memory_space=pltpu.HBM)


def call(body, us, outs, *args, specs=None, scratch=(), sems=0, vmem=VMEM, hbm_outs=()):
    specs = dict(specs or {})
    if args[0].dtype == jnp.int32 and args[0].ndim == 1:
        specs[0] = SMEM
    scratch = [pltpu.VMEM(s, t) for s, t in scratch]
    if sems:
        scratch.append(pltpu.SemaphoreType.DMA((sems,)))
    return pl.pallas_call(
        body,
        grid=(1,),
        in_specs=[specs.get(i, _whole(a.shape)) for i, a in enumerate(args)],
        out_specs=[HBM if k in hbm_outs else _whole(s) for k, (s, _) in enumerate(outs)],
        out_shape=[jax.ShapeDtypeStruct(s, t) for s, t in outs],
        scratch_shapes=scratch,
        compiler_params=pltpu.CompilerParams(vmem_limit_bytes=vmem),
        cost_estimate=pl.CostEstimate(
            flops=int(us * 1e9), bytes_accessed=int(us * 3.6e6), transcendentals=0
        ),
    )(*args)


def mask_of(axes):
    return sum(1 << (7 - AXES.index(a)) for a in axes)


def flip(value, *axes):
    return lax.ppermute(value, AXES, [(s, s ^ mask_of(axes)) for s in range(256)])


def z_step(value, move, *axes):
    pairs = [(s, (s & ~28 | move(s >> 2 & 7) << 2) ^ mask_of(axes)) for s in range(256)]
    return lax.ppermute(value, AXES, pairs)


def lon_step(value, offset, across):
    pairs = [(s, ((s // 2 + offset) % 128) * 2 + (s % 2 ^ across)) for s in range(256)]
    return lax.ppermute(value, AXES, pairs)


def halo(pieces, offset):
    own, lon, lat, dia = pieces
    return (
        own,
        lon_step(lon, offset, 0),
        flip(lat, "yl"),
        lon_step(dia, offset, 1),
    )


def on_device(inputs, grad_out, gains, qkv_weight, proj_weight, bias_table, rel_ids, groups):
    first_const, second_const, third_const, finish_const = [jnp.asarray(t) for t in TABLES]
    at = {a: lax.axis_index(a) for a in AXES}
    hz = at["z0"] ^ at["z1"]
    idx = jnp.stack(
        [
            at["c"],
            at["yl"],
            at["x0"] ^ at["x1"],
            hz,
            2 * at["x1"] + (at["z2"] ^ (hz & at["z1"])),
            2 * at["yh"] + (at["z1"] ^ (hz & (at["z1"] ^ at["z2"]))),
        ]
    ).astype(jnp.int32)
    x_cells, go_cells = [v.transpose(0, 2, 3, 1, 4).reshape(72, 2, D) for v in (inputs, grad_out)]

    def block(b, shape):
        return pl.BlockSpec((1,) + shape, lambda *_: (b,) + (0,) * len(shape))

    def weights(b, first):
        return {
            first: block(b, (D, 3 * D)),
            first + 1: block(b, (D, D)),
            first + 2: block(b, (2, HEADS, NREL)),
        }

    id_shapes = [((144, 128), jnp.int32), ((24, 128), jnp.int32)]
    tables = [((8, 768), jnp.int32), ((HEADS, 128), F32), ((HEADS, 128), F32)]
    piece = ((40, 1024), BF16)
    saved = [((144, D), F32), ((144, 3 * D), BF16), ((2304, 256), BF16), ((144, D), BF16)]
    own, lon, lat, dia, rstd0, n0, qkv0, p0, o0 = call(
        first_kernel,
        8,
        [piece] * 4
        + [
            ((144, 1), F32),
        ]
        + saved,
        x_cells, go_cells, groups.transpose(1, 0, 2), gains, qkv_weight, proj_weight, bias_table, rel_ids,
        first_const,
        specs={k: HBM for k in range(9)},
        scratch=saved
        + [((144, 1024), F32), ((12, 12), F32), ((144, 1024), BF16), ((2304, 256), F32)]
        + id_shapes
        + tables
        + [
            ((72, 2, D), BF16),
            ((72, 2, D), BF16),
            ((6, 2, 12), jnp.int32),
            ((2, D), F32),
            ((D, 3 * D), BF16),
            ((D, D), BF16),
            ((HEADS, NREL), F32),
            ((144, 144), jnp.int32),
            ((7, 160, 256), BF16),
        ],
        sems=16,
        hbm_outs=range(5, 9),
        vmem=57 << 20,
    )
    pieces = halo((own, lon, lat, dia), -1)
    bias1, ids, tails = call(
        bias_kernel,
        4,
        [((2304, 256), F32)] + id_shapes,
        idx, bias_table, rel_ids, jnp.asarray(TABLES[0][2]),
        specs={1: block(1, (2, HEADS, NREL))},
        scratch=tables,
    )
    ds_shapes = [((2304, 128), F32), ((384, 128), F32)]
    own, lon, lat, dia, h1, o1, dqkv1, g1, dgain1, ds10, ds11 = call(
        second_kernel,
        6,
        [piece] * 4
        + [
            ((144, D), BF16),
            ((144, D), BF16),
            ((144, 3 * D), BF16),
            ((144, D), BF16),
            ((1, D), F32),
        ]
        + ds_shapes,
        idx, *pieces, gains, qkv_weight, proj_weight, bias1, second_const,
        specs={6: block(1, (D, 3 * D)), 7: block(1, (D, D))},
        scratch=[((144, 3 * D), BF16), ((144, 2 * D), BF16)],
    )
    pieces = halo((own, lon, lat, dia), 1)
    wshape = ((256, 4 * D), BF16)
    keep1, send1 = call(weights_kernel, 2, [wshape] * 2, idx, h1, o1, dqkv1, g1)
    recv1 = flip(send1, "c")

    def pairs(*shapes):
        return [(s, BF16) for shape in shapes for s in shape]

    cells = ((72, 2, D), BF16)
    g0, h0, dqkv0, ds00, ds01, send0 = call(
        third_kernel,
        4,
        [((144, D), BF16)] * 2 + [((144, 3 * D), BF16)] + ds_shapes + [wshape],
        idx, *pieces, gains, proj_weight, n0, qkv0, p0, o0, third_const, keep1,
        specs={6: block(0, (D, D)), 12: ANY},
    )
    recv0 = flip(send0, "c")
    (keep0,) = call(keep_kernel, 1, [wshape], idx, h0, o0, dqkv0, g0)
    ka, sa, kb, sb, kc, sc = call(
        core_kernel,
        1,
        pairs([(128, 1536)] * 2, [(256, 768)] * 2, [(128, 1024)] * 2),
        idx, keep0, recv0, keep1, recv1,
    )
    ra, rb, rc = flip(sa, "x0"), flip(sb, "yl"), flip(sc, "z0")
    outputs, grad_inputs, dgain0 = call(
        finish_kernel,
        2,
        [cells, cells, ((1, D), F32)],
        *pieces, gains, qkv_weight, n0, rstd0, g0, dqkv0, finish_const, ka,
        specs={5: block(0, (D, 3 * D)), 11: ANY},
        scratch=[((144, 2 * D), F32)],
    )
    outputs, grad_inputs = [
        v.reshape(1, 6, 12, 2, D).transpose(0, 3, 1, 2, 4) for v in (outputs, grad_inputs)
    ]
    tshape = ((16, 1024), F32)
    tkeep, tsend = call(
        scatter_kernel,
        6,
        [tshape] * 2,
        idx, ids, tails, ds00, ds01, dgain0, ds10, ds11, dgain1, ka,
        specs={9: ANY},
    )
    trecv = flip(tsend, "c")
    ka, sa, kb, sb, kc, sc, tk = call(
        step_two_kernel,
        1,
        pairs([(128, 768)] * 4, [(64, 1024), (80, 1024)], [(16, 1024)]),
        idx, ka, ra, kb, rb, kc, rc, tkeep, trecv,
    )
    ra, rb, rc = flip(sa, "yl"), flip(sb, "z0"), flip(sc, "x0")
    ka, sa, kb, sb, kc, sc, tk = call(
        step_three_kernel,
        1,
        pairs([(64, 768), (96, 768)], [(64, 768)] * 2, [(64, 512)] * 2, [(32, 768)]),
        idx, ka, ra, kb, rb, kc, rc, tk,
    )
    ra, rb, rc = flip(sa, "z0"), flip(sb, "x0"), flip(sc, "yl")
    parts = call(
        spread_kernel,
        1,
        [((24, 2048), BF16)] * 4,
        idx, ka, ra, kb, rb, kc, rc, tk,
        scratch=[((4, 16, 2048), BF16)],
    )
    near = lambda z: (z + 1) % 8 if z & 1 else (z - 1) % 8
    far = lambda z: z ^ (7 if (z ^ z >> 1) & 1 else 3)
    parts = call(
        plane_kernel,
        1,
        [((24, 1024), BF16)] * 4,
        idx, parts[0], z_step(parts[1], near), flip(parts[2], "x1", "x0"),
        z_step(parts[3], near, "x1", "x0"),
        scratch=[((4, 8, 2048), F32), ((4, 24, 1024), BF16)],
    )
    own, tab = call(
        close_kernel,
        1,
        [((24, 1024), BF16), ((16, 1024), BF16)],
        idx, parts[0], z_step(parts[1], far), flip(parts[2], "yh"), z_step(parts[3], far, "yh"),
        scratch=[((4, 24, 1024), F32)],
    )
    from_core = flip(tab, "c")
    from_dia = flip(tab, "c", "yl")
    from_lat = flip(own, "yl")
    factor = 36864 ** (-0.5)
    grad_gains, grad_qkv, grad_proj, grad_bias = call(
        functools.partial(last_kernel, factor),
        1,
        [
            ((2, D), F32),
            ((2, 4, 3 * D), F32),
            ((2, 4, D), F32),
            ((2, 2, HEADS, NREL), F32),
        ],
        idx, own, from_lat, from_core, from_dia,
    )
    return (outputs, grad_inputs, grad_gains, grad_qkv, grad_proj, grad_bias)


def solution(mesh):
    fine = Mesh(mesh.devices.reshape((2,) * 8), AXES)
    lon = AXES[:7]
    field = P(None, None, "yl", lon, None)
    rows = P(None, lon, None)
    return jax.shard_map(
        on_device,
        mesh=fine,
        in_specs=(field, field, P(), P(), P(), P(), P(), P(None, "yl", lon)),
        out_specs=(field, field, P(), rows, rows, P()),
        check_vma=False,
    )
```
